32 devices in a mesh: dp: 4 (over y, core), fsdp: 8 (over z, x).
Axes of the slice: x: 2, y: 2, z: 4, core: 2. Of those that a mesh axis runs over, the one named last changes fastest.
Arguments:
- char_codes: int32 [32, 128, 16], P(('dp', 'fsdp')), may hold values from 0 to 255
- char_counts: int32 [32, 128], P(('dp', 'fsdp')), may hold values from 1 to 16, as said below
- word_groups: int32 [32, 128], P(('dp', 'fsdp')), may hold values from 0 to 7
- valid_words: int32 [32], P(('dp', 'fsdp')), may hold values from 16 to 128, as said below
- char_matrix: bfloat16 [8192, 128], P(('dp', 'fsdp'))
- char_lookup: bfloat16 [256, 256], P(('dp', 'fsdp')), may hold values from -6 to 6
- group_lookup: bfloat16 [256, 8], P(('dp', 'fsdp')), may hold values from -6 to 6
- char_vectors: bfloat16 [256, 5], P(('dp', 'fsdp'))
- word_matrix: bfloat16 [24576, 128], P(('dp', 'fsdp'))
- word_vectors: bfloat16 [512, 4], P(('dp', 'fsdp'))
- cotangent: bfloat16 [32, 128, 512], P(('dp', 'fsdp')), may hold values from -6 to 6
Outputs:
- layer_out: bfloat16 [32, 128, 512], P(('dp', 'fsdp'))
- grad_char_matrix: float32 [8192, 128], P(('dp', 'fsdp'))
- grad_char_lookup: float32 [256, 256], P(('dp', 'fsdp'))
- grad_group_lookup: float32 [256, 8], P(('dp', 'fsdp'))
- grad_char_vectors: float32 [256, 5], P(('dp', 'fsdp'))
- grad_word_matrix: float32 [24576, 128], P(('dp', 'fsdp'))
- grad_word_vectors: float32 [512, 4], P(('dp', 'fsdp'))
The draws below stay inside these ranges and needn't reach their ends.
Inputs may be any that keep to these rules, and one draw needn't show every extreme that they name: `char_counts`: in every sequence some word has all 16 characters. `valid_words`: some sequence has all 128 words real.
All inputs are finite; a program needn't handle non-finite values.
Results may differ from the reference program's by a relative error of at most 0.015.
Values may be sent and summed in bfloat16 or wider, within the bound.
A program may use at most 192 MiB of HBM per device.

```python
import jax
import jax.numpy as jnp
from jax import lax

C = 256
HD = 64
CH = 4
CM = 1024
D = 512
H = 8
FF = 2048
W = 16
VOCAB = 256
LANGS = 8
LEN = 128
SEQS = 32


def column_scales(pieces):
    return jnp.concatenate([jnp.full((width,), factor, jnp.float32) for width, factor in pieces])


def vector_mix(sample, factors, offsets):
    return sample * jnp.array(factors, jnp.float32)[None, :] + jnp.array(offsets, jnp.float32)[None, :]


def draw_char_matrix(key, part):
    key = jax.random.fold_in(key, 11)
    sample = jax.random.normal(key, (C, 6 * C + 2 * CM + D), jnp.float32)
    scales = column_scales(((3 * C, C ** (-0.5)), (C, 2.0 * C ** (-0.5)), (CM, C ** (-0.5)), (CM, 2.0 * CM ** (-0.5)), (2 * C, C ** (-0.5)), (D, 3.0 * C ** (-0.5))))
    return (sample * scales[None, :]).reshape(C * (6 * C + 2 * CM + D) // 128, 128).astype(jnp.bfloat16)


def draw_word_matrix(key, part):
    key = jax.random.fold_in(key, 13)
    sample = jax.random.normal(key, (D, 4 * D + 2 * FF), jnp.float32)
    scales = column_scales(((3 * D, D ** (-0.5)), (D, 4.0 * D ** (-0.5)), (FF, D ** (-0.5)), (FF, 2.0 * FF ** (-0.5))))
    return (sample * scales[None, :]).reshape(D * (4 * D + 2 * FF) // 128, 128).astype(jnp.bfloat16)


def draw_char_vectors(key, part):
    key = jax.random.fold_in(key, 17)
    sample = jax.random.normal(key, (C, 5), jnp.float32)
    return vector_mix(sample, (0.15, 0.3, 0.15, 0.3, 1.0), (1.0, 0.0, 1.0, 0.0, 0.0)).astype(jnp.bfloat16)


def draw_word_vectors(key, part):
    key = jax.random.fold_in(key, 19)
    sample = jax.random.normal(key, (D, 4), jnp.float32)
    return vector_mix(sample, (0.15, 0.3, 0.15, 0.3), (1.0, 0.0, 1.0, 0.0)).astype(jnp.bfloat16)


def draw_char_counts(key, part):
    key = jax.random.fold_in(key, 23)
    count_key, place_key = jax.random.split(key)
    counts = jax.random.randint(count_key, (SEQS, LEN), 1, W + 1)
    longest_at = jax.random.randint(place_key, (SEQS, 1), 0, LEN)
    return jnp.where(jnp.arange(LEN)[None, :] == longest_at, W, counts).astype(jnp.int32)


def draw_valid_words(key, part):
    key = jax.random.fold_in(key, 29)
    count_key, place_key = jax.random.split(key)
    lengths = jax.random.randint(count_key, (SEQS,), max(1, LEN // 8), LEN + 1)
    longest = jax.random.randint(place_key, (), 0, SEQS)
    return jnp.where(jnp.arange(SEQS) == longest, LEN, lengths).astype(jnp.int32)


def touch_ends(values, stream_key, low, high):
    longest = values.shape.index(max(values.shape))
    spots = []
    for shift in (0, 1):
        where = [jax.random.randint(jax.random.fold_in(stream_key, axis), (), 0, length) for axis, length in enumerate(values.shape)]
        where[longest] = (where[longest] + shift) % values.shape[longest]
        spots.append(tuple(where))
    return values.at[spots[0]].set(low).at[spots[1]].set(high)


def steps_of(key, shape, cuts, least, high):
    loudness, own = 1.0, jax.random.fold_in(key, 6)
    for axis_at, shards_of in cuts:
        heights = jnp.exp(jax.random.uniform(jax.random.fold_in(own, axis_at), (shards_of,), jnp.float32, least / len(cuts), high / len(cuts)))
        loudness = loudness * jnp.repeat(heights, shape[axis_at] // shards_of).reshape([-1 if axis == axis_at else 1 for axis in range(len(shape))])
    return loudness


def centred(own_key, dims, scale, limit, cuts=(), dtype=jnp.bfloat16):
    values = scale * jax.random.normal(own_key, dims, jnp.float32)
    if cuts:
        values = values * steps_of(own_key, dims, cuts, -0.22, 0.18)
    return jnp.clip(values, -limit, limit).astype(dtype)


def setup_inputs(seed: int = 0) -> dict:
    key_list = jax.random.split(jax.random.key(seed), 12)
    return {
        "char_codes": touch_ends(jax.random.randint(key_list[0], (SEQS, LEN, W), 0, VOCAB), jax.random.fold_in(key_list[0], 1), 0, VOCAB - 1).astype(jnp.int32),
        "char_counts": draw_char_counts(jax.random.fold_in(key_list[11], 71), 0),
        "word_groups": touch_ends(jax.random.randint(key_list[2], (SEQS, LEN), 0, LANGS), jax.random.fold_in(key_list[2], 1), 0, LANGS - 1).astype(jnp.int32),
        "valid_words": draw_valid_words(jax.random.fold_in(key_list[11], 71), 0),
        "char_matrix": draw_char_matrix(jax.random.fold_in(key_list[11], 71), 0),
        "char_lookup": centred(key_list[5], (VOCAB, C), 1.0, 6.0, ((0, 32),)),
        "group_lookup": centred(key_list[6], (C, LANGS), 1.0, 6.0, ((0, 32),)),
        "char_vectors": draw_char_vectors(jax.random.fold_in(key_list[11], 71), 0),
        "word_matrix": draw_word_matrix(jax.random.fold_in(key_list[11], 71), 0),
        "word_vectors": draw_word_vectors(jax.random.fold_in(key_list[11], 71), 0),
        "cotangent": centred(key_list[10], (SEQS, LEN, D), 1.0, 6.0, ((0, 32),)),
    }


EPSILON = 1e-05
NEGATIVE = -1000000000.0
HIGHEST = lax.Precision.HIGHEST

@jax.custom_vjp
def low(v):
    return lax.optimization_barrier(v.astype(jnp.bfloat16)).astype(jnp.float32)

@jax.custom_vjp
def low_back(v):
    return v

def low_keep(v):
    return (low(v), None)

def low_pass(kept, grad):
    return (grad,)

def back_keep(v):
    return (v, None)

def back_low(kept, grad):
    return (low(grad),)
low.defvjp(low_keep, low_pass)
low_back.defvjp(back_keep, back_low)

def full_product(former, latter):
    return jnp.dot(former, latter, precision=HIGHEST, preferred_element_type=jnp.float32)

def right_transposed(former, latter):
    return lax.dot_general(former, latter, (((1,), (1,)), ((), ())), precision=HIGHEST, preferred_element_type=jnp.float32)

def norm_rows(inputs, factor, offset):
    centre = inputs - lax.optimization_barrier(jnp.mean(inputs, -1, keepdims=True))
    spread = lax.optimization_barrier(jnp.mean(centre * centre, -1, keepdims=True))
    return centre * lax.rsqrt(spread + EPSILON) * factor + offset

def gelu_tanh(inputs):
    return 0.5 * inputs * (1.0 + jnp.tanh(0.7978845608028654 * (inputs + 0.044715 * inputs * inputs * inputs)))

def soft_max(scores, along):
    peak_score = lax.optimization_barrier(jnp.max(scores, along, keepdims=True))
    raised = jnp.exp(scores - peak_score)
    return raised / lax.optimization_barrier(jnp.sum(raised, along, keepdims=True))

def pool_chars(pool_keys, pool_values, pool_query, visible):
    scores = jnp.einsum('twhd,hd->twh', pool_keys, pool_query, precision=HIGHEST) * 0.125
    scores = jnp.where(visible[:, :, None], scores, NEGATIVE)
    attention = soft_max(scores, 1)
    return jnp.einsum('twh,twhd->thd', attention, pool_values, precision=HIGHEST)

def layer_forward(packed, symbols, counts, groups, length):
    flat_char, lookup, group_cols, char_vec, flat_word, word_vec = packed
    char_mats = flat_char.reshape(C, 6 * C + 2 * CM + D)
    word_mats = flat_word.reshape(D, 4 * D + 2 * FF)
    char_rows = LEN * W
    visible = jnp.arange(W)[None, :] < counts[:, None]
    embedded = jnp.take(lookup, symbols.reshape(char_rows), axis=0).reshape(LEN, W, C)
    embedded = embedded + jnp.take(group_cols.T, groups, axis=0)[:, None, :]
    embedded = low_back(embedded.reshape(char_rows, C))
    normed = low(norm_rows(embedded, char_vec[:, 0], char_vec[:, 1]))
    triple = low_back(low(full_product(normed, char_mats[:, :3 * C]))).reshape(LEN, W, 3, CH, HD)
    scores = low_back(jnp.einsum('twhd,tshd->thws', triple[:, :, 0], triple[:, :, 1], precision=HIGHEST) * 0.125)
    scores = jnp.where(visible[:, None, None, :], scores, NEGATIVE)
    attention = soft_max(scores, 3)
    mixture = low_back(low(jnp.einsum('thws,tshd->twhd', low(attention), triple[:, :, 2], precision=HIGHEST))).reshape(char_rows, C)
    residual_one = embedded + low_back(full_product(mixture, char_mats[:, 3 * C:4 * C]))
    norm_two = low(norm_rows(residual_one, char_vec[:, 2], char_vec[:, 3]))
    hidden = low(gelu_tanh(low_back(full_product(norm_two, char_mats[:, 4 * C:4 * C + CM]))))
    residual_two = residual_one + low_back(right_transposed(hidden, char_mats[:, 4 * C + CM:4 * C + 2 * CM]))
    pool_pairs = low_back(full_product(low(residual_two), char_mats[:, 4 * C + 2 * CM:6 * C + 2 * CM])).reshape(LEN, W, 2, CH, HD)
    pooled = pool_chars(pool_pairs[:, :, 0], pool_pairs[:, :, 1], char_vec[:, 4].reshape(CH, HD), visible).reshape(LEN, C)
    word_input = low_back(full_product(low(pooled), char_mats[:, 6 * C + 2 * CM:]))
    normed = low(norm_rows(word_input, word_vec[:, 0], word_vec[:, 1]))
    triple = low_back(low(full_product(normed, word_mats[:, :3 * D]))).reshape(LEN, 3, H, HD)
    position = jnp.arange(LEN)
    visible_words = (position[None, :] <= position[:, None]) & (position[None, :] < length)
    scores = low_back(jnp.einsum('qhd,khd->hqk', triple[:, 0], triple[:, 1], precision=HIGHEST) * 0.125)
    scores = jnp.where(visible_words[None], scores, NEGATIVE)
    attention = soft_max(scores, 2)
    mixture = low_back(low(jnp.einsum('hqk,khd->qhd', low(attention), triple[:, 2], precision=HIGHEST))).reshape(LEN, D)
    residual_one = word_input + low_back(full_product(mixture, word_mats[:, 3 * D:4 * D]))
    norm_two = low(norm_rows(residual_one, word_vec[:, 2], word_vec[:, 3]))
    hidden = low(gelu_tanh(low_back(full_product(norm_two, word_mats[:, 4 * D:4 * D + FF]))))
    return residual_one + low_back(right_transposed(hidden, word_mats[:, 4 * D + FF:]))

def reference(char_codes, char_counts, word_groups, valid_words, char_matrix, char_lookup, group_lookup, char_vectors, word_matrix, word_vectors, cotangent):
    weights = (char_matrix.astype(jnp.float32), char_lookup.astype(jnp.float32), group_lookup.astype(jnp.float32), char_vectors.astype(jnp.float32), word_matrix.astype(jnp.float32), word_vectors.astype(jnp.float32))

    def one_sequence(totals, inputs):
        symbols, counts, groups, length, gradient = inputs
        result, pullback = jax.vjp(lambda packed: layer_forward(packed, symbols, counts, groups, length), weights)
        pulled = pullback(gradient.astype(jnp.float32))[0]
        totals = tuple((running + addend for running, addend in zip(totals, pulled)))
        return (totals, result.astype(jnp.bfloat16))
    start_sums = tuple((jnp.zeros_like(weight) for weight in weights))
    totals, layer_out = lax.scan(one_sequence, start_sums, (char_codes, char_counts, word_groups, valid_words, cotangent))
    return (layer_out, totals[0], totals[1], totals[2], totals[3], totals[4], totals[5])
```

```python
import functools

import jax
import jax.numpy as jnp
from jax import lax
from jax.experimental import pallas as pl
from jax.experimental.pallas import tpu as pltpu
from jax.sharding import PartitionSpec as P

C = 256
HD = 64
CH = 4
CM = 1024
D = 512
H = 8
FF = 2048
W = 16
VOCAB = 256
LANGS = 8
LEN = 128


EPSILON = 1e-05
NEGATIVE = -1000000000.0
HIGHEST = lax.Precision.HIGHEST


def lowered(operand):
    return operand.astype(jnp.bfloat16)


def plain_product(former, latter):
    return jnp.dot(former, latter, preferred_element_type=jnp.float32)


def right_transposed(former, latter):
    return lax.dot_general(
        former, latter, (((1,), (1,)), ((), ())), preferred_element_type=jnp.float32
    )


def row_summed(former, latter):
    return lax.dot_general(
        former, latter, (((0,), (0,)), ((), ())), preferred_element_type=jnp.float32
    )


def norm_rows(inputs, factor, offset):
    centre = inputs - jnp.mean(inputs, -1, keepdims=True)
    spread = jnp.mean(centre * centre, -1, keepdims=True)
    return centre * lax.rsqrt(spread + EPSILON) * factor + offset


def gelu_tanh(inputs):
    return (
        0.5
        * inputs
        * (1.0 + jnp.tanh(0.7978845608028654 * (inputs + 0.044715 * inputs * inputs * inputs)))
    )


def soft_max(scores, along):
    peak_score = jnp.max(scores, along, keepdims=True)
    raised = jnp.exp(scores - peak_score)
    return raised / jnp.sum(raised, along, keepdims=True)


def soft_back(attention, gradient, along):
    return attention * (gradient - jnp.sum(attention * gradient, along, keepdims=True))


def pool_chars(pool_keys, pool_values, pool_query, visible):
    scores = jnp.einsum("twhd,hd->twh", pool_keys, pool_query, precision=HIGHEST) * 0.125
    scores = jnp.where(visible[:, :, None], scores, NEGATIVE)
    attention = soft_max(scores, 1)
    return jnp.einsum("twh,twhd->thd", attention, pool_values, precision=HIGHEST)


MESH = pl.DeviceIdType.MESH


class Grid:
    def __init__(self, sizes):
        self.Y, self.Z, self.X = sizes
        dp, fs = lax.axis_index("dp"), lax.axis_index("fsdp")
        self.y, self.c = dp // 2, dp % 2
        self.z, self.x = fs // self.X, fs % self.X

    def at(self, y=None, c=None, z=None, x=None):
        y = self.y if y is None else y
        c = self.c if c is None else c
        z = self.z if z is None else z
        x = self.x if x is None else x
        return (y * 2 + c, z * self.X + x)

    def others(self, axis):
        n, me = {"y": (self.Y, self.y), "z": (self.Z, self.z), "x": (self.X, self.x)}[axis]
        return [(me + k) % n for k in range(1, n)]

    def partners(self):
        out = [self.at(c=1 - self.c)]
        for axis in "yzx":
            out += [self.at(**{axis: v}) for v in self.others(axis)]
        return out

    def greet(self):
        barrier = pltpu.get_barrier_semaphore()
        all_of = self.partners()
        for p in all_of:
            pl.semaphore_signal(barrier, inc=1, device_id=p, device_id_type=MESH)
        pl.semaphore_wait(barrier, len(all_of))


class Sems:
    def __init__(self, send, recv):
        self.send, self.recv, self.n = send, recv, 0

    def copy(self, src, dst, to):
        i = self.n
        self.n += 1
        d = pltpu.make_async_remote_copy(
            src_ref=src, dst_ref=dst, send_sem=self.send.at[i], recv_sem=self.recv.at[i],
            device_id=to, device_id_type=MESH)
        d.start()
        return d


def ag_count(Y, Z, X):
    return (Z - 1) + 1 + 2 * ((X - 1) + (Y - 1)) + 2 * ((X - 1) + (Y - 1))


class Gather:
    def __init__(self, grid, src, G, sems, half):
        self.g, self.src, self.G, self.s, self.half = grid, src, G, sems, half
        self.sent = []
        self.core = []

    def send(self, idx, to, keep):
        d = self.s.copy(self.G.at[idx], self.G.at[idx], to)
        self.sent.append(d)
        keep.append(d)

    def start(self):
        g = self.g
        self.p1 = []
        for z in g.others("z"):
            d = self.s.copy(self.src, self.G.at[g.y, g.c, g.z, g.x], g.at(z=z))
            self.sent.append(d)
            self.p1.append(d)

    def step2(self):
        g, h = self.g, self.half
        n = self.G.shape[4]
        self.A, self.B = pl.ds(0, h), pl.ds(h, n - h)
        for d in self.p1:
            d.wait_recv()
        self.p2a, self.p2b = [], []
        for x in g.others("x"):
            self.send((g.y, g.c, slice(None), g.x, self.A), g.at(x=x), self.p2a)
        for y in g.others("y"):
            self.send((g.y, g.c, slice(None), g.x, self.B), g.at(y=y), self.p2b)
        self.send((g.y, g.c, slice(None), g.x), g.at(c=1 - g.c), self.core)

    def step3(self):
        g = self.g
        self.p3a, self.p3b = [], []
        for d in self.p2a:
            d.wait_recv()
        for y in g.others("y"):
            self.send((g.y, g.c, slice(None), slice(None), self.A), g.at(y=y), self.p3a)
        for d in self.p2b:
            d.wait_recv()
        for x in g.others("x"):
            self.send((slice(None), g.c, slice(None), g.x, self.B), g.at(x=x), self.p3b)
        for x in g.others("x"):
            self.send((g.y, g.c, slice(None), x, self.A), g.at(c=1 - g.c), self.core)
        for y in g.others("y"):
            self.send((y, g.c, slice(None), g.x, self.B), g.at(c=1 - g.c), self.core)

    def step4(self):
        g = self.g
        for d in self.p3a:
            d.wait_recv()
        for y in g.others("y"):
            self.send((y, g.c, slice(None), slice(None), self.A), g.at(c=1 - g.c), self.core)
        for d in self.p3b:
            d.wait_recv()
        for x in g.others("x"):
            self.send((slice(None), g.c, slice(None), x, self.B), g.at(c=1 - g.c), self.core)

    def finish(self):
        for d in self.core:
            d.wait_recv()

    def drain(self):
        for d in self.sent:
            d.wait_send()


def rs_count(Y, Z, X):
    return 1 + 2 * ((X - 1) + (Y - 1)) + 2 * (Z - 1)


def rs_scratch(Y, Z, X, R, half):
    hb = R - half
    b = jnp.bfloat16
    return [
        pltpu.VMEM((Y, Z, X, R, 128), b),
        pltpu.VMEM((Y - 1, Z, X, half, 128), b),
        pltpu.VMEM((X - 1, Z, half, 128), b),
        pltpu.VMEM((X - 1, Y, Z, hb, 128), b),
        pltpu.VMEM((Y - 1, Z, hb, 128), b),
        pltpu.VMEM((Z - 1, R, 128), b),
    ]


def add_into(dst, srcs):
    lead = dst.shape[:-2]
    total = 1
    for n in lead:
        total *= n

    def body(i, _):
        idx, r = [], i
        for n in reversed(lead):
            idx.append(r % n)
            r = r // n
        idx = tuple(reversed(idx))
        acc = dst[idx].astype(jnp.float32)
        for s in srcs:
            acc = acc + s[idx].astype(jnp.float32)
        dst[idx] = acc.astype(jnp.bfloat16)
        return 0

    lax.fori_loop(0, total, body, 0)


class Scatter:
    def __init__(self, grid, PB, recv, sems, half):
        self.g, self.PB, self.s, self.half = grid, PB, sems, half
        self.r1, self.r2a, self.r3a, self.r2b, self.r3b, self.r4 = recv
        self.sent = []

    def send(self, src, dst, to, keep):
        d = self.s.copy(src, dst, to)
        self.sent.append(d)
        keep.append(d)

    def start(self):
        g = self.g
        self.p1 = []
        self.send(self.PB.at[:, 1 - g.c], self.r1, g.at(c=1 - g.c), self.p1)


    def step2(self):
        g, h = self.g, self.half
        n = self.PB.shape[4]
        self.A, self.B = pl.ds(0, h), pl.ds(h, n - h)
        for d in self.p1:
            d.wait_recv()
        add_into(self.PB.at[:, g.c], [self.r1])
        self.p2a, self.p2b = [], []
        for k, y in enumerate(g.others("y")):
            self.send(self.PB.at[y, g.c, :, :, self.A], self.r2a.at[k], g.at(y=y), self.p2a)
        for k, x in enumerate(g.others("x")):
            self.send(self.PB.at[:, g.c, :, x, self.B], self.r2b.at[k], g.at(x=x), self.p2b)

    def step3(self):
        g = self.g
        self.p3a, self.p3b = [], []
        for d in self.p2a:
            d.wait_recv()
        add_into(self.PB.at[g.y, g.c, :, :, self.A], [self.r2a.at[k] for k in range(g.Y - 1)])
        for k, x in enumerate(g.others("x")):
            self.send(self.PB.at[g.y, g.c, :, x, self.A], self.r3a.at[k], g.at(x=x), self.p3a)
        for d in self.p2b:
            d.wait_recv()
        add_into(self.PB.at[:, g.c, :, g.x, self.B], [self.r2b.at[k] for k in range(g.X - 1)])
        for k, y in enumerate(g.others("y")):
            self.send(self.PB.at[y, g.c, :, g.x, self.B], self.r3b.at[k], g.at(y=y), self.p3b)

    def step4(self):
        g = self.g
        self.p4 = []
        for part, waits, recv in ((self.A, self.p3a, self.r3a), (self.B, self.p3b, self.r3b)):
            for d in waits:
                d.wait_recv()
            add_into(self.PB.at[g.y, g.c, :, g.x, part], [recv.at[k] for k in range(recv.shape[0])])
            for k, z in enumerate(g.others("z")):
                self.send(self.PB.at[g.y, g.c, z, g.x, part], self.r4.at[k, part], g.at(z=z), self.p4)

    def finish(self, out):
        g = self.g
        for d in self.p4:
            d.wait_recv()
        rows = out.shape[0]
        step = 96 if rows % 96 == 0 else 16

        def body(i, _):
            r = pl.ds(pl.multiple_of(i * step, step), step)
            acc = self.PB[g.y, g.c, g.z, g.x, r].astype(jnp.float32)
            for k in range(g.Z - 1):
                acc = acc + self.r4[k, r].astype(jnp.float32)
            out[r, :] = acc
            return 0

        lax.fori_loop(0, rows // step, body, 0)

    def drain(self):
        for d in self.sent:
            d.wait_send()


def char_forward(parts, symbols, counts, groups):
    matrices, lookup, group_cols, vectors = parts
    vectors = vectors.astype(jnp.float32)
    char_rows = LEN * W
    visible = jnp.arange(W)[None, :] < counts[:, None]
    onehot = lowered(symbols.reshape(char_rows, 1) == jnp.arange(VOCAB)[None, :])
    group_hot = lowered(groups[:, None] == jnp.arange(LANGS)[None, :])
    embedded = (
        plain_product(onehot, lookup).reshape(LEN, W, C)
        + right_transposed(group_hot, group_cols)[:, None, :]
    )
    embedded = embedded.reshape(char_rows, C)
    normed = lowered(norm_rows(embedded, vectors[:, 0], vectors[:, 1]))
    triple = lowered(plain_product(normed, matrices[:, : 3 * C])).reshape(LEN, W, 3, CH, HD)
    scores = (
        jnp.einsum(
            "twhd,tshd->thws", triple[:, :, 0], triple[:, :, 1], preferred_element_type=jnp.float32
        )
        * 0.125
    )
    scores = jnp.where(visible[:, None, None, :], scores, NEGATIVE)
    attention = soft_max(scores, 3)
    mixture = lowered(
        jnp.einsum(
            "thws,tshd->twhd",
            lowered(attention),
            triple[:, :, 2],
            preferred_element_type=jnp.float32,
        )
    ).reshape(char_rows, C)
    residual_one = embedded + plain_product(mixture, matrices[:, 3 * C : 4 * C])
    norm_two = lowered(norm_rows(residual_one, vectors[:, 2], vectors[:, 3]))
    hidden_pre = plain_product(norm_two, matrices[:, 4 * C : 4 * C + CM])
    hidden = lowered(gelu_tanh(hidden_pre))
    residual_two = residual_one + right_transposed(hidden, matrices[:, 4 * C + CM : 4 * C + 2 * CM])
    pool_in = lowered(residual_two)
    pool_pairs = plain_product(pool_in, matrices[:, 4 * C + 2 * CM : 6 * C + 2 * CM]).reshape(
        LEN, W, 2, CH, HD
    )
    pooled = pool_chars(
        pool_pairs[:, :, 0], pool_pairs[:, :, 1], vectors[:, 4].reshape(CH, HD), visible
    ).reshape(LEN, C)
    pooled_low = lowered(pooled)
    word_input = plain_product(pooled_low, matrices[:, 6 * C + 2 * CM :])
    return dict(
        onehot=onehot,
        group_hot=group_hot,
        embedded=embedded,
        normed=normed,
        triple=triple,
        attention=attention,
        mixture=mixture,
        residual_one=residual_one,
        norm_two=norm_two,
        hidden_pre=hidden_pre,
        hidden=hidden,
        pool_in=pool_in,
        pool_pairs=pool_pairs,
        pooled_low=pooled_low,
        word_input=word_input,
        visible=visible,
    )


def word_forward(parts, word_input, length):
    matrices, vectors = parts
    vectors = vectors.astype(jnp.float32)
    normed = lowered(norm_rows(word_input, vectors[:, 0], vectors[:, 1]))
    triple = lowered(plain_product(normed, matrices[:, : 3 * D])).reshape(LEN, 3, H, HD)
    position = jnp.arange(LEN)
    visible_words = (position[None, :] <= position[:, None]) & (position[None, :] < length)
    scores = (
        jnp.einsum("qhd,khd->hqk", triple[:, 0], triple[:, 1], preferred_element_type=jnp.float32)
        * 0.125
    )
    scores = jnp.where(visible_words[None], scores, NEGATIVE)
    attention = soft_max(scores, 2)
    mixture = lowered(
        jnp.einsum(
            "hqk,khd->qhd", lowered(attention), triple[:, 2], preferred_element_type=jnp.float32
        )
    ).reshape(LEN, D)
    residual_one = word_input + plain_product(mixture, matrices[:, 3 * D : 4 * D])
    norm_two = lowered(norm_rows(residual_one, vectors[:, 2], vectors[:, 3]))
    hidden_pre = plain_product(norm_two, matrices[:, 4 * D : 4 * D + FF])
    hidden = lowered(gelu_tanh(hidden_pre))
    result = residual_one + right_transposed(hidden, matrices[:, 4 * D + FF :])
    return dict(
        normed=normed,
        triple=triple,
        attention=attention,
        mixture=mixture,
        residual_one=residual_one,
        norm_two=norm_two,
        hidden_pre=hidden_pre,
        hidden=hidden,
        result=result,
    )


def word_backward(parts, saved, word_input, gradient):
    matrices, vectors = parts
    vectors = vectors.astype(jnp.float32)
    down_grad = lowered(gradient)
    grad_down = row_summed(down_grad, saved["hidden"])
    grad_hidden = plain_product(down_grad, matrices[:, 4 * D + FF :])
    gelu_pull = jax.vjp(gelu_tanh, saved["hidden_pre"])[1]
    pre_grad = lowered(gelu_pull(grad_hidden)[0])
    grad_up = row_summed(saved["norm_two"], pre_grad)
    norm_pull = jax.vjp(norm_rows, saved["residual_one"], vectors[:, 2], vectors[:, 3])[1]
    first_norm, gain_two, shift_two = norm_pull(
        right_transposed(pre_grad, matrices[:, 4 * D : 4 * D + FF])
    )
    first_grad = gradient + first_norm
    attn_grad = lowered(first_grad)
    grad_out = row_summed(saved["mixture"], attn_grad)
    mixed_grad = lowered(right_transposed(attn_grad, matrices[:, 3 * D : 4 * D])).reshape(
        LEN, H, HD
    )
    triple = saved["triple"]
    attention = saved["attention"]
    prob_grad = jnp.einsum(
        "qhd,khd->hqk", mixed_grad, triple[:, 2], preferred_element_type=jnp.float32
    )
    score_grad = lowered(soft_back(attention, prob_grad, 2))
    query_grad = (
        jnp.einsum("hqk,khd->qhd", score_grad, triple[:, 1], preferred_element_type=jnp.float32)
        * 0.125
    )
    key_grad = (
        jnp.einsum("hqk,qhd->khd", score_grad, triple[:, 0], preferred_element_type=jnp.float32)
        * 0.125
    )
    value_grad = jnp.einsum(
        "hqk,qhd->khd", lowered(attention), mixed_grad, preferred_element_type=jnp.float32
    )
    triple_grad = lowered(jnp.stack([query_grad, key_grad, value_grad], 1)).reshape(LEN, 3 * D)
    grad_triple = row_summed(saved["normed"], triple_grad)
    norm_pull = jax.vjp(norm_rows, word_input, vectors[:, 0], vectors[:, 1])[1]
    input_norm, gain_one, shift_one = norm_pull(right_transposed(triple_grad, matrices[:, : 3 * D]))
    input_grad = first_grad + input_norm
    matrix_grad = jnp.concatenate([grad_triple, grad_out, grad_up, grad_down], 1).reshape(-1, 128)
    vector_grad = jnp.stack([gain_one, shift_one, gain_two, shift_two], 1)
    return (input_grad, matrix_grad, vector_grad)


def char_backward(parts, saved, input_grad):
    matrices, lookup, group_cols, vectors = parts
    vectors = vectors.astype(jnp.float32)
    char_rows = LEN * W
    visible = saved["visible"]
    words_low = lowered(input_grad)
    grad_proj = row_summed(saved["pooled_low"], words_low)
    pooled_grad = right_transposed(words_low, matrices[:, 6 * C + 2 * CM :]).reshape(LEN, CH, HD)
    pool_pairs = saved["pool_pairs"]
    pool_pull = jax.vjp(
        lambda keys_in, values_in, query_in: pool_chars(keys_in, values_in, query_in, visible),
        pool_pairs[:, :, 0],
        pool_pairs[:, :, 1],
        vectors[:, 4].reshape(CH, HD),
    )[1]
    pool_key_grad, pool_value_grad, query_vec_grad = pool_pull(pooled_grad)
    pair_grad = lowered(jnp.stack([pool_key_grad, pool_value_grad], 2)).reshape(char_rows, 2 * C)
    grad_pairs = row_summed(saved["pool_in"], pair_grad)
    second_grad = right_transposed(pair_grad, matrices[:, 4 * C + 2 * CM : 6 * C + 2 * CM])
    down_grad = lowered(second_grad)
    grad_down = row_summed(down_grad, saved["hidden"])
    grad_hidden = plain_product(down_grad, matrices[:, 4 * C + CM : 4 * C + 2 * CM])
    gelu_pull = jax.vjp(gelu_tanh, saved["hidden_pre"])[1]
    pre_grad = lowered(gelu_pull(grad_hidden)[0])
    grad_up = row_summed(saved["norm_two"], pre_grad)
    norm_pull = jax.vjp(norm_rows, saved["residual_one"], vectors[:, 2], vectors[:, 3])[1]
    first_norm, gain_two, shift_two = norm_pull(
        right_transposed(pre_grad, matrices[:, 4 * C : 4 * C + CM])
    )
    first_grad = second_grad + first_norm
    attn_grad = lowered(first_grad)
    grad_out = row_summed(saved["mixture"], attn_grad)
    mixed_grad = lowered(right_transposed(attn_grad, matrices[:, 3 * C : 4 * C])).reshape(
        LEN, W, CH, HD
    )
    triple = saved["triple"]
    attention = saved["attention"]
    prob_grad = jnp.einsum(
        "twhd,tshd->thws", mixed_grad, triple[:, :, 2], preferred_element_type=jnp.float32
    )
    score_grad = lowered(soft_back(attention, prob_grad, 3))
    query_grad = (
        jnp.einsum(
            "thws,tshd->twhd", score_grad, triple[:, :, 1], preferred_element_type=jnp.float32
        )
        * 0.125
    )
    key_grad = (
        jnp.einsum(
            "thws,twhd->tshd", score_grad, triple[:, :, 0], preferred_element_type=jnp.float32
        )
        * 0.125
    )
    value_grad = jnp.einsum(
        "thws,twhd->tshd", lowered(attention), mixed_grad, preferred_element_type=jnp.float32
    )
    triple_grad = lowered(jnp.stack([query_grad, key_grad, value_grad], 2)).reshape(
        char_rows, 3 * C
    )
    grad_triple = row_summed(saved["normed"], triple_grad)
    norm_pull = jax.vjp(norm_rows, saved["embedded"], vectors[:, 0], vectors[:, 1])[1]
    embed_norm, gain_one, shift_one = norm_pull(right_transposed(triple_grad, matrices[:, : 3 * C]))
    embed_grad = lowered(first_grad + embed_norm)
    grad_lookup = row_summed(saved["onehot"], embed_grad)
    per_word = jnp.sum(embed_grad.astype(jnp.float32).reshape(LEN, W, C), 1)
    grad_groups = lax.dot_general(
        per_word,
        saved["group_hot"].astype(jnp.float32),
        (((0,), (0,)), ((), ())),
        precision=HIGHEST,
        preferred_element_type=jnp.float32,
    )
    matrix_grad = jnp.concatenate(
        [grad_triple, grad_out, grad_up, grad_down, grad_pairs, grad_proj], 1
    ).reshape(-1, 128)
    vector_grad = jnp.stack(
        [gain_one, shift_one, gain_two, shift_two, query_vec_grad.reshape(C)], 1
    )
    return (matrix_grad, grad_lookup, grad_groups, vector_grad)


def gather_kernel(sizes, hc, hw, cm, wm, oc, ow, lsem, ss, rs, ss2, rs2):
    g = Grid(sizes)
    l1 = pltpu.make_async_copy(cm, oc.at[g.y, g.c, g.z, g.x], lsem.at[0])
    l2 = pltpu.make_async_copy(wm, ow.at[g.y, g.c, g.z, g.x], lsem.at[1])
    l1.start()
    l2.start()
    g.greet()
    a = Gather(g, cm, oc, Sems(ss, rs), hc)
    b = Gather(g, wm, ow, Sems(ss2, rs2), hw)
    a.start()
    b.start()
    l1.wait()
    l2.wait()
    for part in (a, b):
        part.step2()
        part.step3()
        part.step4()
        part.finish()
        part.drain()


def gather_all(sizes, cm, wm):
    Y, Z, X = sizes
    n = ag_count(Y, Z, X)
    sems = [pltpu.SemaphoreType.DMA((2,))] + [pltpu.SemaphoreType.DMA((n,))] * 4
    return pl.pallas_call(
        functools.partial(gather_kernel, sizes, half_of(cm.shape[0]), half_of(wm.shape[0])),
        out_shape=[jax.ShapeDtypeStruct((Y, 2, Z, X) + a.shape, a.dtype) for a in (cm, wm)],
        in_specs=[pl.BlockSpec(memory_space=pl.ANY)] * 2,
        out_specs=[pl.BlockSpec(memory_space=pl.ANY)] * 2,
        scratch_shapes=sems,
        compiler_params=pltpu.CompilerParams(collective_id=0, has_side_effects=True),
        name="gather",
    )(cm, wm)


def half_of(rows):
    return rows // 32 * 16


def scatter_kernel(sizes, hc, hw, cm, wm, oc, ow, Gc, Gw, lsem, ss, rs, ss2, rs2, *rv):
    g = Grid(sizes)
    l1 = pltpu.make_async_copy(cm, Gc, lsem.at[0])
    l2 = pltpu.make_async_copy(wm, Gw, lsem.at[1])
    l1.start()
    l2.start()
    g.greet()
    a = Scatter(g, Gc, rv[:6], Sems(ss, rs), hc)
    b = Scatter(g, Gw, rv[6:], Sems(ss2, rs2), hw)
    l1.wait()
    l2.wait()
    for part, out in ((b, ow), (a, oc)):
        part.start()
        part.step2()
        part.step3()
        part.step4()
        part.finish(out)
        part.drain()


def scatter_all(sizes, cm, wm):
    Y, Z, X = sizes
    n = rs_count(Y, Z, X)
    rc, rw = cm.shape[-2], wm.shape[-2]
    sems = [pltpu.SemaphoreType.DMA((2,))] + [pltpu.SemaphoreType.DMA((n,))] * 4
    return pl.pallas_call(
        functools.partial(scatter_kernel, sizes, half_of(rc), half_of(rw)),
        out_shape=[jax.ShapeDtypeStruct((r, 128), jnp.float32) for r in (rc, rw)],
        in_specs=[pl.BlockSpec(memory_space=pl.ANY)] * 2,
        out_specs=[pl.BlockSpec(memory_space=pltpu.VMEM)] * 2,
        scratch_shapes=[pltpu.VMEM(a.shape, a.dtype) for a in (cm, wm)]
        + sems
        + rs_scratch(Y, Z, X, rc, half_of(rc))
        + rs_scratch(Y, Z, X, rw, half_of(rw)),
        compiler_params=pltpu.CompilerParams(
            collective_id=1, has_side_effects=True, vmem_limit_bytes=60 << 20
        ),
        name="scatter",
    )(cm, wm)


def pack(pieces, lead):
    flat = jnp.concatenate([p.reshape(lead + (-1,)) for p in pieces], -1)
    have = flat.shape[-1]
    want = -(-have // 4096) * 4096
    flat = jnp.pad(flat, [(0, 0)] * len(lead) + [(0, want - have)])
    return flat.reshape(lead + (-1, 128))


def unpack(rows, shapes):
    lead = rows.shape[:-2]
    flat = rows.reshape(lead + (-1,))
    out, at = [], 0
    for shape in shapes:
        size = shape[0] * shape[1]
        out.append(flat[..., at : at + size].reshape((-1,) + shape[1:]))
        at += size
    return out


def shards(
    sizes,
    char_codes,
    char_counts,
    word_groups,
    valid_words,
    char_matrix,
    char_lookup,
    group_lookup,
    char_vectors,
    word_matrix,
    word_vectors,
    cotangent,
):
    symbols = char_codes[0]
    counts = char_counts[0]
    groups = word_groups[0]
    length = valid_words[0]
    small = (char_lookup, group_lookup, char_vectors, word_vectors)
    shapes = [a.shape for a in small]
    rows = char_matrix.shape[0]
    gc, gw = gather_all(
        sizes, jnp.concatenate([char_matrix, pack(small, ())]), word_matrix
    )
    lookup, group_cols, vectors, word_vecs = unpack(gc[..., rows:, :], shapes)
    char_parts = (gc[..., :rows, :].reshape(C, -1), lookup, group_cols, vectors)
    word_parts = (gw.reshape(D, -1), word_vecs)
    char_saved = char_forward(char_parts, symbols, counts, groups)
    word_saved = word_forward(word_parts, char_saved["word_input"], length)
    layer_out = lowered(word_saved["result"])[None]
    input_grad, word_mat_grad, word_vec_grad = word_backward(
        word_parts, word_saved, char_saved["word_input"], cotangent[0].astype(jnp.float32)
    )
    char_mat_grad, lookup_grad, group_grad, char_vec_grad = char_backward(
        char_parts, char_saved, input_grad
    )
    Y, Z, X = sizes
    lead = (Y, 2, Z, X)
    small_grads = pack(
        [g.astype(jnp.bfloat16) for g in (lookup_grad, group_grad, char_vec_grad, word_vec_grad)], lead
    )
    cg = jnp.concatenate([lowered(char_mat_grad).reshape(lead + (rows, 128)), small_grads], -2)
    wg = lowered(word_mat_grad).reshape(lead + (-1, 128))
    cs, ws = scatter_all(sizes, cg, wg)
    lookup_sum, group_sum, char_vec_sum, word_vec_sum = unpack(cs[rows:], shapes)
    return (layer_out, cs[:rows], lookup_sum, group_sum, char_vec_sum, ws, word_vec_sum)


def solution(mesh):
    dp, fsdp = mesh.shape["dp"], mesh.shape["fsdp"]
    Y = dp // 2
    X = Y if fsdp % Y == 0 else 1
    sizes = (Y, fsdp // X, X)
    placed = (
        P(("dp", "fsdp"), None, None),
        P(("dp", "fsdp"), None),
        P(("dp", "fsdp"), None),
        P(("dp", "fsdp")),
        P(("dp", "fsdp"), None),
        P(("dp", "fsdp"), None),
        P(("dp", "fsdp"), None),
        P(("dp", "fsdp"), None),
        P(("dp", "fsdp"), None),
        P(("dp", "fsdp"), None),
        P(("dp", "fsdp"), None, None),
    )
    return jax.shard_map(
        functools.partial(shards, sizes),
        mesh=mesh,
        in_specs=placed,
        out_specs=(
            P(("dp", "fsdp"), None, None),
            P(("dp", "fsdp"), None),
            P(("dp", "fsdp"), None),
            P(("dp", "fsdp"), None),
            P(("dp", "fsdp"), None),
            P(("dp", "fsdp"), None),
            P(("dp", "fsdp"), None),
        ),
        check_vma=False,
    )
```

```python
import functools

import jax
import jax.numpy as jnp
from jax import lax
from jax.experimental import pallas as pl
from jax.experimental.pallas import tpu as pltpu
from jax.sharding import PartitionSpec as P

C = 256
HD = 64
CH = 4
CM = 1024
D = 512
H = 8
FF = 2048
W = 16
VOCAB = 256
LANGS = 8
LEN = 128
C_COLS = 6 * C + 2 * CM + D
D_COLS = 4 * D + 2 * FF
EPSILON = 1e-05
NEGATIVE = -1000000000.0
F32 = jnp.float32
BF16 = jnp.bfloat16
FWD_ROWS = 256
BWD_ROWS = 256
STAGE = 0
VMEM_LIMIT = 63 << 20

MESH = pl.DeviceIdType.MESH


class Grid:
    def __init__(self, sizes):
        self.Y, self.Z, self.X = sizes
        dp, fs = lax.axis_index("dp"), lax.axis_index("fsdp")
        self.y, self.c = dp // 2, dp % 2
        self.z, self.x = fs // self.X, fs % self.X

    def at(self, y=None, c=None, z=None, x=None):
        y = self.y if y is None else y
        c = self.c if c is None else c
        z = self.z if z is None else z
        x = self.x if x is None else x
        return (y * 2 + c, z * self.X + x)

    def others(self, axis):
        n, me = {"y": (self.Y, self.y), "z": (self.Z, self.z), "x": (self.X, self.x)}[axis]
        return [(me + k) % n for k in range(1, n)]

    def partners(self):
        out = [self.at(c=1 - self.c)]
        for axis in "yzx":
            out += [self.at(**{axis: v}) for v in self.others(axis)]
        return out

    def greet(self):
        barrier = pltpu.get_barrier_semaphore()
        all_of = self.partners()
        for p in all_of:
            pl.semaphore_signal(barrier, inc=1, device_id=p, device_id_type=MESH)
        pl.semaphore_wait(barrier, len(all_of))


class Sems:
    def __init__(self, send, recv):
        self.send, self.recv, self.n = send, recv, 0

    def copy(self, src, dst, to):
        i = self.n
        self.n += 1
        d = pltpu.make_async_remote_copy(
            src_ref=src, dst_ref=dst, send_sem=self.send.at[i], recv_sem=self.recv.at[i],
            device_id=to, device_id_type=MESH)
        d.start()
        return d


def ag_count(Y, Z, X):
    return (Z - 1) + 1 + 2 * ((X - 1) + (Y - 1)) + 2 * ((X - 1) + (Y - 1))


class Gather:
    def __init__(self, grid, src, G, sems, half):
        self.g, self.src, self.G, self.s, self.half = grid, src, G, sems, half
        self.sent = []
        self.core = []

    def send(self, idx, to, keep):
        d = self.s.copy(self.G.at[idx], self.G.at[idx], to)
        self.sent.append(d)
        keep.append(d)

    def start(self):
        g = self.g
        self.p1 = []
        for z in g.others("z"):
            d = self.s.copy(self.src, self.G.at[g.y, g.c, g.z, g.x], g.at(z=z))
            self.sent.append(d)
            self.p1.append(d)

    def step2(self):
        g, h = self.g, self.half
        n = self.G.shape[4]
        self.A, self.B = pl.ds(0, h), pl.ds(h, n - h)
        for d in self.p1:
            d.wait_recv()
        self.p2a, self.p2b = [], []
        for x in g.others("x"):
            self.send((g.y, g.c, slice(None), g.x, self.A), g.at(x=x), self.p2a)
        for y in g.others("y"):
            self.send((g.y, g.c, slice(None), g.x, self.B), g.at(y=y), self.p2b)
        self.send((g.y, g.c, slice(None), g.x), g.at(c=1 - g.c), self.core)

    def step3(self):
        g = self.g
        self.p3a, self.p3b = [], []
        for d in self.p2a:
            d.wait_recv()
        for y in g.others("y"):
            self.send((g.y, g.c, slice(None), slice(None), self.A), g.at(y=y), self.p3a)
        for d in self.p2b:
            d.wait_recv()
        for x in g.others("x"):
            self.send((slice(None), g.c, slice(None), g.x, self.B), g.at(x=x), self.p3b)
        for x in g.others("x"):
            self.send((g.y, g.c, slice(None), x, self.A), g.at(c=1 - g.c), self.core)
        for y in g.others("y"):
            self.send((y, g.c, slice(None), g.x, self.B), g.at(c=1 - g.c), self.core)

    def step4(self):
        g = self.g
        for d in self.p3a:
            d.wait_recv()
        for y in g.others("y"):
            self.send((y, g.c, slice(None), slice(None), self.A), g.at(c=1 - g.c), self.core)
        for d in self.p3b:
            d.wait_recv()
        for x in g.others("x"):
            self.send((slice(None), g.c, slice(None), x, self.B), g.at(c=1 - g.c), self.core)

    def finish(self):
        for d in self.core:
            d.wait_recv()

    def drain(self):
        for d in self.sent:
            d.wait_send()


def rs_count(Y, Z, X):
    return 1 + 2 * ((X - 1) + (Y - 1)) + 2 * (Z - 1)


def rs_scratch(Y, Z, X, R, half):
    hb = R - half
    b = jnp.bfloat16
    return [
        pltpu.VMEM((Y, Z, X, R, 128), b),
        pltpu.VMEM((Y - 1, Z, X, half, 128), b),
        pltpu.VMEM((X - 1, Z, half, 128), b),
        pltpu.VMEM((X - 1, Y, Z, hb, 128), b),
        pltpu.VMEM((Y - 1, Z, hb, 128), b),
        pltpu.VMEM((Z - 1, R, 128), b),
    ]


def add_into(dst, srcs):
    lead = dst.shape[:-2]
    total = 1
    for n in lead:
        total *= n

    def body(i, _):
        idx, r = [], i
        for n in reversed(lead):
            idx.append(r % n)
            r = r // n
        idx = tuple(reversed(idx))
        acc = dst[idx].astype(jnp.float32)
        for s in srcs:
            acc = acc + s[idx].astype(jnp.float32)
        dst[idx] = acc.astype(jnp.bfloat16)
        return 0

    lax.fori_loop(0, total, body, 0)


class Scatter:
    def __init__(self, grid, PB, recv, sems, half):
        self.g, self.PB, self.s, self.half = grid, PB, sems, half
        self.r1, self.r2a, self.r3a, self.r2b, self.r3b, self.r4 = recv
        self.sent = []

    def send(self, src, dst, to, keep):
        d = self.s.copy(src, dst, to)
        self.sent.append(d)
        keep.append(d)

    def start(self):
        g = self.g
        self.p1 = []
        self.send(self.PB.at[:, 1 - g.c], self.r1, g.at(c=1 - g.c), self.p1)


    def step2(self):
        g, h = self.g, self.half
        n = self.PB.shape[4]
        self.A, self.B = pl.ds(0, h), pl.ds(h, n - h)
        for d in self.p1:
            d.wait_recv()
        add_into(self.PB.at[:, g.c], [self.r1])
        self.p2a, self.p2b = [], []
        for k, y in enumerate(g.others("y")):
            self.send(self.PB.at[y, g.c, :, :, self.A], self.r2a.at[k], g.at(y=y), self.p2a)
        for k, x in enumerate(g.others("x")):
            self.send(self.PB.at[:, g.c, :, x, self.B], self.r2b.at[k], g.at(x=x), self.p2b)

    def step3(self):
        g = self.g
        self.p3a, self.p3b = [], []
        for d in self.p2a:
            d.wait_recv()
        add_into(self.PB.at[g.y, g.c, :, :, self.A], [self.r2a.at[k] for k in range(g.Y - 1)])
        for k, x in enumerate(g.others("x")):
            self.send(self.PB.at[g.y, g.c, :, x, self.A], self.r3a.at[k], g.at(x=x), self.p3a)
        for d in self.p2b:
            d.wait_recv()
        add_into(self.PB.at[:, g.c, :, g.x, self.B], [self.r2b.at[k] for k in range(g.X - 1)])
        for k, y in enumerate(g.others("y")):
            self.send(self.PB.at[y, g.c, :, g.x, self.B], self.r3b.at[k], g.at(y=y), self.p3b)

    def step4(self):
        g = self.g
        self.p4 = []
        for part, waits, recv in ((self.A, self.p3a, self.r3a), (self.B, self.p3b, self.r3b)):
            for d in waits:
                d.wait_recv()
            add_into(self.PB.at[g.y, g.c, :, g.x, part], [recv.at[k] for k in range(recv.shape[0])])
            for k, z in enumerate(g.others("z")):
                self.send(self.PB.at[g.y, g.c, z, g.x, part], self.r4.at[k, part], g.at(z=z), self.p4)

    def finish(self, place, rows, count):
        g = self.g
        for d in self.p4:
            d.wait_recv()
        unit = max(1, 16 // rows)
        for t in range(-(-count // unit)):
            r = slice(t * unit * rows, (t + 1) * unit * rows)
            acc = self.PB[g.y, g.c, g.z, g.x, r].astype(jnp.float32)
            for k in range(g.Z - 1):
                acc = acc + self.r4[k, r].astype(jnp.float32)
            for u in range(unit):
                if t * unit + u < count:
                    place(t * unit + u, acc[u * rows : (u + 1) * rows])

    def drain(self):
        for d in self.sent:
            d.wait_send()


def dot(a, b):
    return lax.dot_general(a, b, (((1,), (0,)), ((), ())), preferred_element_type=F32)


def dot_nt(a, b):
    return lax.dot_general(a, b, (((1,), (1,)), ((), ())), preferred_element_type=F32)


def dot_tn(a, b):
    return lax.dot_general(a, b, (((0,), (0,)), ((), ())), preferred_element_type=F32)


def low(v):
    return v.astype(BF16)


def norm_stats(x):
    centre = x - jnp.mean(x, -1, keepdims=True)
    spread = jnp.mean(centre * centre, -1, keepdims=True)
    scale = lax.rsqrt(spread + EPSILON)
    return centre * scale, scale


def norm_back(grad, xhat, scale, gain):
    inner = grad * gain
    first = jnp.mean(inner, -1, keepdims=True)
    second = jnp.mean(inner * xhat, -1, keepdims=True)
    return scale * (inner - first - xhat * second)


def gelu_both(z):
    sq = z * z
    t = jnp.tanh(z * (0.7978845608028654 + (0.7978845608028654 * 0.044715) * sq))
    h = 0.5 * z
    value = h + h * t
    slope = 0.5 + 0.5 * t + h * (1.0 - t * t) * (
        0.7978845608028654 + (3.0 * 0.7978845608028654 * 0.044715) * sq
    )
    return value, slope


def iota(shape, dim):
    return lax.broadcasted_iota(jnp.int32, shape, dim)


def head_rows(dtype):
    lane = iota((1, 128), 1)
    return [(lane // HD == h).astype(F32).astype(dtype) for h in range(2)]


def head_stack(block, heads):
    return jnp.concatenate([block * h for h in heads], 0)


def own_word(scores, lane_word):
    split = scores.reshape(2, 8, W, 128)
    out = split[:, 0]
    for w in range(1, 8):
        out = jnp.where(lane_word == w, split[:, w], out)
    return out


def spread_words(compact, word_rows):
    return jnp.concatenate([compact[h] * word_rows[w] for h in range(2) for w in range(8)], 0)


def side_by_side(stacked, rows):
    return jnp.concatenate([stacked[h * rows : (h + 1) * rows] for h in range(2)], 1)


def place_own(own, raw, staged, extra, rows, blocks, total):
    staged[...] = raw[...].astype(F32)
    unit = max(1, 16 // rows)

    def block(j):
        if j < blocks:
            if rows == 1:
                return staged[j : j + 1, :]
            return staged[pl.ds(j, rows, stride=blocks), :]
        at = (j - blocks) * 128
        if at < extra.shape[1]:
            return extra[:, at : at + 128]
        return jnp.zeros((rows, 128), F32)

    for t in range(total // unit):
        tile = jnp.concatenate([block(j) for j in range(t * unit, (t + 1) * unit)], 0)
        own[t * unit * rows : (t + 1) * unit * rows, :] = low(tile)


def assemble(G, Wd, rows, total):
    unit = max(1, 16 // rows)
    devices = Wd.shape[0] // rows
    for t in range(total // unit):
        tile = G[:, :, :, :, t * unit * rows : (t + 1) * unit * rows, :]
        if unit == 1:
            Wd[:, t * 128 : (t + 1) * 128] = tile.reshape(devices * rows, 128)
            continue
        tile = tile.reshape(devices, 16, 128).astype(F32)
        for u in range(unit):
            j = t * unit + u
            Wd[:, j * 128 : (j + 1) * 128] = low(
                tile[:, u * rows : (u + 1) * rows, :].reshape(devices * rows, 128)
            )


def pack_blocks(PB, at, blocks, rows):
    unit = max(1, 16 // rows)
    lead = PB.shape[:4]
    devices = lead[0] * lead[1] * lead[2] * lead[3]
    for t in range(len(blocks) // unit):
        parts = [b.reshape(devices, rows, 128) for b in blocks[t * unit : (t + 1) * unit]]
        tile = low(parts[0] if unit == 1 else jnp.concatenate(parts, 1))
        row = (at + t * unit) * rows
        PB[:, :, :, :, row : row + unit * rows, :] = tile.reshape(lead + (unit * rows, 128))


def columns(value):
    return [value[:, k : k + 128] for k in range(0, value.shape[1], 128)]


class Layout:
    def __init__(self, sizes):
        self.sizes = sizes
        Y, Z, X = sizes
        self.lead = (Y, 2, Z, X)
        self.devices = Y * 2 * Z * X
        self.rc = C // self.devices
        self.rw = D // self.devices
        self.bc = C_COLS // 128
        self.bw = D_COLS // 128

        def padded(n, rows):
            unit = max(1, 16 // rows)
            return max(-(-n // unit), 2) * unit

        self.jc = padded(self.bc + 3, self.rc)
        self.jw = padded(self.bw + 1, self.rw)
        self.j1 = padded(24, self.rc)
        self.j2 = padded(11, self.rc)


def half_of(rows):
    return max(16, rows // 32 * 16)


def mono(
    lay, stage, ints, cm, exc, wm, exw, cot,
    out_y, out_cm, out_lookup, out_group, out_vec, out_wm, out_wvec,
    Gc, Gw, Wc, Wwt, PB1, PB2, PBw, stc, stw,
    xh1, n1s, qkvs, probs, os, xh2, n2s, acts, slopes, r2s, alphas, scales, dr1s,
    Us, Ys, accq, acco, accu, accd, acct, sums, tsum,
    lsem, ssc, rsc, ssw, rsw, ss1, rs1, ss2, rs2, ssx, rsx, *recv,
):
    Y, Z, X = lay.sizes
    g = Grid(lay.sizes)
    me = (g.y, g.c, g.z, g.x)
    on = stage

    ag_c = Gather(g, Gc.at[me], Gc, Sems(ssc, rsc), half_of(Gc.shape[4]))
    ag_w = Gather(g, Gw.at[me], Gw, Sems(ssw, rsw), half_of(Gw.shape[4]))
    place_own(Gc.at[me], cm, stc, exc, lay.rc, lay.bc, lay.jc)
    g.greet()
    ag_c.start()
    place_own(Gw.at[me], wm, stw, exw, lay.rw, lay.bw, lay.jw)
    ag_w.start()
    ag_c.step2()
    ag_c.step3()
    ag_c.step4()
    ag_c.finish()
    assemble(Gc, Wc, lay.rc, lay.jc)

    eye = (iota((16, 128), 0) == iota((16, 128), 1)).astype(F32).astype(BF16)
    rows_c = dot_nt(eye, Wc[:, (lay.bc + 2) * 128 : (lay.bc + 3) * 128])
    gain1, shift1, gain2, shift2 = (rows_c[8 + k : 9 + k] for k in range(4))
    query = rows_c[12:13]
    table_low = low(jnp.where(iota((16, C), 0) < LANGS, rows_c, 0.0))
    lookup = slice(lay.bc * 128, (lay.bc + 2) * 128)
    AQ, AO = slice(0, 3 * C), slice(3 * C, 4 * C)
    AU, AD = slice(4 * C, 4 * C + CM), slice(4 * C + CM, 4 * C + 2 * CM)
    PK, PV = slice(4 * C + 2 * CM, 5 * C + 2 * CM), slice(5 * C + 2 * CM, 6 * C + 2 * CM)
    PR = slice(6 * C + 2 * CM, 6 * C + 2 * CM + D)

    lane = iota((1, 128), 1)
    lane_word = lane // W
    word_rows = [(lane_word == w).astype(F32).astype(BF16) for w in range(8)]
    heads = head_rows(BF16)
    head_of = iota((128, C), 0) % 32 // 8 == iota((128, C), 1) // HD
    pq_rows = jnp.where(head_of, query * 0.125, 0.0)
    score_map = dot_nt(low(pq_rows), Wc[:, PK])
    map_hi = low(score_map)
    map_lo = low(score_map - map_hi.astype(F32))
    key_row = iota((1, W, 1), 1)
    pool_own = iota((128, 128), 0) // W == iota((128, 128), 1) % 8
    pool_slot = iota((128, 128), 0) % W

    def onehots(i, groups):
        parts = []
        for k in range(groups):
            r = i * groups + k
            codes = ints[pl.ds(r, 1), :]
            langs = ints[pl.ds(16 + r, 1), :]
            a = (iota((VOCAB, 128), 0) == codes).astype(F32).astype(BF16)
            b = (iota((16, 128), 0) == langs).astype(F32).astype(BF16)
            parts.append(jnp.concatenate([a, b], 0))
        return parts

    GF = FWD_ROWS // 128

    def forward(i, _):
        rows = pl.ds(pl.multiple_of(i * FWD_ROWS, FWD_ROWS), FWD_ROWS)
        table = jnp.concatenate([Wc[:, lookup], table_low], 0)
        e = jnp.concatenate([dot_tn(h, table) for h in onehots(i, GF)], 0)
        xhat, scale1 = norm_stats(e)
        n1 = low(xhat * gain1 + shift1)
        xh1[rows, :] = low(xhat)
        n1s[rows, :] = n1
        qkv = low(dot(n1, Wc[:, AQ]))
        qkvs[rows, :] = qkv
        mixed = []
        for k in range(GF):
            visible = key_row < ints[pl.ds(32 + i * GF + k, 1), :].reshape(1, 1, 128)
            pair_out = []
            for p in range(2):
                q, kk, v = (
                    qkv[k * 128 : (k + 1) * 128, b * C + p * 128 : b * C + (p + 1) * 128]
                    for b in range(3)
                )
                s = own_word(dot_nt(head_stack(kk, heads), q), lane_word) * 0.125
                s = jnp.where(visible, s, NEGATIVE)
                s = jnp.exp(s - jnp.max(s, 1, keepdims=True))
                prob = s / jnp.sum(s, 1, keepdims=True)
                probs[i * GF + k, 2 * p : 2 * p + 2] = prob
                pair_out.append(dot_tn(spread_words(low(prob), word_rows), head_stack(v, heads)))
            mixed.append(jnp.concatenate(pair_out, 1))
        o = low(jnp.concatenate(mixed, 0))
        os[rows, :] = o
        r1 = e + dot(o, Wc[:, AO])
        xhat, scale2 = norm_stats(r1)
        n2 = low(xhat * gain2 + shift2)
        xh2[rows, :] = low(xhat)
        n2s[rows, :] = n2
        scales[rows, 0:1] = scale1
        scales[rows, 1:2] = scale2
        value, slope = gelu_both(dot(n2, Wc[:, AU]))
        act = low(value)
        acts[rows, :] = act
        slopes[rows, :] = low(slope)
        r2 = low(r1 + dot_nt(act, Wc[:, AD]))
        r2s[rows, :] = r2
        for k in range(GF):
            r = i * GF + k
            own = r2[k * 128 : (k + 1) * 128]
            s = dot_nt(own, map_hi) + dot_nt(own, map_lo)
            seen = pool_own & (pool_slot < ints[pl.ds(48 + r, 1), :])
            s = jnp.where(seen, s, NEGATIVE)
            s = jnp.where(seen, jnp.exp(s - jnp.max(s, 0, keepdims=True)), 0.0)
            alpha = s / jnp.sum(s, 0, keepdims=True)
            alphas[pl.ds(pl.multiple_of(r * 128, 128), 128), :] = alpha
            u = dot_tn(low(alpha)[:, :32], own)
            for h in range(CH):
                Us[h, pl.ds(pl.multiple_of(r * 8, 8), 8), :] = u[8 * h : 8 * h + 8]
        return 0

    nf = LEN * W // FWD_ROWS
    lax.fori_loop(0, nf // 2, forward, 0)
    ag_w.step2()
    ag_w.step3()
    lax.fori_loop(nf // 2, nf, forward, 0)
    ag_w.step4()

    head_c = [iota((1, C), 1) // HD == h for h in range(CH)]
    pooled = sum(jnp.where(head_c[h], dot(low(Us[h]), Wc[:, PV]), 0.0) for h in range(CH))
    pooled_low = low(pooled)
    w_in = dot(pooled_low, Wc[:, PR])

    ag_w.finish()
    if lay.rw >= 16:

        def wcols(lo, hi):
            return jnp.concatenate(
                [
                    Gw[:, :, :, :, j * lay.rw : (j + 1) * lay.rw, :].reshape(D, 128)
                    for j in range(lo // 128, hi // 128)
                ],
                1,
            )

    else:
        assemble(Gw, Wwt, lay.rw, lay.jw)

        def wcols(lo, hi):
            return Wwt[:, lo:hi]

    rows_w = dot_nt(eye, wcols(D_COLS, D_COLS + 128))
    f1, c1, f2, c2 = (rows_w[k : k + 1] for k in range(4))
    BQ, BO, BU, BD = (0, 3 * D), (3 * D, 4 * D), (4 * D, 4 * D + FF), (4 * D + FF, D_COLS)
    NP = H // 2

    xhat1, sc1 = norm_stats(w_in)
    m1 = low(xhat1 * f1 + c1)
    qkv = low(dot(m1, wcols(*BQ)))
    key = iota((1, 128, 1), 1)
    seen_word = (key <= iota((1, 1, 128), 2)) & (key < ints[64:65, :].reshape(1, 1, 128))
    pw, kst, qst, vst, mix = [], [], [], [], []
    for p in range(NP):
        q, kk, v = (qkv[:, b * D + p * 128 : b * D + (p + 1) * 128] for b in range(3))
        kst.append(head_stack(kk, heads))
        qst.append(head_stack(q, heads))
        vst.append(head_stack(v, heads))
        s = dot_nt(kst[p], q).reshape(2, 128, 128) * 0.125
        s = jnp.where(seen_word, s, NEGATIVE)
        s = jnp.exp(s - jnp.max(s, 1, keepdims=True))
        pw.append(s / jnp.sum(s, 1, keepdims=True))
        mix.append(dot_tn(low(pw[p]).reshape(256, 128), vst[p]))
    ow = low(jnp.concatenate(mix, 1))
    x = w_in + dot(ow, wcols(*BO))
    xhat2, sc2 = norm_stats(x)
    m2 = low(xhat2 * f2 + c2)
    value, slope = gelu_both(dot(m2, wcols(*BU)))
    aw = low(value)
    out_y[...] = low(x + dot_nt(aw, wcols(*BD)))

    gy = cot[...]
    dy = gy.astype(F32)
    rw = lay.rw
    unit_w = max(1, 16 // rw)
    waiting = {}

    def put_w(at, blocks):
        waiting.update({at + k: b for k, b in enumerate(blocks)})
        for first in range(0, lay.jw, unit_w):
            ready = range(first, first + unit_w)
            if all(j in waiting for j in ready):
                pack_blocks(PBw, first, [waiting.pop(j) for j in ready], rw)

    for k in range(0, FF, 512):
        put_w((BD[0] + k) // 128, columns(dot_tn(gy, aw[:, k : k + 512])))
    gzw = low(slope * dot(gy, wcols(*BD)))
    for k in range(0, FF, 512):
        put_w((BU[0] + k) // 128, columns(dot_tn(m2, gzw[:, k : k + 512])))
    dm2 = dot_nt(gzw, wcols(*BU))
    gf2 = jnp.sum(dm2 * xhat2, 0, keepdims=True)
    gc2 = jnp.sum(dm2, 0, keepdims=True)
    dx = dy + norm_back(dm2, xhat2, sc2, f2)
    gx = low(dx)
    put_w(BO[0] // 128, columns(dot_tn(ow, gx)))
    gow = low(dot_nt(gx, wcols(*BO)))
    gq, gk, gv = [], [], []
    for p in range(NP):
        go = gow[:, p * 128 : (p + 1) * 128]
        dp = dot_nt(vst[p], go).reshape(2, 128, 128)
        inner = jnp.sum(pw[p] * dp, 1, keepdims=True)
        gs = low(pw[p] * (dp - inner)).reshape(256, 128)
        gq.append(dot_tn(gs, kst[p]) * 0.125)
        gk.append(dot(side_by_side(gs, 128), qst[p]) * 0.125)
        gv.append(dot(side_by_side(low(pw[p]).reshape(256, 128), 128), head_stack(go, heads)))
    tg = low(jnp.concatenate(gq + gk + gv, 1))
    for k in range(0, 3 * D, 512):
        put_w(k // 128, columns(dot_tn(m1, tg[:, k : k + 512])))
    dm1 = dot_nt(tg, wcols(*BQ))
    gf1 = jnp.sum(dm1 * xhat1, 0, keepdims=True)
    gc1 = jnp.sum(dm1, 0, keepdims=True)
    dw = dx + norm_back(dm1, xhat1, sc1, f1)
    vec_rows = low(jnp.concatenate([gf1, gc1, gf2, gc2, jnp.zeros((12, D), F32)], 0))
    zero_w = [jnp.zeros((D, 128), F32)] * (lay.jw - lay.bw - 1)
    put_w(lay.bw, [dot_tn(vec_rows, eye)] + zero_w)
    rs_w = Scatter(g, PBw, recv[0:6], Sems(ssx, rsx), half_of(PBw.shape[4]))
    rs_w.start()

    gw = low(dw)
    grad_pr = dot_tn(pooled_low, gw)
    dpool = dot_nt(gw, Wc[:, PR])
    dp4 = jnp.concatenate([low(jnp.where(head_c[h], dpool, 0.0)) for h in range(CH)], 0)
    Ys[...] = dot_nt(dp4, Wc[:, PV]).reshape(CH, LEN, C)
    grad_pv = dot_tn(low(Us[...]).reshape(CH * LEN, C), dp4)
    for ref in (accq, acco, accu, accd, acct, sums, tsum):
        ref[...] = jnp.zeros(ref.shape, F32)

    map32 = map_hi[:32]
    GB = BWD_ROWS // 128

    def back_ffn(i, _):
        rows = pl.ds(pl.multiple_of(i * BWD_ROWS, BWD_ROWS), BWD_ROWS)
        parts = []
        for k in range(GB):
            r = i * GB + k
            own = r2s[pl.ds(pl.multiple_of(r * 128, 128), 128), :]
            alpha = alphas[pl.ds(pl.multiple_of(r * 128, 128), 128), :][:, :32]
            yg = low(
                jnp.concatenate(
                    [Ys[h, pl.ds(pl.multiple_of(r * 8, 8), 8), :] for h in range(CH)], 0
                )
            )
            da = dot_nt(own, yg)
            dr = low(alpha * (da - jnp.sum(alpha * da, 0, keepdims=True)))
            tsum[...] += dot_tn(dr, own)
            parts.append(dot(low(alpha), yg) + dot(dr, map32))
        dr2 = jnp.concatenate(parts, 0)
        g2 = low(dr2)
        accd[...] += dot_tn(g2, acts[rows, :])
        gz = low(slopes[rows, :].astype(F32) * dot(g2, Wc[:, AD]))
        accu[...] += dot_tn(n2s[rows, :], gz)
        dn = dot_nt(gz, Wc[:, AU])
        xhat = xh2[rows, :].astype(F32)
        sums[2:3, :] += jnp.sum(dn * xhat, 0, keepdims=True)
        sums[3:4, :] += jnp.sum(dn, 0, keepdims=True)
        dr1s[rows, :] = dr2 + norm_back(dn, xhat, scales[rows, 1:2], gain2)
        return 0

    nb = LEN * W // BWD_ROWS
    lax.fori_loop(0, nb // 2, back_ffn, 0)
    rs_w.step2()
    lax.fori_loop(nb // 2, nb, back_ffn, 0)
    rs_w.step3()

    t_low = low(tsum[...])
    grad_pk = dot_tn(t_low, low(pq_rows[:32]))
    rc = lay.rc
    pad1 = [jnp.zeros((C, 128), F32)] * (lay.j1 - 24)
    pack_blocks(
        PB1,
        0,
        columns(accu[...]) + columns(accd[...]) + columns(grad_pk) + columns(grad_pv)
        + columns(grad_pr) + pad1,
        rc,
    )
    rs_1 = Scatter(g, PB1, recv[6:12], Sems(ss1, rs1), half_of(PB1.shape[4]))
    rs_1.start()
    gpq = dot(t_low, Wc[:, PK]) * 0.125
    gpq = jnp.sum(
        jnp.where(iota((32, C), 0) // 8 == iota((32, C), 1) // HD, gpq, 0.0), 0, keepdims=True
    )

    def back_attention(i, _):
        rows = pl.ds(pl.multiple_of(i * BWD_ROWS, BWD_ROWS), BWD_ROWS)
        dr1 = dr1s[rows, :]
        g1 = low(dr1)
        acco[...] += dot_tn(os[rows, :], g1)
        go = low(dot_nt(g1, Wc[:, AO]))
        qkv = qkvs[rows, :]
        grads = [[], [], []]
        for k in range(GB):
            part = [[], [], []]
            for p in range(2):
                at = slice(k * 128, (k + 1) * 128)
                q, kk, v = (
                    qkv[at, b * C + p * 128 : b * C + (p + 1) * 128] for b in range(3)
                )
                gop = go[at, p * 128 : (p + 1) * 128]
                prob = probs[i * GB + k, 2 * p : 2 * p + 2]
                dp = own_word(dot_nt(head_stack(v, heads), gop), lane_word)
                gs = low(prob * (dp - jnp.sum(prob * dp, 1, keepdims=True)))
                gs = spread_words(gs, word_rows)
                pb = spread_words(low(prob), word_rows)
                part[0].append(dot_tn(gs, head_stack(kk, heads)) * 0.125)
                part[1].append(dot(side_by_side(gs, 128), head_stack(q, heads)) * 0.125)
                part[2].append(dot(side_by_side(pb, 128), head_stack(gop, heads)))
            for b in range(3):
                grads[b].append(jnp.concatenate(part[b], 1))
        tg = low(jnp.concatenate([jnp.concatenate(b, 0) for b in grads], 1))
        accq[...] += dot_tn(n1s[rows, :], tg)
        dn = dot_nt(tg, Wc[:, AQ])
        xhat = xh1[rows, :].astype(F32)
        sums[0:1, :] += jnp.sum(dn * xhat, 0, keepdims=True)
        sums[1:2, :] += jnp.sum(dn, 0, keepdims=True)
        ge = low(dr1 + norm_back(dn, xhat, scales[rows, 0:1], gain1))
        for k, h in enumerate(onehots(i, GB)):
            acct[...] += dot(h, ge[k * 128 : (k + 1) * 128])
        return 0

    lax.fori_loop(0, nb // 2, back_attention, 0)
    rs_w.step4()
    rs_1.step2()
    lax.fori_loop(nb // 2, nb, back_attention, 0)
    rs_1.step3()

    small = low(jnp.concatenate([acct[VOCAB : VOCAB + 8], sums[0:4], gpq, jnp.zeros((3, C), F32)], 0))
    pad2 = [jnp.zeros((C, 128), F32)] * (lay.j2 - 11)
    pack_blocks(
        PB2,
        0,
        columns(accq[...]) + columns(acco[...]) + columns(acct[0:VOCAB, :])
        + [dot_tn(small, eye)] + pad2,
        rc,
    )
    rs_2 = Scatter(g, PB2, recv[12:18], Sems(ss2, rs2), half_of(PB2.shape[4]))
    rs_2.start()
    rs_1.step4()
    rs_2.step2()
    rs_2.step3()

    def put(out, blocks, j, value):
        if value.shape[0] == 1:
            out[j : j + 1, :] = value
        else:
            out[pl.ds(j, value.shape[0], stride=blocks), :] = value

    def place_w(j, value):
        if j < lay.bw:
            put(out_wm, lay.bw, j, value)
        else:
            out_wvec[...] = value[:, 0:4]

    def place_1(j, value):
        put(out_cm, lay.bc, 8 + j, value)

    def place_2(j, value):
        if j < 8:
            put(out_cm, lay.bc, j, value)
        elif j < 10:
            out_lookup[:, (j - 8) * 128 : (j - 7) * 128] = value
        else:
            out_group[...] = value[:, 0:LANGS]
            out_vec[...] = value[:, LANGS : LANGS + 5]

    rs_w.finish(place_w, rw, lay.bw + 1)
    rs_1.finish(place_1, rc, 24)
    rs_2.step4()
    rs_2.finish(place_2, rc, 11)
    for part in (ag_c, ag_w, rs_w, rs_1, rs_2):
        part.drain()


def shards(
    sizes,
    char_codes,
    char_counts,
    word_groups,
    valid_words,
    char_matrix,
    char_lookup,
    group_lookup,
    char_vectors,
    word_matrix,
    word_vectors,
    cotangent,
):
    lay = Layout(sizes)
    Y, Z, X = sizes
    counts = char_counts[0]
    ints = jnp.concatenate(
        [
            char_codes.reshape(16, 128),
            jnp.repeat(word_groups.reshape(16, 8), W, 1),
            jnp.repeat(counts.reshape(16, 8), W, 1),
            jnp.tile(counts.reshape(16, 8), (1, 16)),
            jnp.broadcast_to(valid_words[:, None], (8, 128)),
        ]
    )
    exc = jnp.concatenate(
        [char_lookup, group_lookup, char_vectors, jnp.zeros((lay.rc, 128 - LANGS - 5), BF16)], 1
    ).astype(F32)
    exw = jnp.pad(word_vectors.astype(F32), ((0, 0), (0, 124)))

    def vm(shape, dtype):
        return pltpu.VMEM(shape, dtype)

    rows = LEN * W
    rows1, rows2, rowsw = lay.j1 * lay.rc, lay.j2 * lay.rc, lay.jw * lay.rw
    nag, nrs = ag_count(Y, Z, X), rs_count(Y, Z, X)
    scratch = [
        vm(lay.lead + (lay.jc * lay.rc, 128), BF16),
        vm(lay.lead + (rowsw, 128), BF16),
        vm((C, lay.jc * 128), BF16),
        vm((D, lay.jw * 128) if lay.rw < 16 else (16, 128), BF16),
        vm(lay.lead + (rows1, 128), BF16),
        vm(lay.lead + (rows2, 128), BF16),
        vm(lay.lead + (rowsw, 128), BF16),
        vm(char_matrix.shape, F32),
        vm(word_matrix.shape, F32),
        vm((rows, C), BF16),
        vm((rows, C), BF16),
        vm((rows, 3 * C), BF16),
        vm((16, CH, W, 128), F32),
        vm((rows, C), BF16),
        vm((rows, C), BF16),
        vm((rows, C), BF16),
        vm((rows, CM), BF16),
        vm((rows, CM), BF16),
        vm((rows, C), BF16),
        vm((rows, 128), F32),
        vm((rows, 128), F32),
        vm((rows, C), F32),
        vm((CH, LEN, C), F32),
        vm((CH, LEN, C), F32),
        vm((C, 3 * C), F32),
        vm((C, C), F32),
        vm((C, CM), F32),
        vm((C, CM), F32),
        vm((VOCAB + 16, C), F32),
        vm((8, C), F32),
        vm((32, C), F32),
        pltpu.SemaphoreType.DMA((1,)),
    ]
    for n in (nag, nag, nrs, nrs, nrs):
        scratch += [pltpu.SemaphoreType.DMA((n,))] * 2
    for r in (rowsw, rows1, rows2):
        scratch += rs_scratch(Y, Z, X, r, half_of(r))
    vmem = pl.BlockSpec(memory_space=pltpu.VMEM)
    outs = [
        jax.ShapeDtypeStruct((LEN, D), BF16),
        jax.ShapeDtypeStruct(char_matrix.shape, F32),
        jax.ShapeDtypeStruct(char_lookup.shape, F32),
        jax.ShapeDtypeStruct(group_lookup.shape, F32),
        jax.ShapeDtypeStruct(char_vectors.shape, F32),
        jax.ShapeDtypeStruct(word_matrix.shape, F32),
        jax.ShapeDtypeStruct(word_vectors.shape, F32),
    ]
    got = pl.pallas_call(
        functools.partial(mono, lay, STAGE),
        out_shape=outs,
        in_specs=[vmem] * 6,
        out_specs=[vmem] * 7,
        scratch_shapes=scratch,
        compiler_params=pltpu.CompilerParams(
            collective_id=0, has_side_effects=True, vmem_limit_bytes=VMEM_LIMIT
        ),
        name="layer",
    )(ints, char_matrix, exc, word_matrix, exw, cotangent[0])
    return (got[0][None],) + tuple(got[1:])


def solution(mesh):
    dp, fsdp = mesh.shape["dp"], mesh.shape["fsdp"]
    Y = dp // 2
    X = Y if fsdp % Y == 0 else 1
    sizes = (Y, fsdp // X, X)
    placed = (
        P(("dp", "fsdp"), None, None),
        P(("dp", "fsdp"), None),
        P(("dp", "fsdp"), None),
        P(("dp", "fsdp")),
        P(("dp", "fsdp"), None),
        P(("dp", "fsdp"), None),
        P(("dp", "fsdp"), None),
        P(("dp", "fsdp"), None),
        P(("dp", "fsdp"), None),
        P(("dp", "fsdp"), None),
        P(("dp", "fsdp"), None, None),
    )
    return jax.shard_map(
        functools.partial(shards, sizes),
        mesh=mesh,
        in_specs=placed,
        out_specs=(
            P(("dp", "fsdp"), None, None),
            P(("dp", "fsdp"), None),
            P(("dp", "fsdp"), None),
            P(("dp", "fsdp"), None),
            P(("dp", "fsdp"), None),
            P(("dp", "fsdp"), None),
            P(("dp", "fsdp"), None),
        ),
        check_vma=False,
    )
```

```python
import functools

import jax
import jax.numpy as jnp
from jax import lax
from jax.experimental import pallas as pl
from jax.experimental.pallas import tpu as pltpu
from jax.sharding import PartitionSpec as P

C = 256
HD = 64
CH = 4
CM = 1024
D = 512
H = 8
FF = 2048
W = 16
VOCAB = 256
LANGS = 8
LEN = 128
C_COLS = 6 * C + 2 * CM + D
D_COLS = 4 * D + 2 * FF
EPSILON = 1e-05
NEGATIVE = -1000000000.0
F32 = jnp.float32
BF16 = jnp.bfloat16
FWD_ROWS = 256
BWD_ROWS = 256
AG_PARTS_C = 2
AG_PARTS_W = 3
VMEM_LIMIT = 63 << 20
STAGE = 0


MESH = pl.DeviceIdType.MESH
ALL = slice(None)


class Grid:
    def __init__(self, sizes):
        self.Y, self.Z, self.X = sizes
        dp, fs = lax.axis_index("dp"), lax.axis_index("fsdp")
        self.y, self.c = dp // 2, dp % 2
        self.z, self.x = fs // self.X, fs % self.X
        self.me = (self.y, self.c, self.z, self.x)
        self.ys = [(self.y + k) % self.Y for k in range(1, self.Y)]
        self.zs = [(self.z + k) % self.Z for k in range(1, self.Z)]
        self.xs = [(self.x + k) % self.X for k in range(1, self.X)]
        self.to_y = [self.at(y=y) for y in self.ys]
        self.to_z = [self.at(z=z) for z in self.zs]
        self.to_x = [self.at(x=x) for x in self.xs]
        self.to_c = self.at(c=1 - self.c)

    def at(self, y=None, c=None, z=None, x=None):
        y = self.y if y is None else y
        c = self.c if c is None else c
        z = self.z if z is None else z
        x = self.x if x is None else x
        return (y * 2 + c, z * self.X + x)

    def greet(self):
        barrier = pltpu.get_barrier_semaphore()
        partners = [self.to_c] + self.to_y + self.to_z + self.to_x
        for p in partners:
            pl.semaphore_signal(barrier, inc=1, device_id=p, device_id_type=MESH)
        pl.semaphore_wait(barrier, len(partners))


class Copies:
    def __init__(self, send, recv):
        self.send, self.recv, self.made = send, recv, []

    def plan(self, src, dst, to):
        self.made.append((src, dst, to))
        return len(self.made) - 1

    def make(self, i):
        src, dst, to = self.made[i]
        return pltpu.make_async_remote_copy(
            src_ref=src,
            dst_ref=dst,
            send_sem=self.send.at[i],
            recv_sem=self.recv.at[i],
            device_id=to,
            device_id_type=MESH,
        )

    def start(self, which):
        for i in which:
            self.make(i).start()

    def arrived(self, which):
        for i in which:
            self.make(i).wait_recv()

    def left(self, which):
        for i in which:
            self.make(i).wait_send()


def ag_count(Y, Z, X):
    return (Z - 1) + 1 + 4 * ((X - 1) + (Y - 1))


class Gather:
    def __init__(self, g, G, copies, lo, hi):
        mid = lo + (hi - lo + 31) // 32 * 16
        both, a, b = slice(lo, hi), slice(lo, mid), slice(mid, hi)
        self.copies = copies
        first = len(copies.made)

        def plan(to, *idx):
            return copies.plan(G.at[idx], G.at[idx], to)

        y, c, z, x = g.me
        self.p1 = [plan(to, y, c, z, x, both) for to in g.to_z]
        self.p2a = [plan(to, y, c, ALL, x, a) for to in g.to_x]
        self.p2b = [plan(to, y, c, ALL, x, b) for to in g.to_y]
        self.c1 = [plan(g.to_c, y, c, ALL, x, both)]
        self.p3a = [plan(to, y, c, ALL, ALL, a) for to in g.to_y]
        self.p3b = [plan(to, ALL, c, ALL, x, b) for to in g.to_x]
        self.c2a = [plan(g.to_c, y, c, ALL, v, a) for v in g.xs]
        self.c2b = [plan(g.to_c, v, c, ALL, x, b) for v in g.ys]
        self.c3a = [plan(g.to_c, v, c, ALL, ALL, a) for v in g.ys]
        self.c3b = [plan(g.to_c, ALL, c, ALL, v, b) for v in g.xs]
        self.mine = range(first, len(copies.made))

    def start(self):
        self.copies.start(self.p1)

    def step2(self):
        self.copies.arrived(self.p1)
        self.copies.start(self.p2a + self.p2b + self.c1)

    def step3(self):
        self.copies.arrived(self.p2a)
        self.copies.start(self.p3a)
        self.copies.arrived(self.p2b)
        self.copies.start(self.p3b + self.c2a + self.c2b)

    def step4(self):
        self.copies.arrived(self.p3a)
        self.copies.start(self.c3a)
        self.copies.arrived(self.p3b)
        self.copies.start(self.c3b)

    def finish(self):
        self.copies.arrived(self.c1 + self.c2a + self.c2b + self.c3a + self.c3b)

    def drain(self):
        self.copies.left(self.mine)


def rs_count(Y, Z, X):
    return 1 + 2 * ((X - 1) + (Y - 1)) + 2 * (Z - 1)


def rs_scratch(Y, Z, X, rows):
    a = (rows + 31) // 32 * 16
    b = max(rows - a, 16)
    return [
        pltpu.VMEM((Y, Z, X, rows, 128), BF16),
        pltpu.VMEM((Y - 1, Z, X, a, 128), BF16),
        pltpu.VMEM((X - 1, Z, a, 128), BF16),
        pltpu.VMEM((X - 1, Y, Z, b, 128), BF16),
        pltpu.VMEM((Y - 1, Z, b, 128), BF16),
        pltpu.VMEM((Z - 1, rows, 128), BF16),
    ]


def add_into(dst, srcs):
    lead = dst.shape[:-2]
    total = 1
    for n in lead:
        total *= n

    def body(i, _):
        idx, r = [], i
        for n in reversed(lead):
            idx.append(r % n)
            r = r // n
        idx = tuple(reversed(idx))
        acc = dst[idx].astype(F32)
        for s in srcs:
            acc = acc + s[idx].astype(F32)
        dst[idx] = acc.astype(BF16)
        return 0

    lax.fori_loop(0, total, body, 0)


class Scatter:
    def __init__(self, g, PB, recv, copies, lo, hi):
        mid = lo + (hi - lo + 31) // 32 * 16
        both, a, b = slice(lo, hi), slice(lo, mid), slice(mid, hi)
        self.g, self.PB, self.copies = g, PB, copies
        self.lo, self.both, self.a, self.b = lo, both, a, b
        self.r1, self.r2a, self.r3a, self.r2b, self.r3b, self.r4 = recv
        first = len(copies.made)
        y, c, z, x = g.me

        def plan(to, dst, *idx):
            return copies.plan(PB.at[idx], dst, to)

        self.p1 = [plan(g.to_c, self.r1, ALL, 1 - c, ALL, ALL, both)]
        self.p2a = [plan(to, self.r2a.at[k], g.ys[k], c, ALL, ALL, a) for k, to in enumerate(g.to_y)]
        self.p2b = [plan(to, self.r2b.at[k], ALL, c, ALL, g.xs[k], b) for k, to in enumerate(g.to_x if mid < hi else [])]
        self.p3a = [plan(to, self.r3a.at[k], y, c, ALL, g.xs[k], a) for k, to in enumerate(g.to_x)]
        self.p3b = [plan(to, self.r3b.at[k], g.ys[k], c, ALL, x, b) for k, to in enumerate(g.to_y if mid < hi else [])]
        ra, rb = slice(0, mid - lo), slice(mid - lo, hi - lo)
        self.p4a = [plan(to, self.r4.at[k, ra], y, c, g.zs[k], x, a) for k, to in enumerate(g.to_z)]
        self.p4b = [plan(to, self.r4.at[k, rb], y, c, g.zs[k], x, b) for k, to in enumerate(g.to_z if mid < hi else [])]
        self.mine = range(first, len(copies.made))

    def start(self):
        self.copies.start(self.p1)

    def step2(self):
        c = self.g.c
        self.copies.arrived(self.p1)
        add_into(self.PB.at[:, c, :, :, self.both], [self.r1])
        self.copies.start(self.p2a + self.p2b)

    def step3(self):
        y, c, z, x = self.g.me
        self.copies.arrived(self.p2a)
        add_into(self.PB.at[y, c, :, :, self.a], [self.r2a.at[k] for k in range(len(self.p2a))])
        self.copies.start(self.p3a)
        self.copies.arrived(self.p2b)
        if self.p2b:
            add_into(self.PB.at[:, c, :, x, self.b], [self.r2b.at[k] for k in range(len(self.p2b))])
        self.copies.start(self.p3b)

    def step4(self):
        y, c, z, x = self.g.me
        self.copies.arrived(self.p3a)
        add_into(self.PB.at[y, c, :, x, self.a], [self.r3a.at[k] for k in range(len(self.p3a))])
        self.copies.start(self.p4a)
        self.copies.arrived(self.p3b)
        if self.p3b:
            add_into(self.PB.at[y, c, :, x, self.b], [self.r3b.at[k] for k in range(len(self.p3b))])
        self.copies.start(self.p4b)

    def finish(self, place, rows, count):
        self.copies.arrived(self.p4a + self.p4b)
        unit = max(1, 16 // rows)
        for t in range(-(-count // unit)):
            r = slice(t * unit * rows, (t + 1) * unit * rows)
            own = slice(self.lo + r.start, self.lo + r.stop)
            acc = self.PB[self.g.me + (own,)].astype(F32)
            for k in range(len(self.p4a)):
                acc = acc + self.r4[k, r].astype(F32)
            for u in range(unit):
                if t * unit + u < count:
                    place(t * unit + u, acc[u * rows : (u + 1) * rows])

    def drain(self):
        self.copies.left(self.mine)


def dot(a, b):
    return lax.dot_general(a, b, (((1,), (0,)), ((), ())), preferred_element_type=F32)


def dot_nt(a, b):
    return lax.dot_general(a, b, (((1,), (1,)), ((), ())), preferred_element_type=F32)


def dot_tn(a, b):
    return lax.dot_general(a, b, (((0,), (0,)), ((), ())), preferred_element_type=F32)


def low(v):
    return v.astype(BF16)


def norm_stats(x):
    centre = x - jnp.mean(x, -1, keepdims=True)
    spread = jnp.mean(centre * centre, -1, keepdims=True)
    scale = lax.rsqrt(spread + EPSILON)
    return centre * scale, scale


def norm_back(grad, xhat, scale, gain):
    inner = grad * gain
    first = jnp.mean(inner, -1, keepdims=True)
    second = jnp.mean(inner * xhat, -1, keepdims=True)
    return scale * (inner - first - xhat * second)


def gelu_both(z):
    sq = z * z
    t = jnp.tanh(z * (0.7978845608028654 + (0.7978845608028654 * 0.044715) * sq))
    h = 0.5 * z
    value = h + h * t
    slope = 0.5 + 0.5 * t + h * (1.0 - t * t) * (
        0.7978845608028654 + (3.0 * 0.7978845608028654 * 0.044715) * sq
    )
    return value, slope


def iota(shape, dim):
    return lax.broadcasted_iota(jnp.int32, shape, dim)


def head_rows(dtype):
    lane = iota((1, 128), 1)
    return [(lane // HD == h).astype(F32).astype(dtype) for h in range(2)]


def head_stack(block, heads):
    return jnp.concatenate([block * h for h in heads], 0)


def own_word(scores, lane_word):
    split = scores.reshape(2, 8, W, 128)
    out = split[:, 0]
    for w in range(1, 8):
        out = jnp.where(lane_word == w, split[:, w], out)
    return out


def spread_words(compact, word_rows):
    return jnp.concatenate([compact[h] * word_rows[w] for h in range(2) for w in range(8)], 0)


def side_by_side(stacked, rows):
    return jnp.concatenate([stacked[h * rows : (h + 1) * rows] for h in range(2)], 1)


def place_own(own, raw, staged, extra, rows, blocks, total):
    staged[...] = raw[...].astype(F32)
    unit = max(1, 16 // rows)

    def block(j):
        if j < blocks:
            if rows == 1:
                return staged[j : j + 1, :]
            return staged[pl.ds(j, rows, stride=blocks), :]
        at = (j - blocks) * 128
        if at < extra.shape[1]:
            return extra[:, at : at + 128]
        return jnp.zeros((rows, 128), F32)

    for t in range(total // unit):
        tile = jnp.concatenate([block(j) for j in range(t * unit, (t + 1) * unit)], 0)
        own[t * unit * rows : (t + 1) * unit * rows, :] = low(tile)


def assemble(G, Wd, rows, total, wide, thin):
    unit = max(1, 16 // rows)
    Y, two, Z, X = G.shape[:4]
    some = Z * X * rows

    def body(i, _):
        at = pl.ds(pl.multiple_of(i * some, 16), some)
        for t in range(total // unit):
            tile = G[i // two, i % two, :, :, t * unit * rows : (t + 1) * unit * rows, :]
            tile = tile.reshape(Z * X, 16, 128).astype(F32)
            if rows < 8:
                wide[0 : Z * X * 16, :] = tile.reshape(Z * X * 16, 128)
            for u in range(unit):
                j = t * unit + u
                if j * 128 >= Wd.shape[1]:
                    continue
                if rows < 8:
                    for r in range(rows):
                        own = wide[pl.ds(u * rows + r, Z * X, stride=16), :]
                        thin[pl.ds(r, Z * X, stride=rows) if rows > 1 else ALL, :] = own
                    Wd[at, j * 128 : (j + 1) * 128] = low(thin[...])
                    continue
                Wd[at, j * 128 : (j + 1) * 128] = low(
                    tile[:, u * rows : (u + 1) * rows, :].reshape(some, 128)
                )
        return 0

    lax.fori_loop(0, Y * two, body, 0)


def pack_blocks(PB, at, blocks, rows, wide, thick):
    unit = max(1, 16 // rows)
    lead = PB.shape[:4]
    Y, two, Z, X = lead
    devices = Y * two * Z * X
    for t in range(len(blocks) // unit):
        row = (at + t * unit) * rows
        some = blocks[t * unit : (t + 1) * unit]
        if rows >= 8:
            parts = [b.reshape(devices, rows, 128) for b in some]
            tile = low(parts[0] if unit == 1 else jnp.concatenate(parts, 1))
            PB[:, :, :, :, row : row + unit * rows, :] = tile.reshape(lead + (unit * rows, 128))
            continue
        for k, b in enumerate(some):
            thick[0 : devices * rows, :] = b
            for r in range(rows):
                own = thick[pl.ds(r, devices, stride=rows) if rows > 1 else slice(0, devices), :]
                wide[pl.ds(k * rows + r, devices, stride=16), :] = own
        for i in range(Y * two):
            own = low(wide[i * Z * X * 16 : (i + 1) * Z * X * 16, :])
            PB[i // two, i % two, :, :, row : row + 16, :] = own.reshape(Z, X, 16, 128)


def columns(value):
    return [value[:, k : k + 128] for k in range(0, value.shape[1], 128)]


class Layout:
    def __init__(self, sizes):
        self.sizes = sizes
        Y, Z, X = sizes
        self.lead = (Y, 2, Z, X)
        self.devices = Y * 2 * Z * X
        self.rc = C // self.devices
        self.rw = D // self.devices
        self.bc = C_COLS // 128
        self.bw = D_COLS // 128

        def padded(n, rows):
            unit = max(1, 16 // rows)
            return max(-(-n // unit), 2) * unit

        self.jc = padded(self.bc + 3, self.rc)
        self.jw = padded(self.bw + 1, self.rw)
        self.j1 = padded(24, self.rc)
        self.j2 = self.jc - self.j1
        f = FF // 128
        self.word_cuts = (0, f, 2 * f, self.jw)
        self.word_order = (
            [4 * D // 128 + f + k for k in range(f)]
            + [4 * D // 128 + k for k in range(f)]
            + list(range(4 * D // 128))
            + [self.bw]
        )


def put(out, blocks, j, value):
    if value.shape[0] == 1:
        out[j : j + 1, :] = value
    else:
        out[pl.ds(j, value.shape[0], stride=blocks), :] = value


class Outs:
    def __init__(self, sem):
        self.sem, self.made = sem, []

    def start(self, src, dst):
        copy = pltpu.make_async_copy(src, dst, self.sem.at[len(self.made)])
        copy.start()
        self.made.append(copy)

    def wait(self):
        for copy in self.made:
            copy.wait()


def with_events(body, events):
    def step(i, carry):
        carry = body(i, carry)
        for at, acts in events.items():

            @pl.when(i == at)
            def _(acts=acts):
                for act in acts:
                    act()

        return carry

    return step


def gather_cuts(rows, parts):
    parts = max(1, min(parts, rows // 32))
    at = [rows * k // parts // 16 * 16 for k in range(parts)] + [rows]
    return [(at[k], at[k + 1]) for k in range(parts)]


def one_hot(condition):
    return condition.astype(F32).astype(BF16)


def slot_ints(codes, counts, langs, ints):
    wide = dot_tn(codes[...].astype(F32).astype(BF16), one_hot(iota((W, 128), 1) % W == iota((W, 128), 0)))
    wide = jnp.where(iota((LEN, 128), 0) % 8 == iota((LEN, 128), 1) // W, wide, 0.0)
    ints[0:16, :] = jnp.sum(wide.reshape(16, 8, 128), 1).astype(jnp.int32)
    group_row = iota((16, LEN), 0) == iota((16, LEN), 1) // 8
    by_slot = one_hot(iota((LEN, 128), 0) % 8 == iota((LEN, 128), 1) // W)
    by_word = one_hot(iota((LEN, 128), 0) % 8 == iota((LEN, 128), 1) % 8)
    count_rows = low(jnp.where(group_row, counts[...].astype(F32), 0.0))
    lang_rows = low(jnp.where(group_row, langs[...].astype(F32), 0.0))
    ints[16:32, :] = dot(lang_rows, by_slot).astype(jnp.int32)
    ints[32:48, :] = dot(count_rows, by_slot).astype(jnp.int32)
    ints[48:64, :] = dot(count_rows, by_word).astype(jnp.int32)


def mono(
    lay, stage,
    codes_in, counts_in, langs_in, length, cm_in, lookup_in, group_in, vec_in, wm_in, wvec_in, cot_in,
    y_out, cm_out, lookup_out, group_out, vec_out, wm_out, wvec_out,
    codes, counts, langs, cm, look, grp, vec, wm, wvec, cot,
    out_y, out_lookup, out_group, out_vec, out_wvec, exc, exw, ints,
    Gc, Gw, Wc, Wwt, PBw_own, out_cm, out_wm,
    xh1, n1s, qkvs, probs, os, xh2, n2s, acts, slopes, r2s, alphas, dr1s,
    Us, Ys, accq, acco, accu, accd, acct, sums, tsum,
    wide, thin_c, thin_w, thick,
    in_sem, out_sem, ag_send, ag_recv, rs_send, rs_recv, *recv,
):
    Y, Z, X = lay.sizes
    g = Grid(lay.sizes)
    PBw = PBw_own if lay.rw >= 16 else Gw
    PBc = Gc

    ins = [
        pltpu.make_async_copy(src, dst, in_sem.at[k])
        for k, (src, dst) in enumerate(
            (
                (cm_in, cm), (lookup_in, look), (group_in, grp), (vec_in, vec), (wm_in, wm),
                (wvec_in, wvec), (codes_in, codes), (counts_in, counts), (langs_in, langs), (cot_in, cot),
            )
        )
    ]
    for copy in ins:
        copy.start()
    ag = Copies(ag_send, ag_recv)
    gather_c = [Gather(g, Gc, ag, *cut) for cut in gather_cuts(Gc.shape[4], AG_PARTS_C)]
    gather_w = [Gather(g, Gw, ag, *cut) for cut in gather_cuts(Gw.shape[4], AG_PARTS_W)]
    gathers = gather_c + gather_w
    for copy in ins[0:4]:
        copy.wait()
    exc[...] = jnp.zeros(exc.shape, F32)
    exc[:, 0 : 2 * 128] = look[...].astype(F32)
    exc[:, 256 : 256 + LANGS] = grp[...].astype(F32)
    exc[:, 256 + LANGS : 256 + LANGS + 5] = vec[...].astype(F32)
    place_own(Gc.at[g.me], cm, out_cm, exc, lay.rc, lay.bc, lay.jc)
    g.greet()
    for part in gather_c:
        part.start()
    for copy in ins[4:6]:
        copy.wait()
    exw[...] = dot_tn(wvec[...], one_hot(iota((4, 128), 0) == iota((4, 128), 1)))
    place_own(Gw.at[g.me], wm, out_wm, exw, lay.rw, lay.bw, lay.jw)
    for part in gather_w:
        part.start()
    for copy in ins[6:9]:
        copy.wait()
    slot_ints(codes, counts, langs, ints)
    ca, cb = gather_c[0], gather_c[-1]
    wa, wb, wc = gather_w[0], gather_w[len(gather_w) // 2], gather_w[-1]
    for part in gather_c:
        part.step2()
    for part in gather_c:
        part.step3()
    wa.step2()
    for part in gather_c:
        part.step4()
    if wb is not wa:
        wb.step2()
    for part in gather_c:
        part.finish()
    assemble(Gc, Wc, lay.rc, lay.jc, wide, thin_c)

    eye = (iota((16, 128), 0) == iota((16, 128), 1)).astype(F32).astype(BF16)
    rows_c = dot_nt(eye, Wc[:, (lay.bc + 2) * 128 : (lay.bc + 3) * 128])
    gain1, shift1, gain2, shift2 = (rows_c[8 + k : 9 + k] for k in range(4))
    query = rows_c[12:13]
    table_low = low(jnp.where(iota((16, C), 0) < LANGS, rows_c, 0.0))
    lookup = slice(lay.bc * 128, (lay.bc + 2) * 128)
    AQ, AO = slice(0, 3 * C), slice(3 * C, 4 * C)
    AU, AD = slice(4 * C, 4 * C + CM), slice(4 * C + CM, 4 * C + 2 * CM)
    PK, PV = slice(4 * C + 2 * CM, 5 * C + 2 * CM), slice(5 * C + 2 * CM, 6 * C + 2 * CM)
    PR = slice(6 * C + 2 * CM, 6 * C + 2 * CM + D)

    lane = iota((1, 128), 1)
    lane_word = lane // W
    word_rows = [(lane_word == w).astype(F32).astype(BF16) for w in range(8)]
    heads = head_rows(BF16)
    head_of = iota((128, C), 0) % 32 // 8 == iota((128, C), 1) // HD
    pq_rows = jnp.where(head_of, query * 0.125, 0.0)
    score_map = dot_nt(low(pq_rows), Wc[:, PK])
    map_hi = low(score_map)
    map_lo = low(score_map - map_hi.astype(F32))
    key_row = iota((1, W, 1), 1)
    pool_own = iota((128, 128), 0) // W == iota((128, 128), 1) % 8
    pool_slot = iota((128, 128), 0) % W

    def onehots(i, groups):
        parts = []
        for k in range(groups):
            r = i * groups + k
            codes = ints[pl.ds(r, 1), :]
            langs = ints[pl.ds(16 + r, 1), :]
            a = (iota((VOCAB, 128), 0) == codes).astype(F32).astype(BF16)
            b = (iota((16, 128), 0) == langs).astype(F32).astype(BF16)
            parts.append(jnp.concatenate([a, b], 0))
        return parts

    GF = FWD_ROWS // 128

    def forward(i, _):
        rows = pl.ds(pl.multiple_of(i * FWD_ROWS, FWD_ROWS), FWD_ROWS)
        table = jnp.concatenate([Wc[:, lookup], table_low], 0)
        e = jnp.concatenate([dot_tn(h, table) for h in onehots(i, GF)], 0)
        xhat, scale1 = norm_stats(e)
        n1 = low(xhat * gain1 + shift1)
        xh1[rows, :] = low(xhat)
        n1s[rows, :] = n1
        qkv = low(dot(n1, Wc[:, AQ]))
        qkvs[rows, :] = qkv
        mixed = []
        for k in range(GF):
            visible = key_row < ints[pl.ds(32 + i * GF + k, 1), :].reshape(1, 1, 128)
            pair_out = []
            for p in range(2):
                q, kk, v = (
                    qkv[k * 128 : (k + 1) * 128, b * C + p * 128 : b * C + (p + 1) * 128]
                    for b in range(3)
                )
                s = own_word(dot_nt(head_stack(kk, heads), q), lane_word) * 0.125
                s = jnp.where(visible, s, NEGATIVE)
                s = jnp.exp(s - jnp.max(s, 1, keepdims=True))
                prob = s / jnp.sum(s, 1, keepdims=True)
                probs[i * GF + k, 2 * p : 2 * p + 2] = prob
                pair_out.append(dot_tn(spread_words(low(prob), word_rows), head_stack(v, heads)))
            mixed.append(jnp.concatenate(pair_out, 1))
        o = low(jnp.concatenate(mixed, 0))
        os[rows, :] = o
        r1 = e + dot(o, Wc[:, AO])
        xhat, scale2 = norm_stats(r1)
        n2 = low(xhat * gain2 + shift2)
        xh2[rows, :] = low(xhat)
        n2s[rows, :] = n2
        alphas[rows, 64:65] = scale1
        alphas[rows, 65:66] = scale2
        value, slope = gelu_both(dot(n2, Wc[:, AU]))
        act = low(value)
        acts[rows, :] = act
        slopes[rows, :] = low(slope)
        r2 = low(r1 + dot_nt(act, Wc[:, AD]))
        r2s[rows, :] = r2
        for k in range(GF):
            r = i * GF + k
            own = r2[k * 128 : (k + 1) * 128]
            s = dot_nt(own, map_hi) + dot_nt(own, map_lo)
            seen = pool_own & (pool_slot < ints[pl.ds(48 + r, 1), :])
            s = jnp.where(seen, s, NEGATIVE)
            s = jnp.where(seen, jnp.exp(s - jnp.max(s, 0, keepdims=True)), 0.0)
            alpha = s / jnp.sum(s, 0, keepdims=True)
            alphas[pl.ds(pl.multiple_of(r * 128, 128), 128), 0:32] = alpha[:, :32]
            u = dot_tn(low(alpha)[:, :32], own)
            for h in range(CH):
                Us[h, pl.ds(pl.multiple_of(r * 8, 8), 8), :] = u[8 * h : 8 * h + 8]
        return 0

    events = {
        0: [wc.step2, wa.step3],
        2: [wb.step3],
        3: [wa.step4],
        4: [wc.step3],
        5: [wb.step4],
        7: [wc.step4],
    }
    lax.fori_loop(0, LEN * W // FWD_ROWS, with_events(forward, events), 0)

    head_c = [iota((1, C), 1) // HD == h for h in range(CH)]
    pooled = sum(jnp.where(head_c[h], dot(low(Us[h]), Wc[:, PV]), 0.0) for h in range(CH))
    pooled_low = low(pooled)
    w_in = dot(pooled_low, Wc[:, PR])

    for part in gather_w:
        part.finish()
    if lay.rw >= 16:

        def wcols(lo, hi):
            return jnp.concatenate(
                [
                    Gw[:, :, :, :, j * lay.rw : (j + 1) * lay.rw, :].reshape(D, 128)
                    for j in range(lo // 128, hi // 128)
                ],
                1,
            )

    else:
        assemble(Gw, Wwt, lay.rw, lay.jw, wide, thin_w)

        def wcols(lo, hi):
            return Wwt[:, lo:hi]

    rows_w = dot_nt(eye, wcols(D_COLS, D_COLS + 128))
    f1, c1, f2, c2 = (rows_w[k : k + 1] for k in range(4))
    BQ, BO, BU, BD = (0, 3 * D), (3 * D, 4 * D), (4 * D, 4 * D + FF), (4 * D + FF, D_COLS)
    NP = H // 2

    xhat1, sc1 = norm_stats(w_in)
    m1 = low(xhat1 * f1 + c1)
    qkv = low(dot(m1, wcols(*BQ)))
    key = iota((1, 128, 1), 1)
    seen_word = (key <= iota((1, 1, 128), 2)) & (key < length[0])
    pw, kst, qst, vst, mix = [], [], [], [], []
    for p in range(NP):
        q, kk, v = (qkv[:, b * D + p * 128 : b * D + (p + 1) * 128] for b in range(3))
        kst.append(head_stack(kk, heads))
        qst.append(head_stack(q, heads))
        vst.append(head_stack(v, heads))
        s = dot_nt(kst[p], q).reshape(2, 128, 128) * 0.125
        s = jnp.where(seen_word, s, NEGATIVE)
        s = jnp.exp(s - jnp.max(s, 1, keepdims=True))
        pw.append(s / jnp.sum(s, 1, keepdims=True))
        mix.append(dot_tn(low(pw[p]).reshape(256, 128), vst[p]))
    ow = low(jnp.concatenate(mix, 1))
    x = w_in + dot(ow, wcols(*BO))
    xhat2, sc2 = norm_stats(x)
    m2 = low(xhat2 * f2 + c2)
    value, slope = gelu_both(dot(m2, wcols(*BU)))
    aw = low(value)
    out_y[...] = low(x + dot_nt(aw, wcols(*BD)))
    outs = Outs(out_sem)
    outs.start(out_y, y_out)

    ins[9].wait()
    gy = cot[...]
    dy = gy.astype(F32)
    rw = lay.rw
    unit_w = max(1, 16 // rw)
    waiting = {}

    def put_w(at, blocks):
        waiting.update({at + k: b for k, b in enumerate(blocks)})
        for first in range(0, lay.jw, unit_w):
            ready = range(first, first + unit_w)
            if all(j in waiting for j in ready):
                pack_blocks(PBw, first, [waiting.pop(j) for j in ready], rw, wide, thick)

    cuts = [c * rw for c in lay.word_cuts]
    nrecv = len(recv) // 5
    rs = Copies(rs_send, rs_recv)
    scatters = [
        Scatter(g, PBw, recv[6 * k : 6 * k + 6], rs, cuts[k], cuts[k + 1]) for k in range(3)
    ]
    cut1 = lay.j1 * lay.rc
    scatters.append(Scatter(g, PBc, recv[18:24], rs, 0, cut1))
    scatters.append(Scatter(g, PBc, recv[24:30], rs, cut1, PBc.shape[4]))
    w1, w2, w3, c1_, c2_ = scatters
    if lay.rw < 16:
        for part in gather_w:
            part.drain()
    for k in range(0, FF, 512):
        put_w(k // 128, columns(dot_tn(gy, aw[:, k : k + 512])))
    w1.start()
    gzw = low(slope * dot(gy, wcols(*BD)))
    for k in range(0, FF, 512):
        put_w((FF + k) // 128, columns(dot_tn(m2, gzw[:, k : k + 512])))
    w2.start()
    w1.step2()
    dm2 = dot_nt(gzw, wcols(*BU))
    gf2 = jnp.sum(dm2 * xhat2, 0, keepdims=True)
    gc2 = jnp.sum(dm2, 0, keepdims=True)
    dx = dy + norm_back(dm2, xhat2, sc2, f2)
    gx = low(dx)
    put_w((2 * FF + BO[0]) // 128, columns(dot_tn(ow, gx)))
    gow = low(dot_nt(gx, wcols(*BO)))
    w2.step2()
    gq, gk, gv = [], [], []
    for p in range(NP):
        go = gow[:, p * 128 : (p + 1) * 128]
        dp = dot_nt(vst[p], go).reshape(2, 128, 128)
        inner = jnp.sum(pw[p] * dp, 1, keepdims=True)
        gs = low(pw[p] * (dp - inner)).reshape(256, 128)
        gq.append(dot_tn(gs, kst[p]) * 0.125)
        gk.append(dot(side_by_side(gs, 128), qst[p]) * 0.125)
        gv.append(dot(side_by_side(low(pw[p]).reshape(256, 128), 128), head_stack(go, heads)))
    tg = low(jnp.concatenate(gq + gk + gv, 1))
    for k in range(0, 3 * D, 512):
        put_w((2 * FF + k) // 128, columns(dot_tn(m1, tg[:, k : k + 512])))
    dm1 = dot_nt(tg, wcols(*BQ))
    gf1 = jnp.sum(dm1 * xhat1, 0, keepdims=True)
    gc1 = jnp.sum(dm1, 0, keepdims=True)
    dw = dx + norm_back(dm1, xhat1, sc1, f1)
    vec_rows = low(jnp.concatenate([gf1, gc1, gf2, gc2, jnp.zeros((12, D), F32)], 0))
    zero_w = [jnp.zeros((D, 128), F32)] * (lay.jw - lay.bw - 1)
    put_w(lay.bw, [dot_tn(vec_rows, eye)] + zero_w)
    w3.start()

    for part in gather_c:
        part.drain()
    gw = low(dw)
    dpool = dot_nt(gw, Wc[:, PR])
    dp4 = jnp.concatenate([low(jnp.where(head_c[h], dpool, 0.0)) for h in range(CH)], 0)
    Ys[...] = dot_nt(dp4, Wc[:, PV]).reshape(CH, LEN, C)
    for ref in (accq, acco, accu, accd, acct, sums, tsum):
        ref[...] = jnp.zeros(ref.shape, F32)

    map32 = map_hi[:32]
    GB = BWD_ROWS // 128

    def back_ffn(i, _):
        rows = pl.ds(pl.multiple_of(i * BWD_ROWS, BWD_ROWS), BWD_ROWS)
        parts = []
        for k in range(GB):
            r = i * GB + k
            own = r2s[pl.ds(pl.multiple_of(r * 128, 128), 128), :]
            alpha = alphas[pl.ds(pl.multiple_of(r * 128, 128), 128), 0:32]
            yg = low(
                jnp.concatenate(
                    [Ys[h, pl.ds(pl.multiple_of(r * 8, 8), 8), :] for h in range(CH)], 0
                )
            )
            da = dot_nt(own, yg)
            dr = low(alpha * (da - jnp.sum(alpha * da, 0, keepdims=True)))
            tsum[...] += dot_tn(dr, own)
            parts.append(dot(low(alpha), yg) + dot(dr, map32))
        dr2 = jnp.concatenate(parts, 0)
        g2 = low(dr2)
        accd[...] += dot_tn(g2, acts[rows, :])
        gz = low(slopes[rows, :].astype(F32) * dot(g2, Wc[:, AD]))
        accu[...] += dot_tn(n2s[rows, :], gz)
        dn = dot_nt(gz, Wc[:, AU])
        xhat = xh2[rows, :].astype(F32)
        sums[2:3, :] += jnp.sum(dn * xhat, 0, keepdims=True)
        sums[3:4, :] += jnp.sum(dn, 0, keepdims=True)
        dr1s[rows, :] = dr2 + norm_back(dn, xhat, alphas[rows, 65:66], gain2)
        return 0

    def place_w(j, value):
        j = lay.word_order[j]
        if j < lay.bw:
            put(out_wm, lay.bw, j, value)
        else:
            pick = (iota((8, 128), 0) == iota((8, 128), 1)).astype(F32)
            out_wvec[...] = lax.dot_general(
                pick, value, (((1,), (1,)), ((), ())),
                precision=lax.Precision.HIGHEST, preferred_element_type=F32,
            )[0:4]

    def place_1(j, value):
        put(out_cm, lay.bc, 8 + j, value)

    def place_2(j, value):
        if j < 8:
            put(out_cm, lay.bc, j, value)
        elif j < 10:
            out_lookup[:, (j - 8) * 128 : (j - 7) * 128] = value
        else:
            out_group[...] = value[:, 0:LANGS]
            out_vec[...] = value[:, LANGS : LANGS + 5]

    def fin_w(k):
        first = lay.word_cuts[k]
        count = min(lay.word_cuts[k + 1], lay.bw + 1) - first
        return lambda: scatters[k].finish(lambda j, v: place_w(first + j, v), rw, count)

    nb = LEN * W // BWD_ROWS
    events = {
        0: [w3.step2],
        1: [w1.step3],
        3: [w2.step3],
        4: [w1.step4],
        6: [w3.step3],
        7: [w2.step4],
    }
    lax.fori_loop(0, nb, with_events(back_ffn, events), 0)

    grad_pr = dot_tn(pooled_low, gw)
    grad_pv = dot_tn(low(Us[...]).reshape(CH * LEN, C), dp4)
    t_low = low(tsum[...])
    grad_pk = dot_tn(t_low, low(pq_rows[:32]))
    rc = lay.rc
    pad1 = [jnp.zeros((C, 128), F32)] * (lay.j1 - 24)
    pack_blocks(
        PBc,
        0,
        columns(accu[...]) + columns(accd[...]) + columns(grad_pk) + columns(grad_pv)
        + columns(grad_pr) + pad1,
        rc,
        wide,
        thick,
    )
    c1_.start()
    gpq = dot(t_low, Wc[:, PK]) * 0.125
    gpq = jnp.sum(
        jnp.where(iota((32, C), 0) // 8 == iota((32, C), 1) // HD, gpq, 0.0), 0, keepdims=True
    )

    def back_attention(i, _):
        rows = pl.ds(pl.multiple_of(i * BWD_ROWS, BWD_ROWS), BWD_ROWS)
        dr1 = dr1s[rows, :]
        g1 = low(dr1)
        acco[...] += dot_tn(os[rows, :], g1)
        go = low(dot_nt(g1, Wc[:, AO]))
        qkv = qkvs[rows, :]
        grads = [[], [], []]
        for k in range(GB):
            part = [[], [], []]
            for p in range(2):
                at = slice(k * 128, (k + 1) * 128)
                q, kk, v = (
                    qkv[at, b * C + p * 128 : b * C + (p + 1) * 128] for b in range(3)
                )
                gop = go[at, p * 128 : (p + 1) * 128]
                prob = probs[i * GB + k, 2 * p : 2 * p + 2]
                dp = own_word(dot_nt(head_stack(v, heads), gop), lane_word)
                gs = low(prob * (dp - jnp.sum(prob * dp, 1, keepdims=True)))
                gs = spread_words(gs, word_rows)
                pb = spread_words(low(prob), word_rows)
                part[0].append(dot_tn(gs, head_stack(kk, heads)) * 0.125)
                part[1].append(dot(side_by_side(gs, 128), head_stack(q, heads)) * 0.125)
                part[2].append(dot(side_by_side(pb, 128), head_stack(gop, heads)))
            for b in range(3):
                grads[b].append(jnp.concatenate(part[b], 1))
        tg = low(jnp.concatenate([jnp.concatenate(b, 0) for b in grads], 1))
        accq[...] += dot_tn(n1s[rows, :], tg)
        dn = dot_nt(tg, Wc[:, AQ])
        xhat = xh1[rows, :].astype(F32)
        sums[0:1, :] += jnp.sum(dn * xhat, 0, keepdims=True)
        sums[1:2, :] += jnp.sum(dn, 0, keepdims=True)
        ge = low(dr1 + norm_back(dn, xhat, alphas[rows, 64:65], gain1))
        for k, h in enumerate(onehots(i, GB)):
            acct[...] += dot(h, ge[k * 128 : (k + 1) * 128])
        return 0

    events = {
        1: [c1_.step2, fin_w(0)],
        2: [w3.step4],
        4: [c1_.step3, fin_w(1)],
        6: [c1_.step4],
    }
    lax.fori_loop(0, nb, with_events(back_attention, events), 0)

    small = low(jnp.concatenate([acct[VOCAB : VOCAB + 8], sums[0:4], gpq, jnp.zeros((3, C), F32)], 0))
    pad2 = [jnp.zeros((C, 128), F32)] * (lay.j2 - 11)
    pack_blocks(
        PBc,
        lay.j1,
        columns(accq[...]) + columns(acco[...]) + columns(acct[0:VOCAB, :])
        + [dot_tn(small, eye)] + pad2,
        rc,
        wide,
        thick,
    )
    c2_.start()
    fin_w(2)()
    outs.start(out_wm, wm_out)
    outs.start(out_wvec, wvec_out)
    c2_.step2()
    c1_.finish(place_1, rc, 24)
    c2_.step3()
    c2_.step4()
    c2_.finish(place_2, rc, 11)
    outs.start(out_cm, cm_out)
    outs.start(out_lookup, lookup_out)
    outs.start(out_group, group_out)
    outs.start(out_vec, vec_out)
    for part in (gather_w if lay.rw >= 16 else []) + scatters:
        part.drain()
    outs.wait()


def hand_over(*refs):
    n = 7
    ins, outs, held, sems = refs[:n], refs[n : 2 * n], refs[2 * n : 3 * n], refs[-1]
    first = [pltpu.make_async_copy(ins[k], held[k], sems.at[k]) for k in range(n)]
    then = [pltpu.make_async_copy(held[k], outs[k], sems.at[n + k]) for k in range(n)]
    for copy in first:
        copy.start()
    for k in range(n):
        first[k].wait()
        then[k].start()
    for copy in then:
        copy.wait()


def shards(
    sizes,
    char_codes,
    char_counts,
    word_groups,
    valid_words,
    char_matrix,
    char_lookup,
    group_lookup,
    char_vectors,
    word_matrix,
    word_vectors,
    cotangent,
):
    lay = Layout(sizes)
    Y, Z, X = sizes
    rows = LEN * W
    rows_c, rows_w = lay.jc * lay.rc, lay.jw * lay.rw
    rows_1, rows_2 = lay.j1 * lay.rc, lay.j2 * lay.rc
    word_parts = [(b - a) * lay.rw for a, b in zip(lay.word_cuts, lay.word_cuts[1:])]
    nag = ag_count(Y, Z, X) * (AG_PARTS_C + AG_PARTS_W)
    nrs = rs_count(Y, Z, X) * 5
    dma = pltpu.SemaphoreType.DMA

    def vm(shape, dtype):
        return pltpu.VMEM(shape, dtype)

    def like(a):
        return pltpu.VMEM(a.shape, a.dtype)

    ins = (
        char_codes[0].T,
        char_counts,
        word_groups,
        valid_words,
        char_matrix,
        char_lookup,
        group_lookup,
        char_vectors,
        word_matrix,
        word_vectors.T,
        cotangent[0],
    )
    outs = [
        jax.ShapeDtypeStruct((LEN, D), BF16),
        jax.ShapeDtypeStruct(char_matrix.shape, F32),
        jax.ShapeDtypeStruct(char_lookup.shape, F32),
        jax.ShapeDtypeStruct(group_lookup.shape, F32),
        jax.ShapeDtypeStruct(char_vectors.shape, F32),
        jax.ShapeDtypeStruct(word_matrix.shape, F32),
        jax.ShapeDtypeStruct(word_vectors.shape[::-1], F32),
    ]
    scratch = [like(a) for k, a in enumerate(ins) if k != 3]
    scratch += [like(outs[k]) for k in (0, 2, 3, 4, 6)]
    scratch += [
        vm((lay.rc, 3 * 128), F32),
        vm((lay.rw, 128), F32),
        vm((64, 128), jnp.int32),
        vm(lay.lead + (rows_c, 128), BF16),
        vm(lay.lead + (rows_w, 128), BF16),
        vm((C, (lay.bc + 3) * 128), BF16),
        vm((D, (lay.bw + 1) * 128) if lay.rw < 16 else (16, 128), BF16),
        vm(lay.lead + (rows_w, 128) if lay.rw >= 16 else (16, 128), BF16),
        like(outs[1]),
        like(outs[5]),
        vm((rows, C), BF16),
        vm((rows, C), BF16),
        vm((rows, 3 * C), BF16),
        vm((16, CH, W, 128), F32),
        vm((rows, C), BF16),
        vm((rows, C), BF16),
        vm((rows, C), BF16),
        vm((rows, CM), BF16),
        vm((rows, CM), BF16),
        vm((rows, C), BF16),
        vm((rows, 128), F32),
        vm((rows, C), F32),
        vm((CH, LEN, C), F32),
        vm((CH, LEN, C), F32),
        vm((C, 3 * C), F32),
        vm((C, C), F32),
        vm((C, CM), F32),
        vm((C, CM), F32),
        vm((VOCAB + 16, C), F32),
        vm((8, C), F32),
        vm((32, C), F32),
        vm((lay.devices * 16 if lay.rc < 8 else 8, 128), F32),
        vm((Z * X * lay.rc, 128), F32),
        vm((Z * X * lay.rw, 128), F32),
        vm((D if lay.rc < 8 else 8, 128), F32),
        dma((10,)),
        dma((7,)),
        dma((nag,)),
        dma((nag,)),
        dma((nrs,)),
        dma((nrs,)),
    ]
    for n in word_parts + [rows_1, rows_2]:
        scratch += rs_scratch(Y, Z, X, n)
    anywhere = pl.BlockSpec(memory_space=pl.ANY)
    in_specs = [anywhere] * 11
    in_specs[3] = pl.BlockSpec(memory_space=pltpu.SMEM)
    got = pl.pallas_call(
        functools.partial(mono, lay, STAGE),
        out_shape=outs,
        in_specs=in_specs,
        out_specs=[anywhere] * 7,
        scratch_shapes=scratch,
        compiler_params=pltpu.CompilerParams(
            collective_id=0, has_side_effects=True, vmem_limit_bytes=VMEM_LIMIT
        ),
        name="layer",
    )(*ins)
    got = pl.pallas_call(
        hand_over,
        out_shape=outs,
        in_specs=[anywhere] * 7,
        out_specs=[anywhere] * 7,
        scratch_shapes=[like(a) for a in outs] + [dma((14,))],
        name="hand_over",
    )(*got)
    return (got[0][None],) + tuple(got[1:6]) + (got[6].T,)


def solution(mesh):
    dp, fsdp = mesh.shape["dp"], mesh.shape["fsdp"]
    Y = dp // 2
    X = Y if fsdp % Y == 0 else 1
    sizes = (Y, fsdp // X, X)
    placed = (
        P(("dp", "fsdp"), None, None),
        P(("dp", "fsdp"), None),
        P(("dp", "fsdp"), None),
        P(("dp", "fsdp")),
        P(("dp", "fsdp"), None),
        P(("dp", "fsdp"), None),
        P(("dp", "fsdp"), None),
        P(("dp", "fsdp"), None),
        P(("dp", "fsdp"), None),
        P(("dp", "fsdp"), None),
        P(("dp", "fsdp"), None, None),
    )
    return jax.shard_map(
        functools.partial(shards, sizes),
        mesh=mesh,
        in_specs=placed,
        out_specs=(
            P(("dp", "fsdp"), None, None),
            P(("dp", "fsdp"), None),
            P(("dp", "fsdp"), None),
            P(("dp", "fsdp"), None),
            P(("dp", "fsdp"), None),
            P(("dp", "fsdp"), None),
            P(("dp", "fsdp"), None),
        ),
        check_vma=False,
    )
```

```python
import functools

import jax
import jax.numpy as jnp
from jax import lax
from jax.experimental import pallas as pl
from jax.experimental.pallas import tpu as pltpu
from jax.sharding import PartitionSpec as P

C = 256
HD = 64
CH = 4
CM = 1024
D = 512
H = 8
FF = 2048
W = 16
VOCAB = 256
LANGS = 8
LEN = 128
C_COLS = 6 * C + 2 * CM + D
D_COLS = 4 * D + 2 * FF
EPSILON = 1e-05
NEGATIVE = -1000000000.0
F32 = jnp.float32
BF16 = jnp.bfloat16
FWD_ROWS = 512
BWD_ROWS = 512
FFN_ROWS = 512
VMEM_LIMIT = 63 << 20
STAGE = 0


MESH = pl.DeviceIdType.MESH
ALL = slice(None)


class Grid:
    def __init__(self, sizes):
        self.Y, self.Z, self.X = sizes
        dp, fs = lax.axis_index("dp"), lax.axis_index("fsdp")
        self.y, self.c = dp // 2, dp % 2
        self.z, self.x = fs // self.X, fs % self.X
        self.me = (self.y, self.c, self.z, self.x)
        self.ys = [(self.y + k) % self.Y for k in range(1, self.Y)]
        self.zs = [(self.z + k) % self.Z for k in range(1, self.Z)]
        self.xs = [(self.x + k) % self.X for k in range(1, self.X)]
        self.to_y = [self.at(y=y) for y in self.ys]
        self.to_z = [self.at(z=z) for z in self.zs]
        self.to_x = [self.at(x=x) for x in self.xs]
        self.to_c = self.at(c=1 - self.c)
        self.to = {"y": self.to_y, "z": self.to_z, "x": self.to_x}
        self.src = {
            "y": [(self.y + self.Y - k) % self.Y for k in range(1, self.Y)],
            "z": [(self.z + self.Z - k) % self.Z for k in range(1, self.Z)],
            "x": [(self.x + self.X - k) % self.X for k in range(1, self.X)],
        }
        self.off = {"y": self.ys, "z": self.zs, "x": self.xs}

    def at(self, y=None, c=None, z=None, x=None):
        y = self.y if y is None else y
        c = self.c if c is None else c
        z = self.z if z is None else z
        x = self.x if x is None else x
        return (y * 2 + c, z * self.X + x)

    def greet(self):
        barrier = pltpu.get_barrier_semaphore()
        self.partners = [self.to_c] + self.to_y + self.to_z + self.to_x
        for p in self.partners:
            pl.semaphore_signal(barrier, inc=1, device_id=p, device_id_type=MESH)

    def met(self):
        pl.semaphore_wait(pltpu.get_barrier_semaphore(), len(self.partners))


class Copies:
    def __init__(self, send, recv):
        self.send, self.recv, self.made = send, recv, []

    def plan(self, src, dst, to):
        self.made.append((src, dst, to))
        return len(self.made) - 1

    def make(self, i):
        src, dst, to = self.made[i]
        return pltpu.make_async_remote_copy(
            src_ref=src,
            dst_ref=dst,
            send_sem=self.send.at[i],
            recv_sem=self.recv.at[i],
            device_id=to,
            device_id_type=MESH,
        )

    def start(self, which):
        for i in which:
            self.make(i).start()

    def arrived(self, which):
        for i in which:
            self.make(i).wait_recv()

    def left(self, which):
        for i in which:
            self.make(i).wait_send()


def ag_count(Y, Z, X):
    n = max(Z - 1, X - 1, Y - 1)
    return 6 * n + 1 + 2 * n * n


class Gather:
    def __init__(self, g, G, copies, lo, hi, order):
        self.copies = copies
        first = len(copies.made)
        one, two, three = order
        rows = slice(lo, hi)

        def slot(**at):
            v = {"y": g.y, "z": g.z, "x": g.x, **at}
            return (v["y"], g.c, v["z"], v["x"], rows)

        def plan(to, **at):
            return copies.plan(G.at[slot(**at)], G.at[slot(**at)], to)

        self.first = [plan(to) for to in g.to[one]]
        self.own2 = [plan(to) for to in g.to[two]]
        self.own3 = [plan(to, **{two: ALL}) for to in g.to[three]]
        self.rest2 = [[plan(to, **{one: v}) for to in g.to[two]] for v in g.src[one]]
        self.rest3 = [[plan(to, **{one: v, two: ALL}) for to in g.to[three]] for v in g.src[one]]
        self.core1 = [plan(g.to_c)]
        self.core2 = [plan(g.to_c, **{two: w}) for w in g.src[two]]
        self.core4 = [[plan(g.to_c, **{one: v, two: ALL})] for v in g.src[one]]
        self.core5 = [plan(g.to_c, **{one: ALL, two: ALL, three: u}) for u in g.src[three]]
        self.mine = range(first, len(copies.made))

    def step1(self):
        self.copies.start(self.first + self.own2 + self.core1)

    def step2(self):
        self.copies.arrived(self.own2)
        self.copies.start(self.own3 + self.core2)

    def step3(self):
        for k, which in enumerate(self.rest2):
            self.copies.arrived(self.first[k : k + 1])
            self.copies.start(which)

    def step4(self):
        for k, which in enumerate(self.rest3):
            self.copies.arrived(self.rest2[k])
            self.copies.start(which + self.core4[k])

    def step5(self):
        self.copies.arrived(self.own3)
        for which in self.rest3:
            self.copies.arrived(which)
        self.copies.start(self.core5)

    def finish(self):
        self.copies.arrived(self.core1 + self.core2 + self.core5)
        for which in self.core4:
            self.copies.arrived(which)

    def drain(self):
        self.copies.left(self.mine)


def rs_count(Y, Z, X):
    return 1 + (Z - 1) + (X - 1) + (Y - 1)


def rs_scratch(sizes, rows, order):
    n = dict(zip("yzx", sizes))
    left = dict(n)
    shapes = [pltpu.VMEM(sizes + (rows, 128), BF16)]
    for axis in order:
        left[axis] = 1
        shapes.append(pltpu.VMEM((n[axis] - 1, left["y"], left["z"], left["x"], rows, 128), BF16))
    return shapes


def add_into(dst, srcs):
    lead = dst.shape[:-2]
    total = 1
    for n in lead:
        total *= n

    def body(i, _):
        idx, r = [], i
        for n in reversed(lead):
            idx.append(r % n)
            r = r // n
        idx = tuple(reversed(idx))
        acc = dst[idx].astype(F32)
        for s in srcs:
            acc = acc + s[idx].astype(F32)
        dst[idx] = acc.astype(BF16)
        return 0

    lax.fori_loop(0, total, body, 0)


class Scatter:
    def __init__(self, g, PB, recv, copies, lo, hi, order):
        self.g, self.PB, self.copies, self.recv = g, PB, copies, recv
        self.lo, self.hi = lo, hi
        first = len(copies.made)
        rows = slice(lo, hi)
        me = {"y": g.y, "z": g.z, "x": g.x}
        have = {"y": ALL, "z": ALL, "x": ALL}

        def slot(c, **at):
            v = {**have, **at}
            return (v["y"], c, v["z"], v["x"], rows)

        self.hops = [[copies.plan(PB.at[slot(1 - g.c)], recv[0], g.to_c)]]
        self.sums = [PB.at[slot(g.c)]]
        for n, axis in enumerate(order):
            self.hops.append(
                [
                    copies.plan(PB.at[slot(g.c, **{axis: pl.ds(v, 1)})], recv[n + 1].at[k], to)
                    for k, (v, to) in enumerate(zip(g.off[axis], g.to[axis]))
                ]
            )
            have[axis] = pl.ds(me[axis], 1)
            self.sums.append(PB.at[slot(g.c)])
        self.mine = range(first, len(copies.made))

    def add(self, n):
        self.copies.arrived(self.hops[n])
        if n == 0:
            add_into(self.sums[0], [self.recv[0]])
        else:
            add_into(self.sums[n], [self.recv[n].at[k] for k in range(len(self.hops[n]))])

    def step1(self):
        self.copies.start(self.hops[0])

    def step2(self):
        self.add(0)
        self.copies.start(self.hops[1])

    def step3(self):
        self.add(1)
        self.copies.start(self.hops[2])

    def step4(self):
        self.add(2)
        self.copies.start(self.hops[3])

    def finish(self, place, rows, base, count):
        self.copies.arrived(self.hops[3])
        size = max(rows, 16)
        for row in range(self.lo, self.hi, size):
            r = slice(row - self.lo, row - self.lo + size)
            acc = self.PB[self.g.me + (slice(row, row + size),)].astype(F32)
            for k in range(len(self.hops[3])):
                acc = acc + self.recv[3][k, 0, 0, 0, r].astype(F32)
            for u in range(size // rows):
                j = (row - base) // rows + u
                if j < count:
                    place(j, acc[u * rows : (u + 1) * rows])

    def drain(self):
        self.copies.left(self.mine)


class Pair:
    def __init__(self, parts):
        self.parts = parts

    def all(self, name, *args):
        for part in self.parts:
            getattr(part, name)(*args)

    def step1(self):
        self.all("step1")

    def step2(self):
        self.all("step2")

    def step3(self):
        self.all("step3")

    def step4(self):
        self.all("step4")

    def step5(self):
        self.all("step5")

    def finish(self, *args):
        self.all("finish", *args)

    def drain(self):
        self.all("drain")


def halves(lo, hi):
    mid = lo + (hi - lo + 31) // 32 * 16
    return [(lo, mid), (mid, hi)] if mid < hi else [(lo, hi)]


def gather_pair(g, G, copies, lo, hi):
    orders = ("zxy", "zyx")
    return Pair([Gather(g, G, copies, *cut, o) for cut, o in zip(halves(lo, hi), orders)])


SUM_ORDERS = ("yxz", "xyz")


def scatter_pair(g, PB, recv, copies, lo, hi):
    parts = []
    for cut, o in zip(halves(lo, hi), SUM_ORDERS):
        parts.append(Scatter(g, PB, recv[:4], copies, *cut, o))
        del recv[:4]
    return Pair(parts)


def scatter_pair_scratch(sizes, lo, hi):
    out = []
    for (a, b), o in zip(halves(lo, hi), SUM_ORDERS):
        out += rs_scratch(sizes, b - a, o)
    return out


def dot(a, b):
    return lax.dot_general(a, b, (((1,), (0,)), ((), ())), preferred_element_type=F32)


def dot_nt(a, b):
    return lax.dot_general(a, b, (((1,), (1,)), ((), ())), preferred_element_type=F32)


def dot_tn(a, b):
    return lax.dot_general(a, b, (((0,), (0,)), ((), ())), preferred_element_type=F32)


def low(v):
    return v.astype(BF16)


def norm_stats(x):
    centre = x - jnp.mean(x, -1, keepdims=True)
    spread = jnp.mean(centre * centre, -1, keepdims=True)
    scale = lax.rsqrt(spread + EPSILON)
    return centre * scale, scale


def norm_back(grad, xhat, scale, gain):
    inner = grad * gain
    first = jnp.mean(inner, -1, keepdims=True)
    second = jnp.mean(inner * xhat, -1, keepdims=True)
    return scale * (inner - first - xhat * second)


def gelu_both(z):
    sq = z * z
    t = jnp.tanh(z * (0.7978845608028654 + (0.7978845608028654 * 0.044715) * sq))
    h = 0.5 * z
    value = h + h * t
    slope = 0.5 + 0.5 * t + h * (1.0 - t * t) * (
        0.7978845608028654 + (3.0 * 0.7978845608028654 * 0.044715) * sq
    )
    return value, slope


def iota(shape, dim):
    return lax.broadcasted_iota(jnp.int32, shape, dim)


def head_rows(dtype):
    lane = iota((1, 128), 1)
    return [(lane // HD == h).astype(F32).astype(dtype) for h in range(2)]


def head_stack(block, heads):
    return jnp.concatenate([block * h for h in heads], 0)


def own_word(scores, lane_word):
    split = scores.reshape(2, 8, W, 128)
    out = split[:, 0]
    for w in range(1, 8):
        out = jnp.where(lane_word == w, split[:, w], out)
    return out


def spread_words(compact, word_rows):
    return jnp.concatenate([compact[h] * word_rows[w] for h in range(2) for w in range(8)], 0)


def side_by_side(stacked, rows):
    return jnp.concatenate([stacked[h * rows : (h + 1) * rows] for h in range(2)], 1)


def place_own(own, raw, staged, extra, rows, blocks, order):
    staged[...] = raw[...].astype(F32)
    unit = max(1, 16 // rows)

    def block(j):
        if j is None:
            return jnp.zeros((rows, 128), F32)
        if j < blocks:
            if rows == 1:
                return staged[j : j + 1, :]
            return staged[pl.ds(j, rows, stride=blocks), :]
        at = (j - blocks) * 128
        return extra[:, at : at + 128]

    for t in range(len(order) // unit):
        tile = jnp.concatenate([block(j) for j in order[t * unit : (t + 1) * unit]], 0)
        own[t * unit * rows : (t + 1) * unit * rows, :] = low(tile)


def assemble(G, Wd, rows, order, wide, thin):
    unit = max(1, 16 // rows)
    Y, two, Z, X = G.shape[:4]
    some = Z * X * rows

    def body(i, _):
        at = pl.ds(pl.multiple_of(i * some, 16), some)
        for t in range(len(order) // unit):
            tile = G[i // two, i % two, :, :, t * unit * rows : (t + 1) * unit * rows, :]
            tile = tile.reshape(Z * X, 16, 128).astype(F32)
            if rows < 8:
                wide[0 : Z * X * 16, :] = tile.reshape(Z * X * 16, 128)
            for u in range(unit):
                j = order[t * unit + u]
                if j is None:
                    continue
                if rows < 8:
                    for r in range(rows):
                        own = wide[pl.ds(u * rows + r, Z * X, stride=16), :]
                        thin[pl.ds(r, Z * X, stride=rows) if rows > 1 else ALL, :] = own
                    Wd[at, j * 128 : (j + 1) * 128] = low(thin[...])
                    continue
                Wd[at, j * 128 : (j + 1) * 128] = low(
                    tile[:, u * rows : (u + 1) * rows, :].reshape(some, 128)
                )
        return 0

    lax.fori_loop(0, Y * two, body, 0)


def pack_blocks(PB, at, blocks, rows, wide, thick):
    unit = max(1, 16 // rows)
    lead = PB.shape[:4]
    Y, two, Z, X = lead
    devices = Y * two * Z * X
    for t in range(len(blocks) // unit):
        row = (at + t * unit) * rows
        some = blocks[t * unit : (t + 1) * unit]
        if rows >= 8:
            parts = [b.reshape(devices, rows, 128) for b in some]
            tile = low(parts[0] if unit == 1 else jnp.concatenate(parts, 1))
            PB[:, :, :, :, row : row + unit * rows, :] = tile.reshape(lead + (unit * rows, 128))
            continue
        for k, b in enumerate(some):
            thick[0 : devices * rows, :] = b
            for r in range(rows):
                own = thick[pl.ds(r, devices, stride=rows) if rows > 1 else slice(0, devices), :]
                wide[pl.ds(k * rows + r, devices, stride=16), :] = own
        for i in range(Y * two):
            own = low(wide[i * Z * X * 16 : (i + 1) * Z * X * 16, :])
            PB[i // two, i % two, :, :, row : row + 16, :] = own.reshape(Z, X, 16, 128)


def columns(value):
    return [value[:, k : k + 128] for k in range(0, value.shape[1], 128)]


class Layout:
    def __init__(self, sizes):
        self.sizes = sizes
        Y, Z, X = sizes
        self.lead = (Y, 2, Z, X)
        self.devices = Y * 2 * Z * X
        self.rc = C // self.devices
        self.rw = D // self.devices
        self.bc = C_COLS // 128
        self.bw = D_COLS // 128

        def padded(n, rows):
            unit = max(1, 16 // rows)
            return max(-(-n // unit), 2) * unit

        self.jc = padded(self.bc + 3, self.rc)
        self.j1 = padded(24, self.rc)
        self.j2 = self.jc - self.j1
        thin = self.rc < 8
        self.fwd_rows = 256 if thin else FWD_ROWS
        self.ffn_rows = 256 if thin else FFN_ROWS
        self.bwd_rows = 256 if thin else BWD_ROWS
        f = FF // 128
        rest = 4 * D // 128
        up = padded(rest + 1, self.rw)
        self.jw = up + 2 * f
        self.word_cuts = (0, up, up + f, self.jw)
        self.word_order = list(range(rest)) + [self.bw] + [None] * (up - rest - 1)
        self.word_order += list(range(rest, rest + 2 * f))
        self.word_at = {j: p for p, j in enumerate(self.word_order) if j is not None}


def put(out, blocks, j, value):
    if value.shape[0] == 1:
        out[j : j + 1, :] = value
    else:
        out[pl.ds(j, value.shape[0], stride=blocks), :] = value


class Outs:
    def __init__(self, sem):
        self.sem, self.made = sem, []

    def start(self, src, dst):
        copy = pltpu.make_async_copy(src, dst, self.sem.at[len(self.made)])
        copy.start()
        self.made.append(copy)

    def wait(self):
        for copy in self.made:
            copy.wait()


def hooks(events):
    def hook(i, place):
        for (at, where), acts in events.items():
            if where == place:

                @pl.when(i == at)
                def _(acts=acts):
                    for act in acts:
                        act()

    return hook


def one_hot(condition):
    return condition.astype(F32).astype(BF16)


def slot_ints(codes, counts, langs, ints):
    wide = dot_tn(codes[...].astype(F32).astype(BF16), one_hot(iota((W, 128), 1) % W == iota((W, 128), 0)))
    wide = jnp.where(iota((LEN, 128), 0) % 8 == iota((LEN, 128), 1) // W, wide, 0.0)
    ints[0:16, :] = jnp.sum(wide.reshape(16, 8, 128), 1).astype(jnp.int32)
    group_row = iota((16, LEN), 0) == iota((16, LEN), 1) // 8
    by_slot = one_hot(iota((LEN, 128), 0) % 8 == iota((LEN, 128), 1) // W)
    by_word = one_hot(iota((LEN, 128), 0) % 8 == iota((LEN, 128), 1) % 8)
    count_rows = low(jnp.where(group_row, counts[...].astype(F32), 0.0))
    lang_rows = low(jnp.where(group_row, langs[...].astype(F32), 0.0))
    ints[16:32, :] = dot(lang_rows, by_slot).astype(jnp.int32)
    ints[32:48, :] = dot(count_rows, by_slot).astype(jnp.int32)
    ints[48:64, :] = dot(count_rows, by_word).astype(jnp.int32)


def mono(
    lay, stage,
    codes_in, counts_in, langs_in, length, cm_in, lookup_in, group_in, vec_in, wm_in, wvec_in, cot_in,
    y_out, cm_out, lookup_out, group_out, vec_out, wm_out, wvec_out,
    codes, counts, langs, cm, look, grp, vec, wm, wvec, cot,
    out_y, out_lookup, out_group, out_vec, out_wvec, exc, exw, ints,
    Gc, Gw, PBd, Wc, Wwt, out_cm, out_wm,
    xh1, n1s, qkvs, probs, os, xh2, n2s, acts, slopes, r2s, alphas, dr1s,
    Us, Ys, accq, acco, accu, accd, acct, sums, tsum,
    wide, thin_c, thin_w, thick,
    in_sem, out_sem, ag_send, ag_recv, rs_send, rs_recv, *recv,
):
    Y, Z, X = lay.sizes
    g = Grid(lay.sizes)
    PBc = Gc

    ins = [
        pltpu.make_async_copy(src, dst, in_sem.at[k])
        for k, (src, dst) in enumerate(
            (
                (cm_in, cm), (lookup_in, look), (group_in, grp), (vec_in, vec), (wm_in, wm),
                (wvec_in, wvec), (codes_in, codes), (counts_in, counts), (langs_in, langs), (cot_in, cot),
            )
        )
    ]
    for copy in ins:
        copy.start()
    ag = Copies(ag_send, ag_recv)
    cuts = [c * lay.rw for c in lay.word_cuts]
    gc = gather_pair(g, Gc, ag, 0, Gc.shape[4])
    gu = gather_pair(g, Gw, ag, 0, cuts[2])
    gd = gather_pair(g, Gw, ag, cuts[2], cuts[3])
    g.greet()
    for copy in ins[0:4]:
        copy.wait()
    exc[...] = jnp.zeros(exc.shape, F32)
    exc[:, 0 : 2 * 128] = look[...].astype(F32)
    exc[:, 256 : 256 + LANGS] = grp[...].astype(F32)
    exc[:, 256 + LANGS : 256 + LANGS + 5] = vec[...].astype(F32)
    order_c = list(range(lay.bc + 3)) + [None] * (lay.jc - lay.bc - 3)
    place_own(Gc.at[g.me], cm, out_cm, exc, lay.rc, lay.bc, order_c)
    g.met()
    gc.step1()
    for copy in ins[4:6]:
        copy.wait()
    exw[...] = dot_tn(wvec[...], one_hot(iota((4, 128), 0) == iota((4, 128), 1)))
    place_own(Gw.at[g.me], wm, out_wm, exw, lay.rw, lay.bw, lay.word_order)
    gu.step1()
    gd.step1()
    for copy in ins[6:9]:
        copy.wait()
    slot_ints(codes, counts, langs, ints)
    gc.step2()
    gc.step3()
    gc.step4()
    gd.step2()
    gu.step2()
    gc.step5()
    gc.finish()
    assemble(Gc, Wc, lay.rc, order_c, wide, thin_c)

    eye = (iota((16, 128), 0) == iota((16, 128), 1)).astype(F32).astype(BF16)
    rows_c = dot_nt(eye, Wc[:, (lay.bc + 2) * 128 : (lay.bc + 3) * 128])
    gain1, shift1, gain2, shift2 = (rows_c[8 + k : 9 + k] for k in range(4))
    query = rows_c[12:13]
    table_low = low(jnp.where(iota((16, C), 0) < LANGS, rows_c, 0.0))
    lookup = slice(lay.bc * 128, (lay.bc + 2) * 128)
    AQ, AO = slice(0, 3 * C), slice(3 * C, 4 * C)
    AU, AD = slice(4 * C, 4 * C + CM), slice(4 * C + CM, 4 * C + 2 * CM)
    PK, PV = slice(4 * C + 2 * CM, 5 * C + 2 * CM), slice(5 * C + 2 * CM, 6 * C + 2 * CM)
    PR = slice(6 * C + 2 * CM, 6 * C + 2 * CM + D)

    lane = iota((1, 128), 1)
    lane_word = lane // W
    word_rows = [(lane_word == w).astype(F32).astype(BF16) for w in range(8)]
    heads = head_rows(BF16)
    head_of = iota((128, C), 0) % 32 // 8 == iota((128, C), 1) // HD
    pq_rows = jnp.where(head_of, query * 0.125, 0.0)
    score_map = dot_nt(low(pq_rows), Wc[:, PK])
    map_hi = low(score_map)
    map_lo = low(score_map - map_hi.astype(F32))
    key_row = iota((1, W, 1), 1)
    pool_own = iota((128, 128), 0) // W == iota((128, 128), 1) % 8
    pool_slot = iota((128, 128), 0) % W

    def onehots(i, groups):
        parts = []
        for k in range(groups):
            r = i * groups + k
            codes = ints[pl.ds(r, 1), :]
            langs = ints[pl.ds(16 + r, 1), :]
            a = (iota((VOCAB, 128), 0) == codes).astype(F32).astype(BF16)
            b = (iota((16, 128), 0) == langs).astype(F32).astype(BF16)
            parts.append(jnp.concatenate([a, b], 0))
        return parts

    GF = lay.fwd_rows // 128

    hook_f = hooks({
            (0, 0): [gu.step3],
            (1, 0): [gu.step4],
            (1, 4): [gd.step3],
            (3, 0): [gu.step5],
            (3, 1): [gd.step4],
        })

    def forward(i, _):
        rows = pl.ds(pl.multiple_of(i * lay.fwd_rows, lay.fwd_rows), lay.fwd_rows)
        table = jnp.concatenate([Wc[:, lookup], table_low], 0)
        e = jnp.concatenate([dot_tn(h, table) for h in onehots(i, GF)], 0)
        xhat, scale1 = norm_stats(e)
        n1 = low(xhat * gain1 + shift1)
        xh1[rows, :] = low(xhat)
        n1s[rows, :] = n1
        qkv = low(dot(n1, Wc[:, AQ]))
        qkvs[rows, :] = qkv
        hook_f(i, 0)
        mixed = []
        for k in range(GF):
            visible = key_row < ints[pl.ds(32 + i * GF + k, 1), :].reshape(1, 1, 128)
            pair_out = []
            for p in range(2):
                q, kk, v = (
                    qkv[k * 128 : (k + 1) * 128, b * C + p * 128 : b * C + (p + 1) * 128]
                    for b in range(3)
                )
                s = own_word(dot_nt(head_stack(kk, heads), q), lane_word) * 0.125
                s = jnp.where(visible, s, NEGATIVE)
                s = jnp.exp(s - jnp.max(s, 1, keepdims=True))
                prob = s / jnp.sum(s, 1, keepdims=True)
                probs[i * GF + k, 2 * p : 2 * p + 2] = prob
                pair_out.append(dot_tn(spread_words(low(prob), word_rows), head_stack(v, heads)))
            mixed.append(jnp.concatenate(pair_out, 1))
        o = low(jnp.concatenate(mixed, 0))
        os[rows, :] = o
        hook_f(i, 1)
        r1 = e + dot(o, Wc[:, AO])
        xhat, scale2 = norm_stats(r1)
        n2 = low(xhat * gain2 + shift2)
        xh2[rows, :] = low(xhat)
        n2s[rows, :] = n2
        alphas[rows, 64:65] = scale1
        alphas[rows, 65:66] = scale2
        hook_f(i, 2)
        value, slope = gelu_both(dot(n2, Wc[:, AU]))
        act = low(value)
        acts[rows, :] = act
        slopes[rows, :] = low(slope)
        r2 = low(r1 + dot_nt(act, Wc[:, AD]))
        r2s[rows, :] = r2
        hook_f(i, 3)
        for k in range(GF):
            r = i * GF + k
            own = r2[k * 128 : (k + 1) * 128]
            s = dot_nt(own, map_hi) + dot_nt(own, map_lo)
            seen = pool_own & (pool_slot < ints[pl.ds(48 + r, 1), :])
            s = jnp.where(seen, s, NEGATIVE)
            s = jnp.where(seen, jnp.exp(s - jnp.max(s, 0, keepdims=True)), 0.0)
            alpha = s / jnp.sum(s, 0, keepdims=True)
            alphas[pl.ds(pl.multiple_of(r * 128, 128), 128), 0:32] = alpha[:, :32]
            u = dot_tn(low(alpha)[:, :32], own)
            for h in range(CH):
                Us[h, pl.ds(pl.multiple_of(r * 8, 8), 8), :] = u[8 * h : 8 * h + 8]
        hook_f(i, 4)
        return 0

    lax.fori_loop(0, LEN * W // lay.fwd_rows, forward, 0)

    head_c = [iota((1, C), 1) // HD == h for h in range(CH)]
    pooled = sum(jnp.where(head_c[h], dot(low(Us[h]), Wc[:, PV]), 0.0) for h in range(CH))
    pooled_low = low(pooled)
    w_in = dot(pooled_low, Wc[:, PR])

    gu.finish()
    if lay.rw < 16:
        gd.finish()
    if lay.rw >= 16:

        def wcols(lo, hi):
            return jnp.concatenate(
                [
                    Gw[:, :, :, :, p * lay.rw : (p + 1) * lay.rw, :].reshape(D, 128)
                    for p in [lay.word_at[j] for j in range(lo // 128, hi // 128)]
                ],
                1,
            )

    else:
        assemble(Gw, Wwt, lay.rw, lay.word_order, wide, thin_w)

        def wcols(lo, hi):
            return Wwt[:, lo:hi]

    rows_w = dot_nt(eye, wcols(D_COLS, D_COLS + 128))
    f1, c1, f2, c2 = (rows_w[k : k + 1] for k in range(4))
    BQ, BO, BU, BD = (0, 3 * D), (3 * D, 4 * D), (4 * D, 4 * D + FF), (4 * D + FF, D_COLS)
    NP = H // 2

    xhat1, sc1 = norm_stats(w_in)
    m1 = low(xhat1 * f1 + c1)
    qkv = low(dot(m1, wcols(*BQ)))
    key = iota((1, 128, 1), 1)
    seen_word = (key <= iota((1, 1, 128), 2)) & (key < length[0])
    pw, kst, qst, vst, mix = [], [], [], [], []
    for p in range(NP):
        q, kk, v = (qkv[:, b * D + p * 128 : b * D + (p + 1) * 128] for b in range(3))
        kst.append(head_stack(kk, heads))
        qst.append(head_stack(q, heads))
        vst.append(head_stack(v, heads))
        s = dot_nt(kst[p], q).reshape(2, 128, 128) * 0.125
        s = jnp.where(seen_word, s, NEGATIVE)
        s = jnp.exp(s - jnp.max(s, 1, keepdims=True))
        pw.append(s / jnp.sum(s, 1, keepdims=True))
        mix.append(dot_tn(low(pw[p]).reshape(256, 128), vst[p]))
    ow = low(jnp.concatenate(mix, 1))
    x = w_in + dot(ow, wcols(*BO))
    xhat2, sc2 = norm_stats(x)
    m2 = low(xhat2 * f2 + c2)
    value, slope = gelu_both(dot(m2, wcols(*BU)))
    aw = low(value)
    ins[9].wait()
    gy = cot[...]
    dy = gy.astype(F32)
    rw = lay.rw
    unit_w = max(1, 16 // rw)
    waiting = {}

    def put_w(at, blocks):
        waiting.update({at + k: b for k, b in enumerate(blocks)})
        for first in range(0, lay.jw, unit_w):
            ready = range(first, first + unit_w)
            if all(j in waiting for j in ready):
                some = [waiting.pop(j) for j in ready]
                if rw >= 16 and first >= lay.word_cuts[2]:
                    pack_blocks(PBd, first - lay.word_cuts[2], some, rw, wide, thick)
                else:
                    pack_blocks(Gw, first, some, rw, wide, thick)

    rs = Copies(rs_send, rs_recv)
    land = list(recv)
    first_d = 0 if rw >= 16 else cuts[2]
    cut1 = lay.j1 * lay.rc
    w1 = scatter_pair(g, PBd if rw >= 16 else Gw, land, rs, first_d, first_d + cuts[3] - cuts[2])
    w2 = scatter_pair(g, Gw, land, rs, cuts[1], cuts[2])
    w3 = scatter_pair(g, Gw, land, rs, 0, cuts[1])
    s1 = scatter_pair(g, Gc, land, rs, 0, cut1)
    s2 = scatter_pair(g, Gc, land, rs, cut1, Gc.shape[4])
    if rw < 16:
        gu.drain()
        gd.drain()
    at = lay.word_cuts[2]
    gd.step5()
    for k in range(0, FF, 512):
        put_w(at + k // 128, columns(dot_tn(gy, aw[:, k : k + 512])))
    w1.step1()
    pass
    if rw >= 16:
        gd.finish()
        gu.drain()
        gd.drain()
    out_y[...] = low(x + dot_nt(aw, wcols(*BD)))
    outs = Outs(out_sem)
    outs.start(out_y, y_out)
    gzw = low(slope * dot(gy, wcols(*BD)))
    pass
    dm2 = dot_nt(gzw, wcols(*BU))
    at = lay.word_cuts[1]
    for k in range(0, FF, 512):
        put_w(at + k // 128, columns(dot_tn(m2, gzw[:, k : k + 512])))
    w2.step1()
    w1.step2()
    gf2 = jnp.sum(dm2 * xhat2, 0, keepdims=True)
    gc2 = jnp.sum(dm2, 0, keepdims=True)
    dx = dy + norm_back(dm2, xhat2, sc2, f2)
    gx = low(dx)
    gow = low(dot_nt(gx, wcols(*BO)))
    put_w(BO[0] // 128, columns(dot_tn(ow, gx)))
    pass
    gq, gk, gv = [], [], []
    for p in range(NP):
        go = gow[:, p * 128 : (p + 1) * 128]
        dp = dot_nt(vst[p], go).reshape(2, 128, 128)
        inner = jnp.sum(pw[p] * dp, 1, keepdims=True)
        gs = low(pw[p] * (dp - inner)).reshape(256, 128)
        gq.append(dot_tn(gs, kst[p]) * 0.125)
        gk.append(dot(side_by_side(gs, 128), qst[p]) * 0.125)
        gv.append(dot(side_by_side(low(pw[p]).reshape(256, 128), 128), head_stack(go, heads)))
    tg = low(jnp.concatenate(gq + gk + gv, 1))
    dm1 = dot_nt(tg, wcols(*BQ))
    for k in range(0, 3 * D, 512):
        put_w(k // 128, columns(dot_tn(m1, tg[:, k : k + 512])))
    gf1 = jnp.sum(dm1 * xhat1, 0, keepdims=True)
    gc1 = jnp.sum(dm1, 0, keepdims=True)
    dw = dx + norm_back(dm1, xhat1, sc1, f1)
    vec_rows = low(jnp.concatenate([gf1, gc1, gf2, gc2, jnp.zeros((12, D), F32)], 0))
    at = lay.word_at[lay.bw]
    put_w(at, [dot_tn(vec_rows, eye)] + [jnp.zeros((D, 128), F32)] * (lay.word_cuts[1] - at - 1))
    w3.step1()
    w2.step2()

    gc.drain()
    gw = low(dw)
    dpool = dot_nt(gw, Wc[:, PR])
    pass
    dp4 = jnp.concatenate([low(jnp.where(head_c[h], dpool, 0.0)) for h in range(CH)], 0)
    Ys[...] = dot_nt(dp4, Wc[:, PV]).reshape(CH, LEN, C)
    for ref in (accq, acco, accu, accd, acct, sums, tsum):
        ref[...] = jnp.zeros(ref.shape, F32)

    map32 = map_hi[:32]
    GB = lay.bwd_rows // 128

    GP = lay.ffn_rows // 128

    def back_ffn(i, _):
        rows = pl.ds(pl.multiple_of(i * lay.ffn_rows, lay.ffn_rows), lay.ffn_rows)
        parts = []
        for k in range(GP):
            r = i * GP + k
            own = r2s[pl.ds(pl.multiple_of(r * 128, 128), 128), :]
            alpha = alphas[pl.ds(pl.multiple_of(r * 128, 128), 128), 0:32]
            yg = low(
                jnp.concatenate(
                    [Ys[h, pl.ds(pl.multiple_of(r * 8, 8), 8), :] for h in range(CH)], 0
                )
            )
            da = dot_nt(own, yg)
            dr = low(alpha * (da - jnp.sum(alpha * da, 0, keepdims=True)))
            tsum[...] += dot_tn(dr, own)
            parts.append(dot(low(alpha), yg) + dot(dr, map32))
        dr2 = jnp.concatenate(parts, 0)
        g2 = low(dr2)
        hook_1(i, 0)
        accd[...] += dot_tn(g2, acts[rows, :])
        hook_1(i, 1)
        gz = low(slopes[rows, :].astype(F32) * dot(g2, Wc[:, AD]))
        accu[...] += dot_tn(n2s[rows, :], gz)
        hook_1(i, 2)
        dn = dot_nt(gz, Wc[:, AU])
        xhat = xh2[rows, :].astype(F32)
        sums[2:3, :] += jnp.sum(dn * xhat, 0, keepdims=True)
        sums[3:4, :] += jnp.sum(dn, 0, keepdims=True)
        dr1s[rows, :] = dr2 + norm_back(dn, xhat, alphas[rows, 65:66], gain2)
        hook_1(i, 3)
        return 0

    def place_w(j, value):
        j = lay.word_order[j]
        if j is None:
            return
        if j < lay.bw:
            put(out_wm, lay.bw, j, value)
        else:
            pick = (iota((8, 128), 0) == iota((8, 128), 1)).astype(F32)
            out_wvec[...] = lax.dot_general(
                pick, value, (((1,), (1,)), ((), ())),
                precision=lax.Precision.HIGHEST, preferred_element_type=F32,
            )[0:4]

    def place_1(j, value):
        put(out_cm, lay.bc, 8 + j, value)

    def place_2(j, value):
        if j < 8:
            put(out_cm, lay.bc, j, value)
        elif j < 10:
            out_lookup[:, (j - 8) * 128 : (j - 7) * 128] = value
        else:
            out_group[...] = value[:, 0:LANGS]
            out_vec[...] = value[:, LANGS : LANGS + 5]

    def fin_w1():
        w1.finish(lambda j, v: place_w(lay.word_cuts[2] + j, v), rw, first_d, FF // 128)

    def fin_w2():
        w2.finish(lambda j, v: place_w(lay.word_cuts[1] + j, v), rw, cuts[1], FF // 128)

    def fin_w3():
        w3.finish(place_w, rw, 0, lay.word_cuts[1])

    def fin_s1():
        s1.finish(place_1, rc, 0, 24)

    def fin_s2():
        s2.finish(place_2, rc, cut1, 11)

    hook_1 = hooks({
            (0, 3): [w1.step3, w3.step2],
            (3, 2): [w1.step4, w2.step3],
        })
    lax.fori_loop(0, LEN * W // lay.ffn_rows, back_ffn, 0)

    grad_pr = dot_tn(pooled_low, gw)
    grad_pv = dot_tn(low(Us[...]).reshape(CH * LEN, C), dp4)
    t_low = low(tsum[...])
    grad_pk = dot_tn(t_low, low(pq_rows[:32]))
    rc = lay.rc
    pad1 = [jnp.zeros((C, 128), F32)] * (lay.j1 - 24)
    pack_blocks(
        PBc,
        0,
        columns(accu[...]) + columns(accd[...]) + columns(grad_pk) + columns(grad_pv)
        + columns(grad_pr) + pad1,
        rc,
        wide,
        thick,
    )
    s1.step1()
    pass
    gpq = dot(t_low, Wc[:, PK]) * 0.125
    gpq = jnp.sum(
        jnp.where(iota((32, C), 0) // 8 == iota((32, C), 1) // HD, gpq, 0.0), 0, keepdims=True
    )

    def back_attention(i, _):
        rows = pl.ds(pl.multiple_of(i * lay.bwd_rows, lay.bwd_rows), lay.bwd_rows)
        dr1 = dr1s[rows, :]
        g1 = low(dr1)
        acco[...] += dot_tn(os[rows, :], g1)
        go = low(dot_nt(g1, Wc[:, AO]))
        hook_2(i, 0)
        qkv = qkvs[rows, :]
        grads = [[], [], []]
        for k in range(GB):
            part = [[], [], []]
            for p in range(2):
                at = slice(k * 128, (k + 1) * 128)
                q, kk, v = (
                    qkv[at, b * C + p * 128 : b * C + (p + 1) * 128] for b in range(3)
                )
                gop = go[at, p * 128 : (p + 1) * 128]
                prob = probs[i * GB + k, 2 * p : 2 * p + 2]
                dp = own_word(dot_nt(head_stack(v, heads), gop), lane_word)
                gs = low(prob * (dp - jnp.sum(prob * dp, 1, keepdims=True)))
                gs = spread_words(gs, word_rows)
                pb = spread_words(low(prob), word_rows)
                part[0].append(dot_tn(gs, head_stack(kk, heads)) * 0.125)
                part[1].append(dot(side_by_side(gs, 128), head_stack(q, heads)) * 0.125)
                part[2].append(dot(side_by_side(pb, 128), head_stack(gop, heads)))
            for b in range(3):
                grads[b].append(jnp.concatenate(part[b], 1))
        hook_2(i, 1)
        tg = low(jnp.concatenate([jnp.concatenate(b, 0) for b in grads], 1))
        accq[...] += dot_tn(n1s[rows, :], tg)
        dn = dot_nt(tg, Wc[:, AQ])
        hook_2(i, 2)
        xhat = xh1[rows, :].astype(F32)
        sums[0:1, :] += jnp.sum(dn * xhat, 0, keepdims=True)
        sums[1:2, :] += jnp.sum(dn, 0, keepdims=True)
        ge = low(dr1 + norm_back(dn, xhat, alphas[rows, 64:65], gain1))
        for k, h in enumerate(onehots(i, GB)):
            acct[...] += dot(h, ge[k * 128 : (k + 1) * 128])
        hook_2(i, 3)
        return 0

    hook_2 = hooks({
            (0, 2): [w3.step3],
            (1, 0): [w2.step4, s1.step2],
            (2, 2): [w3.step4],
            (3, 2): [s1.step3],
        })
    lax.fori_loop(0, LEN * W // lay.bwd_rows, back_attention, 0)

    pass
    small = low(jnp.concatenate([acct[VOCAB : VOCAB + 8], sums[0:4], gpq, jnp.zeros((3, C), F32)], 0))
    pad2 = [jnp.zeros((C, 128), F32)] * (lay.j2 - 11)
    pack_blocks(
        PBc,
        lay.j1,
        columns(accq[...]) + columns(acco[...]) + columns(acct[0:VOCAB, :])
        + [dot_tn(small, eye)] + pad2,
        rc,
        wide,
        thick,
    )
    s2.step1()
    s2.step2()
    s1.step4()
    s2.step3()
    fin_w2()
    fin_w1()
    s2.step4()
    fin_w3()
    outs.start(out_wm, wm_out)
    outs.start(out_wvec, wvec_out)
    fin_s1()
    fin_s2()
    outs.start(out_cm, cm_out)
    outs.start(out_lookup, lookup_out)
    outs.start(out_group, group_out)
    outs.start(out_vec, vec_out)
    for part in (w1, w2, w3, s1, s2):
        part.drain()
    outs.wait()


def hand_over(*refs):
    n = 7
    ins, outs, held, sems = refs[:n], refs[n : 2 * n], refs[2 * n : 3 * n], refs[-1]
    first = [pltpu.make_async_copy(ins[k], held[k], sems.at[k]) for k in range(n)]
    then = [pltpu.make_async_copy(held[k], outs[k], sems.at[n + k]) for k in range(n)]
    for copy in first:
        copy.start()
    for k in range(n):
        first[k].wait()
        then[k].start()
    for copy in then:
        copy.wait()


def shards(
    sizes,
    char_codes,
    char_counts,
    word_groups,
    valid_words,
    char_matrix,
    char_lookup,
    group_lookup,
    char_vectors,
    word_matrix,
    word_vectors,
    cotangent,
):
    lay = Layout(sizes)
    Y, Z, X = sizes
    rows = LEN * W
    rows_c, rows_w = lay.jc * lay.rc, lay.jw * lay.rw
    rows_1 = lay.j1 * lay.rc
    nag = ag_count(Y, Z, X) * 6
    nrs = rs_count(Y, Z, X) * 10
    dma = pltpu.SemaphoreType.DMA

    def vm(shape, dtype):
        return pltpu.VMEM(shape, dtype)

    def like(a):
        return pltpu.VMEM(a.shape, a.dtype)

    ins = (
        char_codes[0].T,
        char_counts,
        word_groups,
        valid_words,
        char_matrix,
        char_lookup,
        group_lookup,
        char_vectors,
        word_matrix,
        word_vectors.T,
        cotangent[0],
    )
    outs = [
        jax.ShapeDtypeStruct((LEN, D), BF16),
        jax.ShapeDtypeStruct(char_matrix.shape, F32),
        jax.ShapeDtypeStruct(char_lookup.shape, F32),
        jax.ShapeDtypeStruct(group_lookup.shape, F32),
        jax.ShapeDtypeStruct(char_vectors.shape, F32),
        jax.ShapeDtypeStruct(word_matrix.shape, F32),
        jax.ShapeDtypeStruct(word_vectors.shape[::-1], F32),
    ]
    scratch = [like(a) for k, a in enumerate(ins) if k != 3]
    scratch += [like(outs[k]) for k in (0, 2, 3, 4, 6)]
    scratch += [
        vm((lay.rc, 3 * 128), F32),
        vm((lay.rw, 128), F32),
        vm((64, 128), jnp.int32),
        vm(lay.lead + (rows_c, 128), BF16),
        vm(lay.lead + (rows_w, 128), BF16),
        vm(lay.lead + (FF // 128 * lay.rw, 128) if lay.rw >= 16 else (16, 128), BF16),
        vm((C, (lay.bc + 3) * 128), BF16),
        vm((D, (lay.bw + 1) * 128) if lay.rw < 16 else (16, 128), BF16),
        like(outs[1]),
        like(outs[5]),
        vm((rows, C), BF16),
        vm((rows, C), BF16),
        vm((rows, 3 * C), BF16),
        vm((16, CH, W, 128), F32),
        vm((rows, C), BF16),
        vm((rows, C), BF16),
        vm((rows, C), BF16),
        vm((rows, CM), BF16),
        vm((rows, CM), BF16),
        vm((rows, C), BF16),
        vm((rows, 128), F32),
        vm((rows, C), F32),
        vm((CH, LEN, C), F32),
        vm((CH, LEN, C), F32),
        vm((C, 3 * C), F32),
        vm((C, C), F32),
        vm((C, CM), F32),
        vm((C, CM), F32),
        vm((VOCAB + 16, C), F32),
        vm((8, C), F32),
        vm((32, C), F32),
        vm((lay.devices * 16 if lay.rc < 8 else 8, 128), F32),
        vm((Z * X * lay.rc, 128), F32),
        vm((Z * X * lay.rw, 128), F32),
        vm((D if lay.rc < 8 else 8, 128), F32),
        dma((10,)),
        dma((7,)),
        dma((nag,)),
        dma((nag,)),
        dma((nrs,)),
        dma((nrs,)),
    ]
    at = [c * lay.rw for c in lay.word_cuts]
    for lo, hi in ((at[2], at[3]), (at[1], at[2]), (at[0], at[1]), (0, rows_1), (rows_1, rows_c)):
        scratch += scatter_pair_scratch(sizes, lo, hi)
    anywhere = pl.BlockSpec(memory_space=pl.ANY)
    in_specs = [anywhere] * 11
    in_specs[3] = pl.BlockSpec(memory_space=pltpu.SMEM)
    got = pl.pallas_call(
        functools.partial(mono, lay, STAGE),
        out_shape=outs,
        in_specs=in_specs,
        out_specs=[anywhere] * 7,
        scratch_shapes=scratch,
        compiler_params=pltpu.CompilerParams(
            collective_id=0, has_side_effects=True, vmem_limit_bytes=VMEM_LIMIT
        ),
        name="layer",
    )(*ins)
    got = pl.pallas_call(
        hand_over,
        out_shape=outs,
        in_specs=[anywhere] * 7,
        out_specs=[anywhere] * 7,
        scratch_shapes=[like(a) for a in outs] + [dma((14,))],
        name="hand_over",
    )(*got)
    return (got[0][None],) + tuple(got[1:6]) + (got[6].T,)


def solution(mesh):
    dp, fsdp = mesh.shape["dp"], mesh.shape["fsdp"]
    Y = dp // 2
    X = Y if fsdp % Y == 0 else 1
    sizes = (Y, fsdp // X, X)
    placed = (
        P(("dp", "fsdp"), None, None),
        P(("dp", "fsdp"), None),
        P(("dp", "fsdp"), None),
        P(("dp", "fsdp")),
        P(("dp", "fsdp"), None),
        P(("dp", "fsdp"), None),
        P(("dp", "fsdp"), None),
        P(("dp", "fsdp"), None),
        P(("dp", "fsdp"), None),
        P(("dp", "fsdp"), None),
        P(("dp", "fsdp"), None, None),
    )
    return jax.shard_map(
        functools.partial(shards, sizes),
        mesh=mesh,
        in_specs=placed,
        out_specs=(
            P(("dp", "fsdp"), None, None),
            P(("dp", "fsdp"), None),
            P(("dp", "fsdp"), None),
            P(("dp", "fsdp"), None),
            P(("dp", "fsdp"), None),
            P(("dp", "fsdp"), None),
            P(("dp", "fsdp"), None),
        ),
        check_vma=False,
    )
```

```python
import functools

import jax
import jax.numpy as jnp
from jax import lax
from jax.experimental import pallas as pl
from jax.experimental.pallas import tpu as pltpu
from jax.sharding import PartitionSpec as P

C = 256
HD = 64
CH = 4
CM = 1024
D = 512
H = 8
FF = 2048
W = 16
VOCAB = 256
LANGS = 8
LEN = 128
C_COLS = 6 * C + 2 * CM + D
D_COLS = 4 * D + 2 * FF
EPSILON = 1e-05
NEGATIVE = -1000000000.0
F32 = jnp.float32
BF16 = jnp.bfloat16
FWD_ROWS = 1024
BWD_ROWS = 1024
FFN_ROWS = 1024
VMEM_LIMIT = 63 << 20
STAGE = 0


MESH = pl.DeviceIdType.MESH
ALL = slice(None)


class Grid:
    def __init__(self, sizes):
        self.Y, self.Z, self.X = sizes
        dp, fs = lax.axis_index("dp"), lax.axis_index("fsdp")
        self.y, self.c = dp // 2, dp % 2
        self.z, self.x = fs // self.X, fs % self.X
        self.me = (self.y, self.c, self.z, self.x)
        self.ys = [(self.y + k) % self.Y for k in range(1, self.Y)]
        self.zs = [(self.z + k) % self.Z for k in range(1, self.Z)]
        self.xs = [(self.x + k) % self.X for k in range(1, self.X)]
        self.to_y = [self.at(y=y) for y in self.ys]
        self.to_z = [self.at(z=z) for z in self.zs]
        self.to_x = [self.at(x=x) for x in self.xs]
        self.to_c = self.at(c=1 - self.c)
        self.to = {"y": self.to_y, "z": self.to_z, "x": self.to_x}
        self.src = {
            "y": [(self.y + self.Y - k) % self.Y for k in range(1, self.Y)],
            "z": [(self.z + self.Z - k) % self.Z for k in range(1, self.Z)],
            "x": [(self.x + self.X - k) % self.X for k in range(1, self.X)],
        }
        self.off = {"y": self.ys, "z": self.zs, "x": self.xs}

    def at(self, y=None, c=None, z=None, x=None):
        y = self.y if y is None else y
        c = self.c if c is None else c
        z = self.z if z is None else z
        x = self.x if x is None else x
        return (y * 2 + c, z * self.X + x)

    def greet(self):
        barrier = pltpu.get_barrier_semaphore()
        self.partners = [self.to_c] + self.to_y + self.to_z + self.to_x
        for p in self.partners:
            pl.semaphore_signal(barrier, inc=1, device_id=p, device_id_type=MESH)

    def met(self):
        pl.semaphore_wait(pltpu.get_barrier_semaphore(), len(self.partners))


class Copies:
    def __init__(self, send, recv):
        self.send, self.recv, self.made = send, recv, []

    def plan(self, src, dst, to):
        self.made.append((src, dst, to))
        return len(self.made) - 1

    def make(self, i):
        src, dst, to = self.made[i]
        return pltpu.make_async_remote_copy(
            src_ref=src,
            dst_ref=dst,
            send_sem=self.send.at[i],
            recv_sem=self.recv.at[i],
            device_id=to,
            device_id_type=MESH,
        )

    def start(self, which):
        for i in which:
            self.make(i).start()

    def arrived(self, which):
        for i in which:
            self.make(i).wait_recv()

    def left(self, which):
        for i in which:
            self.make(i).wait_send()


def ag_count(Y, Z, X):
    n = max(Z - 1, X - 1, Y - 1)
    return 6 * n + 1 + 2 * n * n


class Gather:
    def __init__(self, g, G, copies, lo, hi, order):
        self.copies = copies
        first = len(copies.made)
        one, two, three = order
        rows = slice(lo, hi)

        def slot(**at):
            v = {"y": g.y, "z": g.z, "x": g.x, **at}
            return (v["y"], g.c, v["z"], v["x"], rows)

        def plan(to, **at):
            return copies.plan(G.at[slot(**at)], G.at[slot(**at)], to)

        self.first = [plan(to) for to in g.to[one]]
        self.own2 = [plan(to) for to in g.to[two]]
        self.own3 = [plan(to, **{two: ALL}) for to in g.to[three]]
        self.rest2 = [[plan(to, **{one: v}) for to in g.to[two]] for v in g.src[one]]
        self.rest3 = [[plan(to, **{one: v, two: ALL}) for to in g.to[three]] for v in g.src[one]]
        self.core1 = [plan(g.to_c)]
        self.core2 = [plan(g.to_c, **{two: w}) for w in g.src[two]]
        self.core4 = [[plan(g.to_c, **{one: v, two: ALL})] for v in g.src[one]]
        self.core5 = [plan(g.to_c, **{one: ALL, two: ALL, three: u}) for u in g.src[three]]
        self.mine = range(first, len(copies.made))

    def step1(self):
        self.copies.start(self.first + self.own2 + self.core1)

    def step2(self):
        self.copies.arrived(self.own2)
        self.copies.start(self.own3 + self.core2)

    def step3(self):
        for k, which in enumerate(self.rest2):
            self.copies.arrived(self.first[k : k + 1])
            self.copies.start(which)

    def step4(self):
        for k, which in enumerate(self.rest3):
            self.copies.arrived(self.rest2[k])
            self.copies.start(which + self.core4[k])

    def step5(self):
        self.copies.arrived(self.own3)
        for which in self.rest3:
            self.copies.arrived(which)
        self.copies.start(self.core5)

    def finish(self):
        self.copies.arrived(self.core1 + self.core2 + self.core5)
        for which in self.core4:
            self.copies.arrived(which)

    def drain(self):
        self.copies.left(self.mine)


def rs_count(Y, Z, X):
    return 1 + (Z - 1) + (X - 1) + (Y - 1)


def rs_scratch(sizes, rows, order):
    n = dict(zip("yzx", sizes))
    left = dict(n)
    shapes = [pltpu.VMEM(sizes + (rows, 128), BF16)]
    for axis in order:
        left[axis] = 1
        shapes.append(pltpu.VMEM((n[axis] - 1, left["y"], left["z"], left["x"], rows, 128), BF16))
    return shapes


def add_into(dst, srcs):
    lead = dst.shape[:-2]
    total = 1
    for n in lead:
        total *= n
    some = next(n for n in (16, 8, 4, 2, 1) if total % n == 0)

    def body(i, _):
        for part in range(some):
            idx, r = [], i * some + part
            for n in reversed(lead):
                idx.append(r % n)
                r = r // n
            idx = tuple(reversed(idx))
            if len(srcs) == 1:
                dst[idx] = dst[idx] + srcs[0][idx]
                continue
            acc = dst[idx].astype(F32)
            for s in srcs:
                acc = acc + s[idx].astype(F32)
            dst[idx] = acc.astype(BF16)
        return 0

    lax.fori_loop(0, total // some, body, 0)


class Scatter:
    def __init__(self, g, PB, recv, copies, lo, hi, order):
        self.g, self.PB, self.copies, self.recv = g, PB, copies, recv
        self.lo, self.hi = lo, hi
        first = len(copies.made)
        rows = slice(lo, hi)
        me = {"y": g.y, "z": g.z, "x": g.x}
        have = {"y": ALL, "z": ALL, "x": ALL}

        def slot(c, **at):
            v = {**have, **at}
            return (v["y"], c, v["z"], v["x"], rows)

        self.hops = [[copies.plan(PB.at[slot(1 - g.c)], recv[0], g.to_c)]]
        self.sums = [PB.at[slot(g.c)]]
        for n, axis in enumerate(order):
            self.hops.append(
                [
                    copies.plan(PB.at[slot(g.c, **{axis: pl.ds(v, 1)})], recv[n + 1].at[k], to)
                    for k, (v, to) in enumerate(zip(g.off[axis], g.to[axis]))
                ]
            )
            have[axis] = pl.ds(me[axis], 1)
            self.sums.append(PB.at[slot(g.c)])
        self.mine = range(first, len(copies.made))

    def add(self, n):
        self.copies.arrived(self.hops[n])
        if n == 0:
            add_into(self.sums[0], [self.recv[0]])
        else:
            add_into(self.sums[n], [self.recv[n].at[k] for k in range(len(self.hops[n]))])

    def step1(self):
        self.copies.start(self.hops[0])

    def step2(self):
        self.add(0)
        self.copies.start(self.hops[1])

    def step3(self):
        self.add(1)
        self.copies.start(self.hops[2])

    def step4(self):
        self.add(2)
        self.copies.start(self.hops[3])

    def finish(self, place, rows, base, count):
        self.copies.arrived(self.hops[3])
        size = max(rows, 16)
        for row in range(self.lo, self.hi, size):
            r = slice(row - self.lo, row - self.lo + size)
            acc = self.PB[self.g.me + (slice(row, row + size),)].astype(F32)
            for k in range(len(self.hops[3])):
                acc = acc + self.recv[3][k, 0, 0, 0, r].astype(F32)
            for u in range(size // rows):
                j = (row - base) // rows + u
                if j < count:
                    place(j, acc[u * rows : (u + 1) * rows])

    def drain(self):
        self.copies.left(self.mine)


class Pair:
    def __init__(self, parts):
        self.parts = parts

    def all(self, name, *args):
        for part in self.parts:
            getattr(part, name)(*args)

    def step1(self):
        self.all("step1")

    def step2(self):
        self.all("step2")

    def step3(self):
        self.all("step3")

    def step4(self):
        self.all("step4")

    def step5(self):
        self.all("step5")

    def finish(self, *args):
        self.all("finish", *args)

    def drain(self):
        self.all("drain")


def halves(lo, hi):
    mid = lo + (hi - lo + 31) // 32 * 16
    return [(lo, mid), (mid, hi)] if mid < hi else [(lo, hi)]


def gather_pair(g, G, copies, lo, hi):
    orders = ("zxy", "zyx")
    return Pair([Gather(g, G, copies, *cut, o) for cut, o in zip(halves(lo, hi), orders)])


SUM_ORDERS = ("yxz", "xyz")


def scatter_pair(g, PB, recv, copies, lo, hi):
    parts = []
    for cut, o in zip(halves(lo, hi), SUM_ORDERS):
        parts.append(Scatter(g, PB, recv[:4], copies, *cut, o))
        del recv[:4]
    return Pair(parts)


def scatter_pair_scratch(sizes, lo, hi):
    out = []
    for (a, b), o in zip(halves(lo, hi), SUM_ORDERS):
        out += rs_scratch(sizes, b - a, o)
    return out


def dot(a, b):
    return lax.dot_general(a, b, (((1,), (0,)), ((), ())), preferred_element_type=F32)


def dot_nt(a, b):
    return lax.dot_general(a, b, (((1,), (1,)), ((), ())), preferred_element_type=F32)


def dot_tn(a, b):
    return lax.dot_general(a, b, (((0,), (0,)), ((), ())), preferred_element_type=F32)


def low(v):
    return v.astype(BF16)


def norm_stats(x):
    centre = x - jnp.mean(x, -1, keepdims=True)
    spread = jnp.mean(centre * centre, -1, keepdims=True)
    scale = lax.rsqrt(spread + EPSILON)
    return centre * scale, scale


def norm_back(grad, xhat, scale, gain):
    inner = grad * gain
    first = jnp.mean(inner, -1, keepdims=True)
    second = jnp.mean(inner * xhat, -1, keepdims=True)
    return scale * (inner - first - xhat * second)


def gelu_both(z):
    sq = z * z
    t = jnp.tanh(z * (0.7978845608028654 + (0.7978845608028654 * 0.044715) * sq))
    h = 0.5 * z
    value = h + h * t
    slope = 0.5 + 0.5 * t + h * (1.0 - t * t) * (
        0.7978845608028654 + (3.0 * 0.7978845608028654 * 0.044715) * sq
    )
    return value, slope


def iota(shape, dim):
    return lax.broadcasted_iota(jnp.int32, shape, dim)


def head_rows(dtype):
    lane = iota((1, 128), 1)
    return [(lane // HD == h).astype(F32).astype(dtype) for h in range(2)]


def head_stack(block, heads):
    return jnp.concatenate([block * h for h in heads], 0)


def own_word(scores, lane_word):
    split = scores.reshape(2, 8, W, 128)
    out = split[:, 0]
    for w in range(1, 8):
        out = jnp.where(lane_word == w, split[:, w], out)
    return out


def spread_words(compact, word_rows):
    return jnp.concatenate([compact[h] * word_rows[w] for h in range(2) for w in range(8)], 0)


def side_by_side(stacked, rows):
    return jnp.concatenate([stacked[h * rows : (h + 1) * rows] for h in range(2)], 1)


def place_own(own, raw, staged, extra, rows, blocks, order):
    staged[...] = raw[...].astype(F32)
    unit = max(1, 16 // rows)

    def block(j):
        if j is None:
            return jnp.zeros((rows, 128), F32)
        if j < blocks:
            if rows == 1:
                return staged[j : j + 1, :]
            return staged[pl.ds(j, rows, stride=blocks), :]
        at = (j - blocks) * 128
        return extra[:, at : at + 128]

    for t in range(len(order) // unit):
        tile = jnp.concatenate([block(j) for j in order[t * unit : (t + 1) * unit]], 0)
        own[t * unit * rows : (t + 1) * unit * rows, :] = low(tile)


def assemble(G, Wd, rows, order, wide, thin):
    unit = max(1, 16 // rows)
    Y, two, Z, X = G.shape[:4]
    some = Z * X * rows

    def body(i, _):
        at = pl.ds(pl.multiple_of(i * some, 16), some)
        for t in range(len(order) // unit):
            tile = G[i // two, i % two, :, :, t * unit * rows : (t + 1) * unit * rows, :]
            tile = tile.reshape(Z * X, 16, 128).astype(F32)
            if rows < 8:
                wide[0 : Z * X * 16, :] = tile.reshape(Z * X * 16, 128)
            for u in range(unit):
                j = order[t * unit + u]
                if j is None:
                    continue
                if rows < 8:
                    for r in range(rows):
                        own = wide[pl.ds(u * rows + r, Z * X, stride=16), :]
                        thin[pl.ds(r, Z * X, stride=rows) if rows > 1 else ALL, :] = own
                    Wd[at, j * 128 : (j + 1) * 128] = low(thin[...])
                    continue
                Wd[at, j * 128 : (j + 1) * 128] = low(
                    tile[:, u * rows : (u + 1) * rows, :].reshape(some, 128)
                )
        return 0

    lax.fori_loop(0, Y * two, body, 0)


def pack_blocks(PB, at, blocks, rows, wide, thick):
    unit = max(1, 16 // rows)
    lead = PB.shape[:4]
    Y, two, Z, X = lead
    devices = Y * two * Z * X
    for t in range(len(blocks) // unit):
        row = (at + t * unit) * rows
        some = blocks[t * unit : (t + 1) * unit]
        if rows >= 8:
            parts = [b.reshape(devices, rows, 128) for b in some]
            tile = low(parts[0] if unit == 1 else jnp.concatenate(parts, 1))
            PB[:, :, :, :, row : row + unit * rows, :] = tile.reshape(lead + (unit * rows, 128))
            continue
        for k, b in enumerate(some):
            thick[0 : devices * rows, :] = b
            for r in range(rows):
                own = thick[pl.ds(r, devices, stride=rows) if rows > 1 else slice(0, devices), :]
                wide[pl.ds(k * rows + r, devices, stride=16), :] = own
        for i in range(Y * two):
            own = low(wide[i * Z * X * 16 : (i + 1) * Z * X * 16, :])
            PB[i // two, i % two, :, :, row : row + 16, :] = own.reshape(Z, X, 16, 128)


def columns(value):
    return [value[:, k : k + 128] for k in range(0, value.shape[1], 128)]


class Layout:
    def __init__(self, sizes):
        self.sizes = sizes
        Y, Z, X = sizes
        self.lead = (Y, 2, Z, X)
        self.devices = Y * 2 * Z * X
        self.rc = C // self.devices
        self.rw = D // self.devices
        self.bc = C_COLS // 128
        self.bw = D_COLS // 128

        def padded(n, rows):
            unit = max(1, 16 // rows)
            return max(-(-n // unit), 2) * unit

        self.jc = padded(self.bc + 3, self.rc)
        self.j1 = padded(26, self.rc)
        self.j2 = self.jc - self.j1
        thin = self.rc < 8
        self.fwd_rows = 256 if thin else FWD_ROWS
        self.ffn_rows = 256 if thin else FFN_ROWS
        self.bwd_rows = 256 if thin else BWD_ROWS
        f = FF // 128
        rest = 4 * D // 128
        up = padded(rest + 1, self.rw)
        self.jw = up + 2 * f
        self.word_cuts = (0, up, up + f, self.jw)
        self.word_order = list(range(rest)) + [self.bw] + [None] * (up - rest - 1)
        self.word_order += list(range(rest, rest + 2 * f))
        self.word_at = {j: p for p, j in enumerate(self.word_order) if j is not None}


def put(out, blocks, j, value):
    if value.shape[0] == 1:
        out[j : j + 1, :] = value
    else:
        out[pl.ds(j, value.shape[0], stride=blocks), :] = value


class Outs:
    def __init__(self, sem):
        self.sem, self.made = sem, []

    def start(self, src, dst):
        copy = pltpu.make_async_copy(src, dst, self.sem.at[len(self.made)])
        copy.start()
        self.made.append(copy)

    def wait(self):
        for copy in self.made:
            copy.wait()


def hooks(events):
    def hook(i, place):
        for (at, where), acts in events.items():
            if where == place:

                @pl.when(i == at)
                def _(acts=acts):
                    for act in acts:
                        act()

    return hook


def one_hot(condition):
    return condition.astype(F32).astype(BF16)


def slot_ints(codes, counts, langs, ints):
    wide = dot_tn(codes[...].astype(F32).astype(BF16), one_hot(iota((W, 128), 1) % W == iota((W, 128), 0)))
    wide = jnp.where(iota((LEN, 128), 0) % 8 == iota((LEN, 128), 1) // W, wide, 0.0)
    ints[0:16, :] = jnp.sum(wide.reshape(16, 8, 128), 1).astype(jnp.int32)
    group_row = iota((16, LEN), 0) == iota((16, LEN), 1) // 8
    by_slot = one_hot(iota((LEN, 128), 0) % 8 == iota((LEN, 128), 1) // W)
    by_word = one_hot(iota((LEN, 128), 0) % 8 == iota((LEN, 128), 1) % 8)
    count_rows = low(jnp.where(group_row, counts[...].astype(F32), 0.0))
    lang_rows = low(jnp.where(group_row, langs[...].astype(F32), 0.0))
    ints[16:32, :] = dot(lang_rows, by_slot).astype(jnp.int32)
    ints[32:48, :] = dot(count_rows, by_slot).astype(jnp.int32)
    ints[48:64, :] = dot(count_rows, by_word).astype(jnp.int32)


def mono(
    lay, stage,
    codes_in, counts_in, langs_in, length, cm_in, lookup_in, group_in, vec_in, wm_in, wvec_in, cot_in,
    y_out, cm_out, lookup_out, group_out, vec_out, wm_out, wvec_out,
    codes, counts, langs, cm, look, grp, vec, wm, wvec, cot,
    out_y, out_lookup, out_group, out_vec, out_wvec, exc, exw, ints,
    Gc, Gw, PBd, Wc, Wwt, out_cm, out_wm,
    xh1, n1s, qkvs, probs, os, xh2, n2s, acts, slopes, r2s, alphas, dr1s,
    Us, Ys, acct, sums, tsum,
    wide, thin_c, thin_w, thick,
    in_sem, out_sem, ag_send, ag_recv, rs_send, rs_recv, *recv,
):
    Y, Z, X = lay.sizes
    g = Grid(lay.sizes)
    PBc = Gc

    ins = [
        pltpu.make_async_copy(src, dst, in_sem.at[k])
        for k, (src, dst) in enumerate(
            (
                (cm_in, cm), (lookup_in, look), (group_in, grp), (vec_in, vec), (wm_in, wm),
                (wvec_in, wvec), (codes_in, codes), (counts_in, counts), (langs_in, langs), (cot_in, cot),
            )
        )
    ]
    for copy in ins:
        copy.start()
    ag = Copies(ag_send, ag_recv)
    cuts = [c * lay.rw for c in lay.word_cuts]
    gc = gather_pair(g, Gc, ag, 0, Gc.shape[4])
    gu = gather_pair(g, Gw, ag, 0, cuts[2])
    gd = gather_pair(g, Gw, ag, cuts[2], cuts[3])
    g.greet()
    for copy in ins[0:4]:
        copy.wait()
    exc[...] = jnp.zeros(exc.shape, F32)
    exc[:, 0 : 2 * 128] = look[...].astype(F32)
    exc[:, 256 : 256 + LANGS] = grp[...].astype(F32)
    exc[:, 256 + LANGS : 256 + LANGS + 5] = vec[...].astype(F32)
    order_c = list(range(lay.bc + 3)) + [None] * (lay.jc - lay.bc - 3)
    place_own(Gc.at[g.me], cm, out_cm, exc, lay.rc, lay.bc, order_c)
    g.met()
    gc.step1()
    for copy in ins[4:6]:
        copy.wait()
    exw[...] = dot_tn(wvec[...], one_hot(iota((4, 128), 0) == iota((4, 128), 1)))
    place_own(Gw.at[g.me], wm, out_wm, exw, lay.rw, lay.bw, lay.word_order)
    gu.step1()
    gd.step1()
    for copy in ins[6:9]:
        copy.wait()
    slot_ints(codes, counts, langs, ints)
    gc.step2()
    gc.step3()
    gc.step4()
    gu.step2()
    gc.step5()
    gc.finish()
    gu.step3()
    gd.step2()
    assemble(Gc, Wc, lay.rc, order_c, wide, thin_c)

    eye = (iota((16, 128), 0) == iota((16, 128), 1)).astype(F32).astype(BF16)
    rows_c = dot_nt(eye, Wc[:, (lay.bc + 2) * 128 : (lay.bc + 3) * 128])
    gain1, shift1, gain2, shift2 = (rows_c[8 + k : 9 + k] for k in range(4))
    query = rows_c[12:13]
    table_low = low(jnp.where(iota((16, C), 0) < LANGS, rows_c, 0.0))
    lookup = slice(lay.bc * 128, (lay.bc + 2) * 128)
    AQ, AO = slice(0, 3 * C), slice(3 * C, 4 * C)
    AU, AD = slice(4 * C, 4 * C + CM), slice(4 * C + CM, 4 * C + 2 * CM)
    PK, PV = slice(4 * C + 2 * CM, 5 * C + 2 * CM), slice(5 * C + 2 * CM, 6 * C + 2 * CM)
    PR = slice(6 * C + 2 * CM, 6 * C + 2 * CM + D)

    lane = iota((1, 128), 1)
    lane_word = lane // W
    word_rows = [(lane_word == w).astype(F32).astype(BF16) for w in range(8)]
    heads = head_rows(BF16)
    head_of = iota((128, C), 0) % 32 // 8 == iota((128, C), 1) // HD
    pq_rows = jnp.where(head_of, query * 0.125, 0.0)
    score_map = dot_nt(low(pq_rows), Wc[:, PK])
    map_hi = low(score_map)
    map_lo = low(score_map - map_hi.astype(F32))
    key_row = iota((1, W, 1), 1)
    pool_own = iota((128, 128), 0) // W == iota((128, 128), 1) % 8
    pool_slot = iota((128, 128), 0) % W

    def onehots(i, groups):
        parts = []
        for k in range(groups):
            r = i * groups + k
            codes = ints[pl.ds(r, 1), :]
            langs = ints[pl.ds(16 + r, 1), :]
            a = (iota((VOCAB, 128), 0) == codes).astype(F32).astype(BF16)
            b = (iota((16, 128), 0) == langs).astype(F32).astype(BF16)
            parts.append(jnp.concatenate([a, b], 0))
        return parts

    GF = lay.fwd_rows // 128

    hook_f = hooks({
            (0, 2): [gu.step4],
            (0, 4): [gd.step3],
            (1, 3): [gu.step5, gd.step4],
        })

    def forward(i, _):
        rows = pl.ds(pl.multiple_of(i * lay.fwd_rows, lay.fwd_rows), lay.fwd_rows)
        table = jnp.concatenate([Wc[:, lookup], table_low], 0)
        e = jnp.concatenate([dot_tn(h, table) for h in onehots(i, GF)], 0)
        xhat, scale1 = norm_stats(e)
        n1 = low(xhat * gain1 + shift1)
        xh1[rows, :] = low(xhat)
        n1s[rows, :] = n1
        qkv = low(dot(n1, Wc[:, AQ]))
        qkvs[rows, :] = qkv
        hook_f(i, 0)
        mixed = []
        for k in range(GF):
            visible = key_row < ints[pl.ds(32 + i * GF + k, 1), :].reshape(1, 1, 128)
            pair_out = []
            for p in range(2):
                q, kk, v = (
                    qkv[k * 128 : (k + 1) * 128, b * C + p * 128 : b * C + (p + 1) * 128]
                    for b in range(3)
                )
                s = own_word(dot_nt(head_stack(kk, heads), q), lane_word) * 0.125
                s = jnp.where(visible, s, NEGATIVE)
                s = jnp.exp(s - jnp.max(s, 1, keepdims=True))
                prob = s / jnp.sum(s, 1, keepdims=True)
                probs[i * GF + k, 2 * p : 2 * p + 2] = prob
                pair_out.append(dot_tn(spread_words(low(prob), word_rows), head_stack(v, heads)))
            mixed.append(jnp.concatenate(pair_out, 1))
        o = low(jnp.concatenate(mixed, 0))
        os[rows, :] = o
        hook_f(i, 1)
        r1 = e + dot(o, Wc[:, AO])
        xhat, scale2 = norm_stats(r1)
        n2 = low(xhat * gain2 + shift2)
        xh2[rows, :] = low(xhat)
        n2s[rows, :] = n2
        alphas[rows, 64:65] = scale1
        alphas[rows, 65:66] = scale2
        hook_f(i, 2)
        value, slope = gelu_both(dot(n2, Wc[:, AU]))
        act = low(value)
        acts[rows, :] = act
        slopes[rows, :] = low(slope)
        r2 = low(r1 + dot_nt(act, Wc[:, AD]))
        r2s[rows, :] = r2
        hook_f(i, 3)
        for k in range(GF):
            r = i * GF + k
            own = r2[k * 128 : (k + 1) * 128]
            s = dot_nt(own, map_hi) + dot_nt(own, map_lo)
            seen = pool_own & (pool_slot < ints[pl.ds(48 + r, 1), :])
            s = jnp.where(seen, s, NEGATIVE)
            s = jnp.where(seen, jnp.exp(s - jnp.max(s, 0, keepdims=True)), 0.0)
            alpha = s / jnp.sum(s, 0, keepdims=True)
            alphas[pl.ds(pl.multiple_of(r * 128, 128), 128), 0:32] = alpha[:, :32]
            u = dot_tn(low(alpha)[:, :32], own)
            for h in range(CH):
                Us[h, pl.ds(pl.multiple_of(r * 8, 8), 8), :] = u[8 * h : 8 * h + 8]
        hook_f(i, 4)
        return 0

    lax.fori_loop(0, LEN * W // lay.fwd_rows, forward, 0)

    head_c = [iota((1, C), 1) // HD == h for h in range(CH)]
    pooled = sum(jnp.where(head_c[h], dot(low(Us[h]), Wc[:, PV]), 0.0) for h in range(CH))
    pooled_low = low(pooled)
    w_in = dot(pooled_low, Wc[:, PR])

    gu.finish()
    if lay.rw < 16:
        gd.finish()
    if lay.rw >= 16:

        def wcols(lo, hi):
            return jnp.concatenate(
                [
                    Gw[:, :, :, :, p * lay.rw : (p + 1) * lay.rw, :].reshape(D, 128)
                    for p in [lay.word_at[j] for j in range(lo // 128, hi // 128)]
                ],
                1,
            )

    else:
        assemble(Gw, Wwt, lay.rw, lay.word_order, wide, thin_w)

        def wcols(lo, hi):
            return Wwt[:, lo:hi]

    rows_w = dot_nt(eye, wcols(D_COLS, D_COLS + 128))
    f1, c1, f2, c2 = (rows_w[k : k + 1] for k in range(4))
    BQ, BO, BU, BD = (0, 3 * D), (3 * D, 4 * D), (4 * D, 4 * D + FF), (4 * D + FF, D_COLS)
    NP = H // 2

    xhat1, sc1 = norm_stats(w_in)
    m1 = low(xhat1 * f1 + c1)
    qkv = low(dot(m1, wcols(*BQ)))
    key = iota((1, 128, 1), 1)
    seen_word = (key <= iota((1, 1, 128), 2)) & (key < length[0])
    pw, kst, qst, vst, mix = [], [], [], [], []
    for p in range(NP):
        q, kk, v = (qkv[:, b * D + p * 128 : b * D + (p + 1) * 128] for b in range(3))
        kst.append(head_stack(kk, heads))
        qst.append(head_stack(q, heads))
        vst.append(head_stack(v, heads))
        s = dot_nt(kst[p], q).reshape(2, 128, 128) * 0.125
        s = jnp.where(seen_word, s, NEGATIVE)
        s = jnp.exp(s - jnp.max(s, 1, keepdims=True))
        pw.append(s / jnp.sum(s, 1, keepdims=True))
        mix.append(dot_tn(low(pw[p]).reshape(256, 128), vst[p]))
    ow = low(jnp.concatenate(mix, 1))
    x = w_in + dot(ow, wcols(*BO))
    xhat2, sc2 = norm_stats(x)
    m2 = low(xhat2 * f2 + c2)
    value, slope = gelu_both(dot(m2, wcols(*BU)))
    aw = low(value)
    ins[9].wait()
    gy = cot[...]
    dy = gy.astype(F32)
    rw = lay.rw
    unit_w = max(1, 16 // rw)
    waiting = {}

    def put_w(at, blocks):
        waiting.update({at + k: b for k, b in enumerate(blocks)})
        for first in range(0, lay.jw, unit_w):
            ready = range(first, first + unit_w)
            if all(j in waiting for j in ready):
                some = [waiting.pop(j) for j in ready]
                if rw >= 16 and first >= lay.word_cuts[2]:
                    pack_blocks(PBd, first - lay.word_cuts[2], some, rw, wide, thick)
                else:
                    pack_blocks(Gw, first, some, rw, wide, thick)

    rs = Copies(rs_send, rs_recv)
    land = list(recv)
    first_d = 0 if rw >= 16 else cuts[2]
    cut1 = lay.j1 * lay.rc
    w1 = scatter_pair(g, PBd if rw >= 16 else Gw, land, rs, first_d, first_d + cuts[3] - cuts[2])
    w2 = scatter_pair(g, Gw, land, rs, cuts[1], cuts[2])
    w3 = scatter_pair(g, Gw, land, rs, 0, cuts[1])
    s1 = scatter_pair(g, Gc, land, rs, 0, cut1)
    s2 = scatter_pair(g, Gc, land, rs, cut1, Gc.shape[4])
    if rw < 16:
        gu.drain()
        gd.drain()
    at = lay.word_cuts[2]
    pass
    for k in range(0, FF, 512):
        put_w(at + k // 128, columns(dot_tn(gy, aw[:, k : k + 512])))
    w1.step1()
    gd.step5()
    w1.step2()
    if rw >= 16:
        gd.finish()
        gu.drain()
        gd.drain()
    out_y[...] = low(x + dot_nt(aw, wcols(*BD)))
    outs = Outs(out_sem)
    outs.start(out_y, y_out)
    gzw = low(slope * dot(gy, wcols(*BD)))
    pass
    dm2 = dot_nt(gzw, wcols(*BU))
    at = lay.word_cuts[1]
    for k in range(0, FF, 512):
        put_w(at + k // 128, columns(dot_tn(m2, gzw[:, k : k + 512])))
    w2.step1()
    pass
    gf2 = jnp.sum(dm2 * xhat2, 0, keepdims=True)
    gc2 = jnp.sum(dm2, 0, keepdims=True)
    dx = dy + norm_back(dm2, xhat2, sc2, f2)
    gx = low(dx)
    gow = low(dot_nt(gx, wcols(*BO)))
    put_w(BO[0] // 128, columns(dot_tn(ow, gx)))
    pass
    gq, gk, gv = [], [], []
    for p in range(NP):
        go = gow[:, p * 128 : (p + 1) * 128]
        dp = dot_nt(vst[p], go).reshape(2, 128, 128)
        inner = jnp.sum(pw[p] * dp, 1, keepdims=True)
        gs = low(pw[p] * (dp - inner)).reshape(256, 128)
        gq.append(dot_tn(gs, kst[p]) * 0.125)
        gk.append(dot(side_by_side(gs, 128), qst[p]) * 0.125)
        gv.append(dot(side_by_side(low(pw[p]).reshape(256, 128), 128), head_stack(go, heads)))
    tg = low(jnp.concatenate(gq + gk + gv, 1))
    dm1 = dot_nt(tg, wcols(*BQ))
    for k in range(0, 3 * D, 512):
        put_w(k // 128, columns(dot_tn(m1, tg[:, k : k + 512])))
    gf1 = jnp.sum(dm1 * xhat1, 0, keepdims=True)
    gc1 = jnp.sum(dm1, 0, keepdims=True)
    dw = dx + norm_back(dm1, xhat1, sc1, f1)
    vec_rows = low(jnp.concatenate([gf1, gc1, gf2, gc2, jnp.zeros((12, D), F32)], 0))
    at = lay.word_at[lay.bw]
    put_w(at, [dot_tn(vec_rows, eye)] + [jnp.zeros((D, 128), F32)] * (lay.word_cuts[1] - at - 1))
    w3.step1()
    w2.step2()

    gc.drain()
    gw = low(dw)
    dpool = dot_nt(gw, Wc[:, PR])
    pass
    dp4 = jnp.concatenate([low(jnp.where(head_c[h], dpool, 0.0)) for h in range(CH)], 0)
    Ys[...] = dot_nt(dp4, Wc[:, PV]).reshape(CH, LEN, C)
    for ref in (acct, sums, tsum):
        ref[...] = jnp.zeros(ref.shape, F32)

    map32 = map_hi[:32]
    GB = lay.bwd_rows // 128

    GP = lay.ffn_rows // 128

    def back_ffn(i, _):
        rows = pl.ds(pl.multiple_of(i * lay.ffn_rows, lay.ffn_rows), lay.ffn_rows)
        parts = []
        for k in range(GP):
            r = i * GP + k
            own = r2s[pl.ds(pl.multiple_of(r * 128, 128), 128), :]
            alpha = alphas[pl.ds(pl.multiple_of(r * 128, 128), 128), 0:32]
            yg = low(
                jnp.concatenate(
                    [Ys[h, pl.ds(pl.multiple_of(r * 8, 8), 8), :] for h in range(CH)], 0
                )
            )
            da = dot_nt(own, yg)
            dr = low(alpha * (da - jnp.sum(alpha * da, 0, keepdims=True)))
            tsum[...] += dot_tn(dr, own)
            parts.append(dot(low(alpha), yg) + dot(dr, map32))
        dr2 = jnp.concatenate(parts, 0)
        g2 = low(dr2)
        hook_1(i, 0)
        r2s[rows, :] = g2
        hook_1(i, 1)
        gz = low(slopes[rows, :].astype(F32) * dot(g2, Wc[:, AD]))
        slopes[rows, :] = gz
        hook_1(i, 2)
        dn = dot_nt(gz, Wc[:, AU])
        xhat = xh2[rows, :].astype(F32)
        sums[2:3, :] += jnp.sum(dn * xhat, 0, keepdims=True)
        sums[3:4, :] += jnp.sum(dn, 0, keepdims=True)
        dr1 = dr2 + norm_back(dn, xhat, alphas[rows, 65:66], gain2)
        dr1s[rows, :] = dr1
        xh2[rows, :] = low(dr1)
        hook_1(i, 3)
        return 0

    def place_w(j, value):
        j = lay.word_order[j]
        if j is None:
            return
        if j < lay.bw:
            put(out_wm, lay.bw, j, value)
        else:
            pick = (iota((8, 128), 0) == iota((8, 128), 1)).astype(F32)
            out_wvec[...] = lax.dot_general(
                pick, value, (((1,), (1,)), ((), ())),
                precision=lax.Precision.HIGHEST, preferred_element_type=F32,
            )[0:4]

    def place_1(j, value):
        put(out_cm, lay.bc, 8 + j if j < 24 else j - 18, value)

    def place_2(j, value):
        if j < 6:
            put(out_cm, lay.bc, j, value)
        elif j < 8:
            out_lookup[:, (j - 6) * 128 : (j - 5) * 128] = value
        else:
            out_group[...] = value[:, 0:LANGS]
            out_vec[...] = value[:, LANGS : LANGS + 5]

    def fin_w1():
        w1.finish(lambda j, v: place_w(lay.word_cuts[2] + j, v), rw, first_d, FF // 128)

    def fin_w2():
        w2.finish(lambda j, v: place_w(lay.word_cuts[1] + j, v), rw, cuts[1], FF // 128)

    def fin_w3():
        w3.finish(place_w, rw, 0, lay.word_cuts[1])

    def fin_s1():
        s1.finish(place_1, rc, 0, 26)

    def fin_s2():
        s2.finish(place_2, rc, cut1, 9)

    hook_1 = hooks({
            (1, 0): [w1.step3, w3.step2],
        })
    lax.fori_loop(0, LEN * W // lay.ffn_rows, back_ffn, 0)

    grad_pr = dot_tn(pooled_low, gw)
    grad_pv = dot_tn(low(Us[...]).reshape(CH * LEN, C), dp4)
    t_low = low(tsum[...])
    grad_pk = dot_tn(t_low, low(pq_rows[:32]))
    rc = lay.rc
    pad1 = [jnp.zeros((C, 128), F32)] * (lay.j1 - 26)
    pack_blocks(
        PBc,
        0,
        columns(dot_tn(n2s[...], slopes[...])) + columns(dot_tn(r2s[...], acts[...])) + columns(grad_pk) + columns(grad_pv)
        + columns(grad_pr) + columns(dot_tn(os[...], xh2[...])) + pad1,
        rc,
        wide,
        thick,
    )
    s1.step1()
    w1.step4()
    w2.step3()
    gpq = dot(t_low, Wc[:, PK]) * 0.125
    gpq = jnp.sum(
        jnp.where(iota((32, C), 0) // 8 == iota((32, C), 1) // HD, gpq, 0.0), 0, keepdims=True
    )

    def back_attention(i, _):
        rows = pl.ds(pl.multiple_of(i * lay.bwd_rows, lay.bwd_rows), lay.bwd_rows)
        dr1 = dr1s[rows, :]
        go = low(dot_nt(xh2[rows, :], Wc[:, AO]))
        hook_2(i, 0)
        qkv = qkvs[rows, :]
        grads = [[], [], []]
        for k in range(GB):
            part = [[], [], []]
            for p in range(2):
                at = slice(k * 128, (k + 1) * 128)
                q, kk, v = (
                    qkv[at, b * C + p * 128 : b * C + (p + 1) * 128] for b in range(3)
                )
                gop = go[at, p * 128 : (p + 1) * 128]
                prob = probs[i * GB + k, 2 * p : 2 * p + 2]
                dp = own_word(dot_nt(head_stack(v, heads), gop), lane_word)
                gs = low(prob * (dp - jnp.sum(prob * dp, 1, keepdims=True)))
                gs = spread_words(gs, word_rows)
                pb = spread_words(low(prob), word_rows)
                part[0].append(dot_tn(gs, head_stack(kk, heads)) * 0.125)
                part[1].append(dot(side_by_side(gs, 128), head_stack(q, heads)) * 0.125)
                part[2].append(dot(side_by_side(pb, 128), head_stack(gop, heads)))
            for b in range(3):
                grads[b].append(jnp.concatenate(part[b], 1))
        hook_2(i, 1)
        tg = low(jnp.concatenate([jnp.concatenate(b, 0) for b in grads], 1))
        qkvs[rows, :] = tg
        dn = dot_nt(tg, Wc[:, AQ])
        hook_2(i, 2)
        xhat = xh1[rows, :].astype(F32)
        sums[0:1, :] += jnp.sum(dn * xhat, 0, keepdims=True)
        sums[1:2, :] += jnp.sum(dn, 0, keepdims=True)
        ge = low(dr1 + norm_back(dn, xhat, alphas[rows, 64:65], gain1))
        acct[...] += dot(jnp.concatenate(onehots(i, GB), 1), ge)
        hook_2(i, 3)
        return 0

    hook_2 = hooks({
            (0, 2): [w3.step3],
            (0, 3): [s1.step2, w2.step4],
        })
    lax.fori_loop(0, LEN * W // lay.bwd_rows, back_attention, 0)

    pass
    small = low(jnp.concatenate([acct[VOCAB : VOCAB + 8], sums[0:4], gpq, jnp.zeros((3, C), F32)], 0))
    pad2 = [jnp.zeros((C, 128), F32)] * (lay.j2 - 9)
    pack_blocks(
        PBc,
        lay.j1,
        columns(dot_tn(n1s[...], qkvs[...])) + columns(acct[0:VOCAB, :])
        + [dot_tn(small, eye)] + pad2,
        rc,
        wide,
        thick,
    )
    s2.step1()
    w3.step4()
    s1.step3()
    fin_w1()
    s2.step2()
    s1.step4()
    s2.step3()
    s2.step4()
    fin_w3()
    fin_w2()
    outs.start(out_wm, wm_out)
    outs.start(out_wvec, wvec_out)
    fin_s1()
    fin_s2()
    outs.start(out_cm, cm_out)
    outs.start(out_lookup, lookup_out)
    outs.start(out_group, group_out)
    outs.start(out_vec, vec_out)
    for part in (w1, w2, w3, s1, s2):
        part.drain()
    outs.wait()


def hand_over(*refs):
    n = 7
    ins, outs, held, sems = refs[:n], refs[n : 2 * n], refs[2 * n : 3 * n], refs[-1]
    first = [pltpu.make_async_copy(ins[k], held[k], sems.at[k]) for k in range(n)]
    then = [pltpu.make_async_copy(held[k], outs[k], sems.at[n + k]) for k in range(n)]
    for copy in first:
        copy.start()
    for k in range(n):
        first[k].wait()
        then[k].start()
    for copy in then:
        copy.wait()


def shards(
    sizes,
    char_codes,
    char_counts,
    word_groups,
    valid_words,
    char_matrix,
    char_lookup,
    group_lookup,
    char_vectors,
    word_matrix,
    word_vectors,
    cotangent,
):
    lay = Layout(sizes)
    Y, Z, X = sizes
    rows = LEN * W
    rows_c, rows_w = lay.jc * lay.rc, lay.jw * lay.rw
    rows_1 = lay.j1 * lay.rc
    nag = ag_count(Y, Z, X) * 6
    nrs = rs_count(Y, Z, X) * 10
    dma = pltpu.SemaphoreType.DMA

    def vm(shape, dtype):
        return pltpu.VMEM(shape, dtype)

    def like(a):
        return pltpu.VMEM(a.shape, a.dtype)

    ins = (
        char_codes[0].T,
        char_counts,
        word_groups,
        valid_words,
        char_matrix,
        char_lookup,
        group_lookup,
        char_vectors,
        word_matrix,
        word_vectors.T,
        cotangent[0],
    )
    outs = [
        jax.ShapeDtypeStruct((LEN, D), BF16),
        jax.ShapeDtypeStruct(char_matrix.shape, F32),
        jax.ShapeDtypeStruct(char_lookup.shape, F32),
        jax.ShapeDtypeStruct(group_lookup.shape, F32),
        jax.ShapeDtypeStruct(char_vectors.shape, F32),
        jax.ShapeDtypeStruct(word_matrix.shape, F32),
        jax.ShapeDtypeStruct(word_vectors.shape[::-1], F32),
    ]
    scratch = [like(a) for k, a in enumerate(ins) if k != 3]
    scratch += [like(outs[k]) for k in (0, 2, 3, 4, 6)]
    scratch += [
        vm((lay.rc, 3 * 128), F32),
        vm((lay.rw, 128), F32),
        vm((64, 128), jnp.int32),
        vm(lay.lead + (rows_c, 128), BF16),
        vm(lay.lead + (rows_w, 128), BF16),
        vm(lay.lead + (FF // 128 * lay.rw, 128) if lay.rw >= 16 else (16, 128), BF16),
        vm((C, (lay.bc + 3) * 128), BF16),
        vm((D, (lay.bw + 1) * 128) if lay.rw < 16 else (16, 128), BF16),
        like(outs[1]),
        like(outs[5]),
        vm((rows, C), BF16),
        vm((rows, C), BF16),
        vm((rows, 3 * C), BF16),
        vm((16, CH, W, 128), F32),
        vm((rows, C), BF16),
        vm((rows, C), BF16),
        vm((rows, C), BF16),
        vm((rows, CM), BF16),
        vm((rows, CM), BF16),
        vm((rows, C), BF16),
        vm((rows, 128), F32),
        vm((rows, C), F32),
        vm((CH, LEN, C), F32),
        vm((CH, LEN, C), F32),
        vm((VOCAB + 16, C), F32),
        vm((8, C), F32),
        vm((32, C), F32),
        vm((lay.devices * 16 if lay.rc < 8 else 8, 128), F32),
        vm((Z * X * lay.rc, 128), F32),
        vm((Z * X * lay.rw, 128), F32),
        vm((D if lay.rc < 8 else 8, 128), F32),
        dma((10,)),
        dma((7,)),
        dma((nag,)),
        dma((nag,)),
        dma((nrs,)),
        dma((nrs,)),
    ]
    at = [c * lay.rw for c in lay.word_cuts]
    for lo, hi in ((at[2], at[3]), (at[1], at[2]), (at[0], at[1]), (0, rows_1), (rows_1, rows_c)):
        scratch += scatter_pair_scratch(sizes, lo, hi)
    anywhere = pl.BlockSpec(memory_space=pl.ANY)
    in_specs = [anywhere] * 11
    in_specs[3] = pl.BlockSpec(memory_space=pltpu.SMEM)
    got = pl.pallas_call(
        functools.partial(mono, lay, STAGE),
        out_shape=outs,
        in_specs=in_specs,
        out_specs=[anywhere] * 7,
        scratch_shapes=scratch,
        compiler_params=pltpu.CompilerParams(
            collective_id=0, has_side_effects=True, vmem_limit_bytes=VMEM_LIMIT
        ),
        name="layer",
    )(*ins)
    got = pl.pallas_call(
        hand_over,
        out_shape=outs,
        in_specs=[anywhere] * 7,
        out_specs=[anywhere] * 7,
        scratch_shapes=[like(a) for a in outs] + [dma((14,))],
        name="hand_over",
    )(*got)
    return (got[0][None],) + tuple(got[1:6]) + (got[6].T,)


def solution(mesh):
    dp, fsdp = mesh.shape["dp"], mesh.shape["fsdp"]
    Y = dp // 2
    X = Y if fsdp % Y == 0 else 1
    sizes = (Y, fsdp // X, X)
    placed = (
        P(("dp", "fsdp"), None, None),
        P(("dp", "fsdp"), None),
        P(("dp", "fsdp"), None),
        P(("dp", "fsdp")),
        P(("dp", "fsdp"), None),
        P(("dp", "fsdp"), None),
        P(("dp", "fsdp"), None),
        P(("dp", "fsdp"), None),
        P(("dp", "fsdp"), None),
        P(("dp", "fsdp"), None),
        P(("dp", "fsdp"), None, None),
    )
    return jax.shard_map(
        functools.partial(shards, sizes),
        mesh=mesh,
        in_specs=placed,
        out_specs=(
            P(("dp", "fsdp"), None, None),
            P(("dp", "fsdp"), None),
            P(("dp", "fsdp"), None),
            P(("dp", "fsdp"), None),
            P(("dp", "fsdp"), None),
            P(("dp", "fsdp"), None),
            P(("dp", "fsdp"), None),
        ),
        check_vma=False,
    )
```

```python
import functools

import jax
import jax.numpy as jnp
from jax import lax
from jax.experimental import pallas as pl
from jax.experimental.pallas import tpu as pltpu
from jax.sharding import PartitionSpec as P

C = 256
HD = 64
CH = 4
CM = 1024
D = 512
H = 8
FF = 2048
W = 16
VOCAB = 256
LANGS = 8
LEN = 128
C_COLS = 6 * C + 2 * CM + D
D_COLS = 4 * D + 2 * FF
EPSILON = 1e-05
NEGATIVE = -1000000000.0
F32 = jnp.float32
BF16 = jnp.bfloat16
FWD_ROWS = 1024
BWD_ROWS = 1024
FFN_ROWS = 1024
VMEM_LIMIT = 63 << 20
STAGE = 0


MESH = pl.DeviceIdType.MESH
ALL = slice(None)


class Grid:
    def __init__(self, sizes):
        self.Y, self.Z, self.X = sizes
        dp, fs = lax.axis_index("dp"), lax.axis_index("fsdp")
        self.y, self.c = dp // 2, dp % 2
        self.z, self.x = fs // self.X, fs % self.X
        self.me = (self.y, self.c, self.z, self.x)
        self.ys = [(self.y + k) % self.Y for k in range(1, self.Y)]
        self.zs = [(self.z + k) % self.Z for k in range(1, self.Z)]
        self.xs = [(self.x + k) % self.X for k in range(1, self.X)]
        self.to_y = [self.at(y=y) for y in self.ys]
        self.to_z = [self.at(z=z) for z in self.zs]
        self.to_x = [self.at(x=x) for x in self.xs]
        self.to_c = self.at(c=1 - self.c)
        self.to = {"y": self.to_y, "z": self.to_z, "x": self.to_x}
        self.src = {
            "y": [(self.y + self.Y - k) % self.Y for k in range(1, self.Y)],
            "z": [(self.z + self.Z - k) % self.Z for k in range(1, self.Z)],
            "x": [(self.x + self.X - k) % self.X for k in range(1, self.X)],
        }
        self.off = {"y": self.ys, "z": self.zs, "x": self.xs}

    def at(self, y=None, c=None, z=None, x=None):
        y = self.y if y is None else y
        c = self.c if c is None else c
        z = self.z if z is None else z
        x = self.x if x is None else x
        return (y * 2 + c, z * self.X + x)

    def greet(self):
        barrier = pltpu.get_barrier_semaphore()
        self.partners = [self.to_c] + self.to_y + self.to_z + self.to_x
        for p in self.partners:
            pl.semaphore_signal(barrier, inc=1, device_id=p, device_id_type=MESH)

    def met(self):
        pl.semaphore_wait(pltpu.get_barrier_semaphore(), len(self.partners))


class Copies:
    def __init__(self, send, recv):
        self.send, self.recv, self.made = send, recv, []

    def plan(self, src, dst, to):
        self.made.append((src, dst, to))
        return len(self.made) - 1

    def make(self, i):
        src, dst, to = self.made[i]
        return pltpu.make_async_remote_copy(
            src_ref=src,
            dst_ref=dst,
            send_sem=self.send.at[i],
            recv_sem=self.recv.at[i],
            device_id=to,
            device_id_type=MESH,
        )

    def start(self, which):
        for i in which:
            self.make(i).start()

    def arrived(self, which):
        for i in which:
            self.make(i).wait_recv()

    def left(self, which):
        for i in which:
            self.make(i).wait_send()


def ag_count(Y, Z, X):
    n = max(Z - 1, X - 1, Y - 1)
    return 6 * n + 1 + 2 * n * n


class Gather:
    def __init__(self, g, G, copies, lo, hi, order):
        self.copies = copies
        first = len(copies.made)
        one, two, three = order
        rows = slice(lo, hi)

        def slot(**at):
            v = {"y": g.y, "z": g.z, "x": g.x, **at}
            return (v["y"], g.c, v["z"], v["x"], rows)

        def plan(to, **at):
            return copies.plan(G.at[slot(**at)], G.at[slot(**at)], to)

        self.first = [plan(to) for to in g.to[one]]
        self.own2 = [plan(to) for to in g.to[two]]
        self.own3 = [plan(to, **{two: ALL}) for to in g.to[three]]
        self.rest2 = [[plan(to, **{one: v}) for to in g.to[two]] for v in g.src[one]]
        self.rest3 = [[plan(to, **{one: v, two: ALL}) for to in g.to[three]] for v in g.src[one]]
        self.core1 = [plan(g.to_c)]
        self.core2 = [plan(g.to_c, **{two: w}) for w in g.src[two]]
        self.core4 = [[plan(g.to_c, **{one: v, two: ALL})] for v in g.src[one]]
        self.core5 = [plan(g.to_c, **{one: ALL, two: ALL, three: u}) for u in g.src[three]]
        self.mine = range(first, len(copies.made))

    def step1(self):
        self.copies.start(self.first + self.own2 + self.core1)

    def step2(self):
        self.copies.arrived(self.own2)
        self.copies.start(self.own3 + self.core2)

    def step3(self):
        for k, which in enumerate(self.rest2):
            self.copies.arrived(self.first[k : k + 1])
            self.copies.start(which)

    def step4(self):
        for k, which in enumerate(self.rest3):
            self.copies.arrived(self.rest2[k])
            self.copies.start(which + self.core4[k])

    def step5(self):
        self.copies.arrived(self.own3)
        for which in self.rest3:
            self.copies.arrived(which)
        self.copies.start(self.core5)

    def finish(self):
        self.copies.arrived(self.core1 + self.core2 + self.core5)
        for which in self.core4:
            self.copies.arrived(which)

    def drain(self):
        self.copies.left(self.mine)


def rs_count(Y, Z, X):
    return 1 + (Z - 1) + ((X - 1) + (Y - 1)) * Z


def rs_scratch(sizes, rows, order):
    n = dict(zip("yzx", sizes))
    left = dict(n)
    shapes = [pltpu.VMEM(sizes + (rows, 128), BF16)]
    for axis in order:
        left[axis] = 1
        shapes.append(pltpu.VMEM((n[axis] - 1, left["y"], left["z"], left["x"], rows, 128), BF16))
    return shapes


def add_into(dst, srcs):
    lead = dst.shape[:-2]
    total = 1
    for n in lead:
        total *= n
    some = next(n for n in (16, 8, 4, 2, 1) if total % n == 0)

    def body(i, _):
        for part in range(some):
            idx, r = [], i * some + part
            for n in reversed(lead):
                idx.append(r % n)
                r = r // n
            idx = tuple(reversed(idx))
            if len(srcs) == 1:
                dst[idx] = dst[idx] + srcs[0][idx]
                continue
            acc = dst[idx].astype(F32)
            for s in srcs:
                acc = acc + s[idx].astype(F32)
            dst[idx] = acc.astype(BF16)
        return 0

    lax.fori_loop(0, total // some, body, 0)


class Scatter:
    def __init__(self, g, PB, recv, copies, lo, hi, order):
        self.g, self.PB, self.copies, self.recv = g, PB, copies, recv
        self.lo, self.hi = lo, hi
        first = len(copies.made)
        rows = slice(lo, hi)
        one, two, three = order
        me = {"y": g.y, "z": g.z, "x": g.x}
        own = {axis: pl.ds(v, 1) for axis, v in me.items()}

        def slot(c, **at):
            v = {"y": ALL, "z": ALL, "x": ALL, **at}
            return (v["y"], c, v["z"], v["x"], rows)

        def land(n, k, v):
            at = {"y": ALL, "z": ALL, "x": ALL, three: pl.ds(v, 1)}
            return recv[n].at[k, at["y"], at["z"], at["x"]]

        def hop(n, axis, v, **at):
            return [
                copies.plan(PB.at[slot(g.c, **{**at, axis: pl.ds(u, 1), three: pl.ds(v, 1)})], land(n, k, v), to)
                for k, (u, to) in enumerate(zip(g.off[axis], g.to[axis]))
            ]

        self.core = [copies.plan(PB.at[slot(1 - g.c)], recv[0], g.to_c)]
        self.places = g.off[three] + [me[three]]
        self.hop1 = [hop(1, one, v) for v in self.places]
        self.hop2 = [hop(2, two, v, **{one: own[one]}) for v in self.places]
        self.hop3 = [
            copies.plan(PB.at[slot(g.c, **{**own, three: pl.ds(v, 1)})], recv[3].at[k], to)
            for k, (v, to) in enumerate(zip(g.off[three], g.to[three]))
        ]
        self.sum0 = PB.at[slot(g.c)]
        self.sum1 = [PB.at[slot(g.c, **{one: own[one], three: pl.ds(v, 1)})] for v in self.places]
        self.sum2 = [PB.at[slot(g.c, **{**own, three: pl.ds(v, 1)})] for v in self.places]
        self.from1 = [[land(1, k, v) for k in range(len(g.off[one]))] for v in self.places]
        self.from2 = [[land(2, k, v) for k in range(len(g.off[two]))] for v in self.places]
        self.mine = range(first, len(copies.made))

    def step1(self):
        self.copies.start(self.core)

    def step2(self):
        self.copies.arrived(self.core)
        add_into(self.sum0, [self.recv[0]])
        for which in self.hop1:
            self.copies.start(which)

    def step3(self):
        for k, which in enumerate(self.hop1):
            self.copies.arrived(which)
            add_into(self.sum1[k], self.from1[k])
            self.copies.start(self.hop2[k])

    def step4(self):
        for k, which in enumerate(self.hop2[:-1]):
            self.copies.arrived(which)
            add_into(self.sum2[k], self.from2[k])
            self.copies.start(self.hop3[k : k + 1])

    def finish(self, place, rows, base, count):
        self.copies.arrived(self.hop2[-1] + self.hop3)
        size = max(rows, 16)
        for row in range(self.lo, self.hi, size):
            r = slice(row - self.lo, row - self.lo + size)
            acc = self.PB[self.g.me + (slice(row, row + size),)].astype(F32)
            for part in self.from2[-1]:
                acc = acc + part[0, 0, 0, r].astype(F32)
            for k in range(len(self.hop3)):
                acc = acc + self.recv[3][k, 0, 0, 0, r].astype(F32)
            for u in range(size // rows):
                j = (row - base) // rows + u
                if j < count:
                    place(j, acc[u * rows : (u + 1) * rows])

    def drain(self):
        self.copies.left(self.mine)


class Pair:
    def __init__(self, parts):
        self.parts = parts

    def all(self, name, *args):
        for part in self.parts:
            getattr(part, name)(*args)

    def step1(self):
        self.all("step1")

    def step2(self):
        self.all("step2")

    def step3(self):
        self.all("step3")

    def step4(self):
        self.all("step4")

    def step5(self):
        self.all("step5")

    def finish(self, *args):
        self.all("finish", *args)

    def drain(self):
        self.all("drain")


def halves(lo, hi):
    mid = lo + (hi - lo + 31) // 32 * 16
    return [(lo, mid), (mid, hi)] if mid < hi else [(lo, hi)]


def gather_pair(g, G, copies, lo, hi):
    orders = ("zxy", "zyx")
    return Pair([Gather(g, G, copies, *cut, o) for cut, o in zip(halves(lo, hi), orders)])


SUM_ORDERS = ("yxz", "xyz")


def scatter_pair(g, PB, recv, copies, lo, hi):
    parts = []
    for cut, o in zip(halves(lo, hi), SUM_ORDERS):
        parts.append(Scatter(g, PB, recv[:4], copies, *cut, o))
        del recv[:4]
    return Pair(parts)


def scatter_pair_scratch(sizes, lo, hi):
    out = []
    for (a, b), o in zip(halves(lo, hi), SUM_ORDERS):
        out += rs_scratch(sizes, b - a, o)
    return out


def dot(a, b):
    return lax.dot_general(a, b, (((1,), (0,)), ((), ())), preferred_element_type=F32)


def dot_nt(a, b):
    return lax.dot_general(a, b, (((1,), (1,)), ((), ())), preferred_element_type=F32)


def dot_tn(a, b):
    return lax.dot_general(a, b, (((0,), (0,)), ((), ())), preferred_element_type=F32)


def low(v):
    return v.astype(BF16)


def norm_stats(x):
    centre = x - jnp.mean(x, -1, keepdims=True)
    spread = jnp.mean(centre * centre, -1, keepdims=True)
    scale = lax.rsqrt(spread + EPSILON)
    return centre * scale, scale


def norm_back(grad, xhat, scale, gain):
    inner = grad * gain
    first = jnp.mean(inner, -1, keepdims=True)
    second = jnp.mean(inner * xhat, -1, keepdims=True)
    return scale * (inner - first - xhat * second)


def gelu_both(z):
    sq = z * z
    t = jnp.tanh(z * (0.7978845608028654 + (0.7978845608028654 * 0.044715) * sq))
    h = 0.5 * z
    value = h + h * t
    slope = 0.5 + 0.5 * t + h * (1.0 - t * t) * (
        0.7978845608028654 + (3.0 * 0.7978845608028654 * 0.044715) * sq
    )
    return value, slope


def iota(shape, dim):
    return lax.broadcasted_iota(jnp.int32, shape, dim)


def head_rows(dtype):
    lane = iota((1, 128), 1)
    return [(lane // HD == h).astype(F32).astype(dtype) for h in range(2)]


def head_stack(block, heads):
    return jnp.concatenate([block * h for h in heads], 0)


def own_word(scores, lane_word):
    split = scores.reshape(2, 8, W, 128)
    out = split[:, 0]
    for w in range(1, 8):
        out = jnp.where(lane_word == w, split[:, w], out)
    return out


def spread_words(compact, word_rows):
    return jnp.concatenate([compact[h] * word_rows[w] for h in range(2) for w in range(8)], 0)


def side_by_side(stacked, rows):
    return jnp.concatenate([stacked[h * rows : (h + 1) * rows] for h in range(2)], 1)


def place_own(own, raw, staged, extra, rows, blocks, order):
    staged[...] = raw[...].astype(F32)
    unit = max(1, 16 // rows)

    def block(j):
        if j is None:
            return jnp.zeros((rows, 128), F32)
        if j < blocks:
            if rows == 1:
                return staged[j : j + 1, :]
            return staged[pl.ds(j, rows, stride=blocks), :]
        at = (j - blocks) * 128
        return extra[:, at : at + 128]

    for t in range(len(order) // unit):
        tile = jnp.concatenate([block(j) for j in order[t * unit : (t + 1) * unit]], 0)
        own[t * unit * rows : (t + 1) * unit * rows, :] = low(tile)


def assemble(G, Wd, rows, order, wide, thin):
    unit = max(1, 16 // rows)
    Y, two, Z, X = G.shape[:4]
    some = Z * X * rows

    def body(i, _):
        at = pl.ds(pl.multiple_of(i * some, 16), some)
        for t in range(len(order) // unit):
            tile = G[i // two, i % two, :, :, t * unit * rows : (t + 1) * unit * rows, :]
            tile = tile.reshape(Z * X, 16, 128).astype(F32)
            if rows < 8:
                wide[0 : Z * X * 16, :] = tile.reshape(Z * X * 16, 128)
            for u in range(unit):
                j = order[t * unit + u]
                if j is None:
                    continue
                if rows < 8:
                    for r in range(rows):
                        own = wide[pl.ds(u * rows + r, Z * X, stride=16), :]
                        thin[pl.ds(r, Z * X, stride=rows) if rows > 1 else ALL, :] = own
                    Wd[at, j * 128 : (j + 1) * 128] = low(thin[...])
                    continue
                Wd[at, j * 128 : (j + 1) * 128] = low(
                    tile[:, u * rows : (u + 1) * rows, :].reshape(some, 128)
                )
        return 0

    lax.fori_loop(0, Y * two, body, 0)


def pack_blocks(PB, at, blocks, rows, wide, thick):
    unit = max(1, 16 // rows)
    lead = PB.shape[:4]
    Y, two, Z, X = lead
    devices = Y * two * Z * X
    for t in range(len(blocks) // unit):
        row = (at + t * unit) * rows
        some = blocks[t * unit : (t + 1) * unit]
        if rows >= 8:
            parts = [b.reshape(devices, rows, 128) for b in some]
            tile = low(parts[0] if unit == 1 else jnp.concatenate(parts, 1))
            PB[:, :, :, :, row : row + unit * rows, :] = tile.reshape(lead + (unit * rows, 128))
            continue
        for k, b in enumerate(some):
            thick[0 : devices * rows, :] = b
            for r in range(rows):
                own = thick[pl.ds(r, devices, stride=rows) if rows > 1 else slice(0, devices), :]
                wide[pl.ds(k * rows + r, devices, stride=16), :] = own
        for i in range(Y * two):
            own = low(wide[i * Z * X * 16 : (i + 1) * Z * X * 16, :])
            PB[i // two, i % two, :, :, row : row + 16, :] = own.reshape(Z, X, 16, 128)


def columns(value):
    return [value[:, k : k + 128] for k in range(0, value.shape[1], 128)]


class Layout:
    def __init__(self, sizes):
        self.sizes = sizes
        Y, Z, X = sizes
        self.lead = (Y, 2, Z, X)
        self.devices = Y * 2 * Z * X
        self.rc = C // self.devices
        self.rw = D // self.devices
        self.bc = C_COLS // 128
        self.bw = D_COLS // 128

        def padded(n, rows):
            unit = max(1, 16 // rows)
            return max(-(-n // unit), 2) * unit

        self.jc = padded(self.bc + 3, self.rc)
        self.j1 = padded(26, self.rc)
        self.j2 = self.jc - self.j1
        thin = self.rc < 8
        self.fwd_rows = 256 if thin else FWD_ROWS
        self.ffn_rows = 256 if thin else FFN_ROWS
        self.bwd_rows = 256 if thin else BWD_ROWS
        f = FF // 128
        rest = 4 * D // 128
        up = padded(rest + 1, self.rw)
        self.jw = up + 2 * f
        self.word_cuts = (0, up, up + f, self.jw)
        self.word_order = list(range(rest)) + [self.bw] + [None] * (up - rest - 1)
        self.word_order += list(range(rest, rest + 2 * f))
        self.word_at = {j: p for p, j in enumerate(self.word_order) if j is not None}


def put(out, blocks, j, value):
    if value.shape[0] == 1:
        out[j : j + 1, :] = value
    else:
        out[pl.ds(j, value.shape[0], stride=blocks), :] = value


class Outs:
    def __init__(self, sem):
        self.sem, self.made = sem, []

    def start(self, src, dst):
        copy = pltpu.make_async_copy(src, dst, self.sem.at[len(self.made)])
        copy.start()
        self.made.append(copy)

    def wait(self):
        for copy in self.made:
            copy.wait()


def hooks(events):
    def hook(i, place):
        for (at, where), acts in events.items():
            if where == place:

                @pl.when(i == at)
                def _(acts=acts):
                    for act in acts:
                        act()

    return hook


def one_hot(condition):
    return condition.astype(F32).astype(BF16)


def slot_ints(codes, counts, langs, ints):
    wide = dot_tn(codes[...].astype(F32).astype(BF16), one_hot(iota((W, 128), 1) % W == iota((W, 128), 0)))
    wide = jnp.where(iota((LEN, 128), 0) % 8 == iota((LEN, 128), 1) // W, wide, 0.0)
    ints[0:16, :] = jnp.sum(wide.reshape(16, 8, 128), 1).astype(jnp.int32)
    group_row = iota((16, LEN), 0) == iota((16, LEN), 1) // 8
    by_slot = one_hot(iota((LEN, 128), 0) % 8 == iota((LEN, 128), 1) // W)
    by_word = one_hot(iota((LEN, 128), 0) % 8 == iota((LEN, 128), 1) % 8)
    count_rows = low(jnp.where(group_row, counts[...].astype(F32), 0.0))
    lang_rows = low(jnp.where(group_row, langs[...].astype(F32), 0.0))
    ints[16:32, :] = dot(lang_rows, by_slot).astype(jnp.int32)
    ints[32:48, :] = dot(count_rows, by_slot).astype(jnp.int32)
    ints[48:64, :] = dot(count_rows, by_word).astype(jnp.int32)


def mono(
    lay, stage,
    codes_in, counts_in, langs_in, length, cm_in, lookup_in, group_in, vec_in, wm_in, wvec_in, cot_in,
    y_out, cm_out, lookup_out, group_out, vec_out, wm_out, wvec_out,
    codes, counts, langs, cm, look, grp, vec, wm, wvec, cot,
    out_y, out_lookup, out_group, out_vec, out_wvec, exc, exw, ints,
    Gc, Gw, PBd, Wc, Wwt, out_cm, out_wm,
    xh1, n1s, qkvs, probs, os, xh2, n2s, acts, slopes, r2s, alphas, dr1s,
    Us, Ys, acct, sums, tsum,
    wide, thin_c, thin_w, thick,
    in_sem, out_sem, ag_send, ag_recv, rs_send, rs_recv, *recv,
):
    Y, Z, X = lay.sizes
    g = Grid(lay.sizes)
    PBc = Gc

    ins = [
        pltpu.make_async_copy(src, dst, in_sem.at[k])
        for k, (src, dst) in enumerate(
            (
                (cm_in, cm), (lookup_in, look), (group_in, grp), (vec_in, vec), (wm_in, wm),
                (wvec_in, wvec), (codes_in, codes), (counts_in, counts), (langs_in, langs), (cot_in, cot),
            )
        )
    ]
    for copy in ins:
        copy.start()
    ag = Copies(ag_send, ag_recv)
    cuts = [c * lay.rw for c in lay.word_cuts]
    gc = gather_pair(g, Gc, ag, 0, Gc.shape[4])
    gu = gather_pair(g, Gw, ag, 0, cuts[2])
    gd = gather_pair(g, Gw, ag, cuts[2], cuts[3])
    g.greet()
    for copy in ins[0:4]:
        copy.wait()
    exc[...] = jnp.zeros(exc.shape, F32)
    exc[:, 0 : 2 * 128] = look[...].astype(F32)
    exc[:, 256 : 256 + LANGS] = grp[...].astype(F32)
    exc[:, 256 + LANGS : 256 + LANGS + 5] = vec[...].astype(F32)
    order_c = list(range(lay.bc + 3)) + [None] * (lay.jc - lay.bc - 3)
    place_own(Gc.at[g.me], cm, out_cm, exc, lay.rc, lay.bc, order_c)
    g.met()
    gc.step1()
    for copy in ins[4:6]:
        copy.wait()
    exw[...] = dot_tn(wvec[...], one_hot(iota((4, 128), 0) == iota((4, 128), 1)))
    place_own(Gw.at[g.me], wm, out_wm, exw, lay.rw, lay.bw, lay.word_order)
    gu.step1()
    gd.step1()
    for copy in ins[6:9]:
        copy.wait()
    slot_ints(codes, counts, langs, ints)
    gc.step2()
    gc.step3()
    gc.step4()
    gu.step2()
    gc.step5()
    gc.finish()
    gu.step3()
    gd.step2()
    assemble(Gc, Wc, lay.rc, order_c, wide, thin_c)

    eye = (iota((16, 128), 0) == iota((16, 128), 1)).astype(F32).astype(BF16)
    rows_c = dot_nt(eye, Wc[:, (lay.bc + 2) * 128 : (lay.bc + 3) * 128])
    gain1, shift1, gain2, shift2 = (rows_c[8 + k : 9 + k] for k in range(4))
    query = rows_c[12:13]
    table_low = low(jnp.where(iota((16, C), 0) < LANGS, rows_c, 0.0))
    lookup = slice(lay.bc * 128, (lay.bc + 2) * 128)
    AQ, AO = slice(0, 3 * C), slice(3 * C, 4 * C)
    AU, AD = slice(4 * C, 4 * C + CM), slice(4 * C + CM, 4 * C + 2 * CM)
    PK, PV = slice(4 * C + 2 * CM, 5 * C + 2 * CM), slice(5 * C + 2 * CM, 6 * C + 2 * CM)
    PR = slice(6 * C + 2 * CM, 6 * C + 2 * CM + D)

    lane = iota((1, 128), 1)
    lane_word = lane // W
    word_rows = [(lane_word == w).astype(F32).astype(BF16) for w in range(8)]
    heads = head_rows(BF16)
    head_of = iota((128, C), 0) % 32 // 8 == iota((128, C), 1) // HD
    pq_rows = jnp.where(head_of, query * 0.125, 0.0)
    score_map = dot_nt(low(pq_rows), Wc[:, PK])
    map_hi = low(score_map)
    map_lo = low(score_map - map_hi.astype(F32))
    key_row = iota((1, W, 1), 1)
    pool_own = iota((128, 128), 0) // W == iota((128, 128), 1) % 8
    pool_slot = iota((128, 128), 0) % W

    def onehots(i, groups):
        parts = []
        for k in range(groups):
            r = i * groups + k
            codes = ints[pl.ds(r, 1), :]
            langs = ints[pl.ds(16 + r, 1), :]
            a = (iota((VOCAB, 128), 0) == codes).astype(F32).astype(BF16)
            b = (iota((16, 128), 0) == langs).astype(F32).astype(BF16)
            parts.append(jnp.concatenate([a, b], 0))
        return parts

    GF = lay.fwd_rows // 128

    hook_f = hooks({
            (0, 2): [gu.step4],
            (0, 4): [gd.step3],
            (1, 3): [gu.step5, gd.step4],
        })

    def forward(i, _):
        rows = pl.ds(pl.multiple_of(i * lay.fwd_rows, lay.fwd_rows), lay.fwd_rows)
        table = jnp.concatenate([Wc[:, lookup], table_low], 0)
        e = jnp.concatenate([dot_tn(h, table) for h in onehots(i, GF)], 0)
        xhat, scale1 = norm_stats(e)
        n1 = low(xhat * gain1 + shift1)
        xh1[rows, :] = low(xhat)
        n1s[rows, :] = n1
        qkv = low(dot(n1, Wc[:, AQ]))
        qkvs[rows, :] = qkv
        hook_f(i, 0)
        mixed = []
        for k in range(GF):
            visible = key_row < ints[pl.ds(32 + i * GF + k, 1), :].reshape(1, 1, 128)
            pair_out = []
            for p in range(2):
                q, kk, v = (
                    qkv[k * 128 : (k + 1) * 128, b * C + p * 128 : b * C + (p + 1) * 128]
                    for b in range(3)
                )
                s = own_word(dot_nt(head_stack(kk, heads), q), lane_word) * 0.125
                s = jnp.where(visible, s, NEGATIVE)
                s = jnp.exp(s - jnp.max(s, 1, keepdims=True))
                prob = s / jnp.sum(s, 1, keepdims=True)
                probs[i * GF + k, 2 * p : 2 * p + 2] = prob
                pair_out.append(dot_tn(spread_words(low(prob), word_rows), head_stack(v, heads)))
            mixed.append(jnp.concatenate(pair_out, 1))
        o = low(jnp.concatenate(mixed, 0))
        os[rows, :] = o
        hook_f(i, 1)
        r1 = e + dot(o, Wc[:, AO])
        xhat, scale2 = norm_stats(r1)
        n2 = low(xhat * gain2 + shift2)
        xh2[rows, :] = low(xhat)
        n2s[rows, :] = n2
        alphas[rows, 64:65] = scale1
        alphas[rows, 65:66] = scale2
        hook_f(i, 2)
        value, slope = gelu_both(dot(n2, Wc[:, AU]))
        act = low(value)
        acts[rows, :] = act
        slopes[rows, :] = low(slope)
        r2 = low(r1 + dot_nt(act, Wc[:, AD]))
        r2s[rows, :] = r2
        hook_f(i, 3)
        for k in range(GF):
            r = i * GF + k
            own = r2[k * 128 : (k + 1) * 128]
            s = dot_nt(own, map_hi) + dot_nt(own, map_lo)
            seen = pool_own & (pool_slot < ints[pl.ds(48 + r, 1), :])
            s = jnp.where(seen, s, NEGATIVE)
            s = jnp.where(seen, jnp.exp(s - jnp.max(s, 0, keepdims=True)), 0.0)
            alpha = s / jnp.sum(s, 0, keepdims=True)
            alphas[pl.ds(pl.multiple_of(r * 128, 128), 128), 0:32] = alpha[:, :32]
            u = dot_tn(low(alpha)[:, :32], own)
            for h in range(CH):
                Us[h, pl.ds(pl.multiple_of(r * 8, 8), 8), :] = u[8 * h : 8 * h + 8]
        hook_f(i, 4)
        return 0

    lax.fori_loop(0, LEN * W // lay.fwd_rows, forward, 0)

    head_c = [iota((1, C), 1) // HD == h for h in range(CH)]
    pooled = sum(jnp.where(head_c[h], dot(low(Us[h]), Wc[:, PV]), 0.0) for h in range(CH))
    pooled_low = low(pooled)
    w_in = dot(pooled_low, Wc[:, PR])

    gu.finish()
    if lay.rw < 16:
        gd.finish()
    if lay.rw >= 16:

        def wcols(lo, hi):
            return jnp.concatenate(
                [
                    Gw[:, :, :, :, p * lay.rw : (p + 1) * lay.rw, :].reshape(D, 128)
                    for p in [lay.word_at[j] for j in range(lo // 128, hi // 128)]
                ],
                1,
            )

    else:
        assemble(Gw, Wwt, lay.rw, lay.word_order, wide, thin_w)

        def wcols(lo, hi):
            return Wwt[:, lo:hi]

    rows_w = dot_nt(eye, wcols(D_COLS, D_COLS + 128))
    f1, c1, f2, c2 = (rows_w[k : k + 1] for k in range(4))
    BQ, BO, BU, BD = (0, 3 * D), (3 * D, 4 * D), (4 * D, 4 * D + FF), (4 * D + FF, D_COLS)
    NP = H // 2

    xhat1, sc1 = norm_stats(w_in)
    m1 = low(xhat1 * f1 + c1)
    qkv = low(dot(m1, wcols(*BQ)))
    key = iota((1, 128, 1), 1)
    seen_word = (key <= iota((1, 1, 128), 2)) & (key < length[0])
    pw, kst, qst, vst, mix = [], [], [], [], []
    for p in range(NP):
        q, kk, v = (qkv[:, b * D + p * 128 : b * D + (p + 1) * 128] for b in range(3))
        kst.append(head_stack(kk, heads))
        qst.append(head_stack(q, heads))
        vst.append(head_stack(v, heads))
        s = dot_nt(kst[p], q).reshape(2, 128, 128) * 0.125
        s = jnp.where(seen_word, s, NEGATIVE)
        s = jnp.exp(s - jnp.max(s, 1, keepdims=True))
        pw.append(s / jnp.sum(s, 1, keepdims=True))
        mix.append(dot_tn(low(pw[p]).reshape(256, 128), vst[p]))
    ow = low(jnp.concatenate(mix, 1))
    x = w_in + dot(ow, wcols(*BO))
    xhat2, sc2 = norm_stats(x)
    m2 = low(xhat2 * f2 + c2)
    value, slope = gelu_both(dot(m2, wcols(*BU)))
    aw = low(value)
    ins[9].wait()
    gy = cot[...]
    dy = gy.astype(F32)
    rw = lay.rw
    unit_w = max(1, 16 // rw)
    waiting = {}

    def put_w(at, blocks):
        waiting.update({at + k: b for k, b in enumerate(blocks)})
        for first in range(0, lay.jw, unit_w):
            ready = range(first, first + unit_w)
            if all(j in waiting for j in ready):
                some = [waiting.pop(j) for j in ready]
                if rw >= 16 and first >= lay.word_cuts[2]:
                    pack_blocks(PBd, first - lay.word_cuts[2], some, rw, wide, thick)
                else:
                    pack_blocks(Gw, first, some, rw, wide, thick)

    rs = Copies(rs_send, rs_recv)
    land = list(recv)
    first_d = 0 if rw >= 16 else cuts[2]
    cut1 = lay.j1 * lay.rc
    w1 = scatter_pair(g, PBd if rw >= 16 else Gw, land, rs, first_d, first_d + cuts[3] - cuts[2])
    w2 = scatter_pair(g, Gw, land, rs, cuts[1], cuts[2])
    w3 = scatter_pair(g, Gw, land, rs, 0, cuts[1])
    s1 = scatter_pair(g, Gc, land, rs, 0, cut1)
    s2 = scatter_pair(g, Gc, land, rs, cut1, Gc.shape[4])
    if rw < 16:
        gu.drain()
        gd.drain()
    at = lay.word_cuts[2]
    pass
    for k in range(0, FF, 512):
        put_w(at + k // 128, columns(dot_tn(gy, aw[:, k : k + 512])))
    w1.step1()
    gd.step5()
    w1.step2()
    if rw >= 16:
        gd.finish()
        gu.drain()
        gd.drain()
    out_y[...] = low(x + dot_nt(aw, wcols(*BD)))
    outs = Outs(out_sem)
    outs.start(out_y, y_out)
    gzw = low(slope * dot(gy, wcols(*BD)))
    pass
    dm2 = dot_nt(gzw, wcols(*BU))
    at = lay.word_cuts[1]
    for k in range(0, FF, 512):
        put_w(at + k // 128, columns(dot_tn(m2, gzw[:, k : k + 512])))
    w2.step1()
    pass
    gf2 = jnp.sum(dm2 * xhat2, 0, keepdims=True)
    gc2 = jnp.sum(dm2, 0, keepdims=True)
    dx = dy + norm_back(dm2, xhat2, sc2, f2)
    gx = low(dx)
    gow = low(dot_nt(gx, wcols(*BO)))
    put_w(BO[0] // 128, columns(dot_tn(ow, gx)))
    pass
    gq, gk, gv = [], [], []
    for p in range(NP):
        go = gow[:, p * 128 : (p + 1) * 128]
        dp = dot_nt(vst[p], go).reshape(2, 128, 128)
        inner = jnp.sum(pw[p] * dp, 1, keepdims=True)
        gs = low(pw[p] * (dp - inner)).reshape(256, 128)
        gq.append(dot_tn(gs, kst[p]) * 0.125)
        gk.append(dot(side_by_side(gs, 128), qst[p]) * 0.125)
        gv.append(dot(side_by_side(low(pw[p]).reshape(256, 128), 128), head_stack(go, heads)))
    tg = low(jnp.concatenate(gq + gk + gv, 1))
    dm1 = dot_nt(tg, wcols(*BQ))
    for k in range(0, 3 * D, 512):
        put_w(k // 128, columns(dot_tn(m1, tg[:, k : k + 512])))
    gf1 = jnp.sum(dm1 * xhat1, 0, keepdims=True)
    gc1 = jnp.sum(dm1, 0, keepdims=True)
    dw = dx + norm_back(dm1, xhat1, sc1, f1)
    vec_rows = low(jnp.concatenate([gf1, gc1, gf2, gc2, jnp.zeros((12, D), F32)], 0))
    at = lay.word_at[lay.bw]
    put_w(at, [dot_tn(vec_rows, eye)] + [jnp.zeros((D, 128), F32)] * (lay.word_cuts[1] - at - 1))
    w3.step1()
    w2.step2()

    gc.drain()
    gw = low(dw)
    dpool = dot_nt(gw, Wc[:, PR])
    pass
    dp4 = jnp.concatenate([low(jnp.where(head_c[h], dpool, 0.0)) for h in range(CH)], 0)
    Ys[...] = dot_nt(dp4, Wc[:, PV]).reshape(CH, LEN, C)
    for ref in (acct, sums, tsum):
        ref[...] = jnp.zeros(ref.shape, F32)

    map32 = map_hi[:32]
    GB = lay.bwd_rows // 128

    GP = lay.ffn_rows // 128

    def back_ffn(i, _):
        rows = pl.ds(pl.multiple_of(i * lay.ffn_rows, lay.ffn_rows), lay.ffn_rows)
        parts = []
        for k in range(GP):
            r = i * GP + k
            own = r2s[pl.ds(pl.multiple_of(r * 128, 128), 128), :]
            alpha = alphas[pl.ds(pl.multiple_of(r * 128, 128), 128), 0:32]
            yg = low(
                jnp.concatenate(
                    [Ys[h, pl.ds(pl.multiple_of(r * 8, 8), 8), :] for h in range(CH)], 0
                )
            )
            da = dot_nt(own, yg)
            dr = low(alpha * (da - jnp.sum(alpha * da, 0, keepdims=True)))
            tsum[...] += dot_tn(dr, own)
            parts.append(dot(low(alpha), yg) + dot(dr, map32))
        dr2 = jnp.concatenate(parts, 0)
        g2 = low(dr2)
        hook_1(i, 0)
        r2s[rows, :] = g2
        hook_1(i, 1)
        gz = low(slopes[rows, :].astype(F32) * dot(g2, Wc[:, AD]))
        slopes[rows, :] = gz
        hook_1(i, 2)
        dn = dot_nt(gz, Wc[:, AU])
        xhat = xh2[rows, :].astype(F32)
        sums[2:3, :] += jnp.sum(dn * xhat, 0, keepdims=True)
        sums[3:4, :] += jnp.sum(dn, 0, keepdims=True)
        dr1 = dr2 + norm_back(dn, xhat, alphas[rows, 65:66], gain2)
        dr1s[rows, :] = dr1
        xh2[rows, :] = low(dr1)
        hook_1(i, 3)
        return 0

    def place_w(j, value):
        j = lay.word_order[j]
        if j is None:
            return
        if j < lay.bw:
            put(out_wm, lay.bw, j, value)
        else:
            pick = (iota((8, 128), 0) == iota((8, 128), 1)).astype(F32)
            out_wvec[...] = lax.dot_general(
                pick, value, (((1,), (1,)), ((), ())),
                precision=lax.Precision.HIGHEST, preferred_element_type=F32,
            )[0:4]

    def place_1(j, value):
        put(out_cm, lay.bc, 8 + j if j < 24 else j - 18, value)

    def place_2(j, value):
        if j < 6:
            put(out_cm, lay.bc, j, value)
        elif j < 8:
            out_lookup[:, (j - 6) * 128 : (j - 5) * 128] = value
        else:
            out_group[...] = value[:, 0:LANGS]
            out_vec[...] = value[:, LANGS : LANGS + 5]

    def fin_w1():
        w1.finish(lambda j, v: place_w(lay.word_cuts[2] + j, v), rw, first_d, FF // 128)

    def fin_w2():
        w2.finish(lambda j, v: place_w(lay.word_cuts[1] + j, v), rw, cuts[1], FF // 128)

    def fin_w3():
        w3.finish(place_w, rw, 0, lay.word_cuts[1])

    def fin_s1():
        s1.finish(place_1, rc, 0, 26)

    def fin_s2():
        s2.finish(place_2, rc, cut1, 9)

    hook_1 = hooks({
            (1, 0): [w1.step3, w3.step2],
        })
    lax.fori_loop(0, LEN * W // lay.ffn_rows, back_ffn, 0)

    grad_pr = dot_tn(pooled_low, gw)
    grad_pv = dot_tn(low(Us[...]).reshape(CH * LEN, C), dp4)
    t_low = low(tsum[...])
    grad_pk = dot_tn(t_low, low(pq_rows[:32]))
    rc = lay.rc
    pad1 = [jnp.zeros((C, 128), F32)] * (lay.j1 - 26)
    pack_blocks(
        PBc,
        0,
        columns(dot_tn(n2s[...], slopes[...])) + columns(dot_tn(r2s[...], acts[...])) + columns(grad_pk) + columns(grad_pv)
        + columns(grad_pr) + columns(dot_tn(os[...], xh2[...])) + pad1,
        rc,
        wide,
        thick,
    )
    s1.step1()
    w1.step4()
    w2.step3()
    gpq = dot(t_low, Wc[:, PK]) * 0.125
    gpq = jnp.sum(
        jnp.where(iota((32, C), 0) // 8 == iota((32, C), 1) // HD, gpq, 0.0), 0, keepdims=True
    )

    def back_attention(i, _):
        rows = pl.ds(pl.multiple_of(i * lay.bwd_rows, lay.bwd_rows), lay.bwd_rows)
        dr1 = dr1s[rows, :]
        go = low(dot_nt(xh2[rows, :], Wc[:, AO]))
        hook_2(i, 0)
        qkv = qkvs[rows, :]
        grads = [[], [], []]
        for k in range(GB):
            part = [[], [], []]
            for p in range(2):
                at = slice(k * 128, (k + 1) * 128)
                q, kk, v = (
                    qkv[at, b * C + p * 128 : b * C + (p + 1) * 128] for b in range(3)
                )
                gop = go[at, p * 128 : (p + 1) * 128]
                prob = probs[i * GB + k, 2 * p : 2 * p + 2]
                dp = own_word(dot_nt(head_stack(v, heads), gop), lane_word)
                gs = low(prob * (dp - jnp.sum(prob * dp, 1, keepdims=True)))
                gs = spread_words(gs, word_rows)
                pb = spread_words(low(prob), word_rows)
                part[0].append(dot_tn(gs, head_stack(kk, heads)) * 0.125)
                part[1].append(dot(side_by_side(gs, 128), head_stack(q, heads)) * 0.125)
                part[2].append(dot(side_by_side(pb, 128), head_stack(gop, heads)))
            for b in range(3):
                grads[b].append(jnp.concatenate(part[b], 1))
        hook_2(i, 1)
        tg = low(jnp.concatenate([jnp.concatenate(b, 0) for b in grads], 1))
        qkvs[rows, :] = tg
        dn = dot_nt(tg, Wc[:, AQ])
        hook_2(i, 2)
        xhat = xh1[rows, :].astype(F32)
        sums[0:1, :] += jnp.sum(dn * xhat, 0, keepdims=True)
        sums[1:2, :] += jnp.sum(dn, 0, keepdims=True)
        ge = low(dr1 + norm_back(dn, xhat, alphas[rows, 64:65], gain1))
        acct[...] += dot(jnp.concatenate(onehots(i, GB), 1), ge)
        hook_2(i, 3)
        return 0

    hook_2 = hooks({
            (0, 2): [w3.step3],
            (0, 3): [s1.step2, w2.step4],
        })
    lax.fori_loop(0, LEN * W // lay.bwd_rows, back_attention, 0)

    pass
    small = low(jnp.concatenate([acct[VOCAB : VOCAB + 8], sums[0:4], gpq, jnp.zeros((3, C), F32)], 0))
    pad2 = [jnp.zeros((C, 128), F32)] * (lay.j2 - 9)
    pack_blocks(
        PBc,
        lay.j1,
        columns(dot_tn(n1s[...], qkvs[...])) + columns(acct[0:VOCAB, :])
        + [dot_tn(small, eye)] + pad2,
        rc,
        wide,
        thick,
    )
    s2.step1()
    w3.step4()
    s1.step3()
    fin_w1()
    s2.step2()
    s1.step4()
    s2.step3()
    s2.step4()
    fin_w3()
    fin_w2()
    outs.start(out_wm, wm_out)
    outs.start(out_wvec, wvec_out)
    fin_s1()
    fin_s2()
    outs.start(out_cm, cm_out)
    outs.start(out_lookup, lookup_out)
    outs.start(out_group, group_out)
    outs.start(out_vec, vec_out)
    for part in (w1, w2, w3, s1, s2):
        part.drain()
    outs.wait()


def hand_over(*refs):
    n = 7
    ins, outs, held, sems = refs[:n], refs[n : 2 * n], refs[2 * n : 3 * n], refs[-1]
    first = [pltpu.make_async_copy(ins[k], held[k], sems.at[k]) for k in range(n)]
    then = [pltpu.make_async_copy(held[k], outs[k], sems.at[n + k]) for k in range(n)]
    for copy in first:
        copy.start()
    for k in range(n):
        first[k].wait()
        then[k].start()
    for copy in then:
        copy.wait()


def shards(
    sizes,
    char_codes,
    char_counts,
    word_groups,
    valid_words,
    char_matrix,
    char_lookup,
    group_lookup,
    char_vectors,
    word_matrix,
    word_vectors,
    cotangent,
):
    lay = Layout(sizes)
    Y, Z, X = sizes
    rows = LEN * W
    rows_c, rows_w = lay.jc * lay.rc, lay.jw * lay.rw
    rows_1 = lay.j1 * lay.rc
    nag = ag_count(Y, Z, X) * 6
    nrs = rs_count(Y, Z, X) * 10
    dma = pltpu.SemaphoreType.DMA

    def vm(shape, dtype):
        return pltpu.VMEM(shape, dtype)

    def like(a):
        return pltpu.VMEM(a.shape, a.dtype)

    ins = (
        char_codes[0].T,
        char_counts,
        word_groups,
        valid_words,
        char_matrix,
        char_lookup,
        group_lookup,
        char_vectors,
        word_matrix,
        word_vectors.T,
        cotangent[0],
    )
    outs = [
        jax.ShapeDtypeStruct((LEN, D), BF16),
        jax.ShapeDtypeStruct(char_matrix.shape, F32),
        jax.ShapeDtypeStruct(char_lookup.shape, F32),
        jax.ShapeDtypeStruct(group_lookup.shape, F32),
        jax.ShapeDtypeStruct(char_vectors.shape, F32),
        jax.ShapeDtypeStruct(word_matrix.shape, F32),
        jax.ShapeDtypeStruct(word_vectors.shape[::-1], F32),
    ]
    scratch = [like(a) for k, a in enumerate(ins) if k != 3]
    scratch += [like(outs[k]) for k in (0, 2, 3, 4, 6)]
    scratch += [
        vm((lay.rc, 3 * 128), F32),
        vm((lay.rw, 128), F32),
        vm((64, 128), jnp.int32),
        vm(lay.lead + (rows_c, 128), BF16),
        vm(lay.lead + (rows_w, 128), BF16),
        vm(lay.lead + (FF // 128 * lay.rw, 128) if lay.rw >= 16 else (16, 128), BF16),
        vm((C, (lay.bc + 3) * 128), BF16),
        vm((D, (lay.bw + 1) * 128) if lay.rw < 16 else (16, 128), BF16),
        like(outs[1]),
        like(outs[5]),
        vm((rows, C), BF16),
        vm((rows, C), BF16),
        vm((rows, 3 * C), BF16),
        vm((16, CH, W, 128), F32),
        vm((rows, C), BF16),
        vm((rows, C), BF16),
        vm((rows, C), BF16),
        vm((rows, CM), BF16),
        vm((rows, CM), BF16),
        vm((rows, C), BF16),
        vm((rows, 128), F32),
        vm((rows, C), F32),
        vm((CH, LEN, C), F32),
        vm((CH, LEN, C), F32),
        vm((VOCAB + 16, C), F32),
        vm((8, C), F32),
        vm((32, C), F32),
        vm((lay.devices * 16 if lay.rc < 8 else 8, 128), F32),
        vm((Z * X * lay.rc, 128), F32),
        vm((Z * X * lay.rw, 128), F32),
        vm((D if lay.rc < 8 else 8, 128), F32),
        dma((10,)),
        dma((7,)),
        dma((nag,)),
        dma((nag,)),
        dma((nrs,)),
        dma((nrs,)),
    ]
    at = [c * lay.rw for c in lay.word_cuts]
    for lo, hi in ((at[2], at[3]), (at[1], at[2]), (at[0], at[1]), (0, rows_1), (rows_1, rows_c)):
        scratch += scatter_pair_scratch(sizes, lo, hi)
    anywhere = pl.BlockSpec(memory_space=pl.ANY)
    in_specs = [anywhere] * 11
    in_specs[3] = pl.BlockSpec(memory_space=pltpu.SMEM)
    got = pl.pallas_call(
        functools.partial(mono, lay, STAGE),
        out_shape=outs,
        in_specs=in_specs,
        out_specs=[anywhere] * 7,
        scratch_shapes=scratch,
        compiler_params=pltpu.CompilerParams(
            collective_id=0, has_side_effects=True, vmem_limit_bytes=VMEM_LIMIT
        ),
        name="layer",
    )(*ins)
    got = pl.pallas_call(
        hand_over,
        out_shape=outs,
        in_specs=[anywhere] * 7,
        out_specs=[anywhere] * 7,
        scratch_shapes=[like(a) for a in outs] + [dma((14,))],
        name="hand_over",
    )(*got)
    return (got[0][None],) + tuple(got[1:6]) + (got[6].T,)


def solution(mesh):
    dp, fsdp = mesh.shape["dp"], mesh.shape["fsdp"]
    Y = dp // 2
    X = Y if fsdp % Y == 0 else 1
    sizes = (Y, fsdp // X, X)
    placed = (
        P(("dp", "fsdp"), None, None),
        P(("dp", "fsdp"), None),
        P(("dp", "fsdp"), None),
        P(("dp", "fsdp")),
        P(("dp", "fsdp"), None),
        P(("dp", "fsdp"), None),
        P(("dp", "fsdp"), None),
        P(("dp", "fsdp"), None),
        P(("dp", "fsdp"), None),
        P(("dp", "fsdp"), None),
        P(("dp", "fsdp"), None, None),
    )
    return jax.shard_map(
        functools.partial(shards, sizes),
        mesh=mesh,
        in_specs=placed,
        out_specs=(
            P(("dp", "fsdp"), None, None),
            P(("dp", "fsdp"), None),
            P(("dp", "fsdp"), None),
            P(("dp", "fsdp"), None),
            P(("dp", "fsdp"), None),
            P(("dp", "fsdp"), None),
            P(("dp", "fsdp"), None),
        ),
        check_vma=False,
    )
```
